256 devices in a mesh: section: 8 (over x, z_hi), expert: 8 (over y, core), mp: 4 (over z_lo).
Axes of the slice: x: 4, y: 4, z: 8 (z_hi: 2, z_lo: 4; z = z_hi * 4 + z_lo), core: 2. Of those that a mesh axis runs over, the one named last changes fastest.
Arguments:
- tokens_in: bfloat16 [8, 1024, 4096], P('section', 'expert', 'mp'), may hold values from -6 to 6
- route_ids: int32 [8, 1024, 2], P('section', 'expert'), may hold values from 0 to 7, all different within a row; in each aligned block of 128 rows (0 to 127, 128 to 255, ..., all dimensions but the last counted through in order) at most 64 rows name the same one
- route_weights: float32 [8, 1024, 2], P('section', 'expert'), may hold values from 0.25 to 1
- stash: bfloat16 [8, 2, 1024, 4096], P('section', None, 'expert', 'mp'), may hold values from -6 to 6
- returned_batch_index: int32 [8, 8], P('section', 'expert'), may hold values from 0 to 1
- back_ids: int32 [8, 1024, 2], P('section', 'expert'), may hold values from 0 to 7, all different within a row; in each aligned block of 128 rows (0 to 127, 128 to 255, ..., all dimensions but the last counted through in order) at most 64 rows name the same one
- back_weights: float32 [8, 1024, 2], P('section', 'expert'), may hold values from 0.25 to 1
- upstream: bfloat16 [8, 1024, 4096], P('section', 'expert', 'mp'), may hold values from -1.5 to 1.5
- window_expert: int32 [8], P('section'), may hold values from 0 to 7
- w_gate: bfloat16 [8, 7168, 4096], P('section', ('expert', 'mp')), may hold values from -0.09375 to 0.09375
- w_up: bfloat16 [8, 7168, 4096], P('section', ('expert', 'mp')), may hold values from -0.09375 to 0.09375
- w_down: bfloat16 [8, 7168, 4096], P('section', ('expert', 'mp')), may hold values from -0.0625 to 0.0625
Outputs:
- expert_out: bfloat16 [8, 1024, 4096], P('section', 'expert', 'mp')
- input_grad: bfloat16 [8, 1024, 4096], P('section', 'expert', 'mp')
- grad_gate: bfloat16 [8, 7168, 4096], P('section', ('expert', 'mp'))
- grad_up: bfloat16 [8, 7168, 4096], P('section', ('expert', 'mp'))
- grad_down: bfloat16 [8, 7168, 4096], P('section', ('expert', 'mp'))
The draws below stay inside these ranges and needn't reach their ends.
Inputs may be any that keep to these rules, and one draw needn't show every extreme that they name: `route_ids`: each token names two different experts; among the 128 tokens of one group no expert is named by more than 64 tokens, a bound that some block reaches. `back_ids`: as route_ids.
All inputs are finite; a program needn't handle non-finite values.
Results may differ from the reference program's by a relative error of at most 0.0058.
Values may be sent and summed in bfloat16 or wider, within the bound.
No kernel may reach another device: no remote copies, remote signals or barrier semaphores. Data moves between devices by JAX's collectives and lax.ppermute only.
A program may use at most 128 MiB of HBM per device.

```python
import math
import jax
import jax.numpy as jnp
import numpy as np

MODEL_WIDTH = 4096
EXPERTS = 8
FF = 7168
TOK_DEV = 128
HELD_BATCHES = 2
CAP = 64
RELAY_SECTIONS = 8
GROUPS = 8
SECTION_TOKENS = 1024
N_SECTION = 8
N_EXPERT = 8


def with_ends(drawn, rng, smallest, largest):
    longest = drawn.shape.index(max(drawn.shape))
    spots = []
    for shift in (0, 1):
        where = [jax.random.randint(jax.random.fold_in(rng, axis), (), 0, length) for axis, length in enumerate(drawn.shape)]
        where[longest] = (where[longest] + shift) % drawn.shape[longest]
        spots.append(tuple(where))
    return drawn.at[spots[0]].set(smallest).at[spots[1]].set(largest)


def shard_levels(own_key, extent, cuts, least, largest):
    def one(axis_at, parts):
        steps = jax.random.uniform(jax.random.fold_in(jax.random.fold_in(own_key, 6), axis_at), (parts,), jnp.float32, least / len(cuts), largest / len(cuts))
        return jnp.repeat(jnp.exp(steps), extent[axis_at] // parts).reshape((-1,) + (1,) * (len(extent) - axis_at - 1))

    factor_of = one(*cuts[0])
    for cut in cuts[1:]:
        factor_of = factor_of * one(*cut)
    return factor_of


def routed_block(stream_key, own, number, rows, number_of, top, most, skew):
    order = jax.random.permutation(stream_key, number_of)
    crowded, usual = load_shares(number_of, rows * top, most, skew, True), load_shares(number_of, rows * top, most, skew, False)
    places = jnp.arange(number_of)

    def named(tallies, offset_by):
        used = int((tallies > 0).sum())
        fixed = max(1, used // 4)
        passed = fixed + (places - fixed + offset_by * (used - fixed)) % max(1, number_of - fixed)
        return jnp.zeros((number_of,), jnp.int32).at[order[jnp.where(places < fixed, places, passed)]].set(jnp.asarray(tallies, jnp.int32))

    tallies = jnp.where(number % 4 == 0, named(crowded, number // 4), named(usual, number - number // 4 - 1))
    mixed = jax.random.permutation(jax.random.fold_in(own, 3), number_of)
    giver, sink = mixed[0:number_of // 2 * 2:2], mixed[1:number_of // 2 * 2:2]
    slack = jnp.minimum(tallies[giver] - 1, most - tallies[sink]) // 2
    slack = jnp.where((giver == order[0]) | (sink == order[0]) | (tallies[sink] == 0), 0, jnp.maximum(slack, 0))
    passed = jax.random.randint(jax.random.fold_in(own, 4), (number_of // 2,), 0, 1 << 20) % (slack + 1)
    tallies = tallies.at[giver].add(-passed).at[sink].add(passed)
    labels = jnp.searchsorted(jnp.cumsum(tallies), jnp.arange(rows * top), side="right").astype(jnp.int32)
    grid = labels.reshape(top, rows).T
    grid = grid[jax.random.permutation(jax.random.fold_in(own, 1), rows)]
    offset_by = jax.random.randint(jax.random.fold_in(own, 2), (rows, 1), 0, top)
    return jnp.take_along_axis(grid, (jnp.arange(top)[None, :] + offset_by) % top, axis=1)


def load_shares(count, total, reach, lean, full):
    portions = [(1 << 20) // math.isqrt(standing ** lean) + 1 for standing in range(1, count + 1)]
    largest = reach if full else min(reach, max(-(-total // count), total * portions[0] // sum(portions)))
    least = 1 if total - largest >= count - 1 else 0
    holding, surplus = [largest] + [least] * (count - 1), total - largest - least * (count - 1)
    while surplus > 0:
        free = [i for i in range(1, count) if holding[i] < largest] or [i for i in range(1, count) if holding[i] < reach]
        pool, left = sum([portions[i] for i in free]), surplus
        for i in free:
            extra = min(reach - holding[i], max(1, left * portions[i] // pool), surplus)
            holding[i] = holding[i] + extra
            surplus = surplus - extra
    return np.array(holding)


def bell_draw(key, shape, scale, limit, split=(), kind=jnp.bfloat16):
    values = jax.random.normal(key, shape, jnp.float32) * scale
    if len(split) > 0:
        values = shard_levels(key, shape, split, -0.22, 0.18) * values
    return jnp.clip(values, min=-limit, max=limit).astype(kind)


def setup_inputs(seed: int = 0) -> dict:
    splits = jax.random.split(jax.random.key(seed), 13)
    tokens_in = bell_draw(splits[0], (RELAY_SECTIONS, SECTION_TOKENS, MODEL_WIDTH), 1.0, 6.0, ((0, 8), (1, 8), (2, 4)))
    route_ids_keys = jax.random.split(jax.random.fold_in(splits[1], 1), RELAY_SECTIONS * SECTION_TOKENS // TOK_DEV)
    route_ids_turns = jax.random.permutation(jax.random.fold_in(splits[1], 3), RELAY_SECTIONS * SECTION_TOKENS // TOK_DEV)
    route_ids = jax.vmap(lambda own, number: routed_block(jax.random.fold_in(splits[1], 2), own, number, TOK_DEV, EXPERTS, 2, CAP, 2))(route_ids_keys, route_ids_turns).reshape((RELAY_SECTIONS, SECTION_TOKENS, 2))
    route_weights = jnp.clip(jnp.exp(math.log(1.0) - 1.3862944 * jax.random.uniform(splits[2], (RELAY_SECTIONS, SECTION_TOKENS, 2), jnp.float32) ** shard_levels(splits[2], (RELAY_SECTIONS, SECTION_TOKENS, 2), ((0, 8), (1, 8)), -0.2, 0.2)), 0.25, 1.0)
    stash = bell_draw(splits[3], (RELAY_SECTIONS, HELD_BATCHES, SECTION_TOKENS, MODEL_WIDTH), 1.0, 6.0, ((0, 8), (2, 8), (3, 4)))
    returned_batch_index = with_ends(jax.random.randint(splits[4], (RELAY_SECTIONS, GROUPS), 0, HELD_BATCHES), jax.random.fold_in(splits[4], 1), 0, HELD_BATCHES - 1).astype(jnp.int32)
    back_ids_keys = jax.random.split(jax.random.fold_in(splits[5], 1), RELAY_SECTIONS * SECTION_TOKENS // TOK_DEV)
    back_ids_turns = jax.random.permutation(jax.random.fold_in(splits[5], 3), RELAY_SECTIONS * SECTION_TOKENS // TOK_DEV)
    back_ids = jax.vmap(lambda own, number: routed_block(jax.random.fold_in(splits[5], 2), own, number, TOK_DEV, EXPERTS, 2, CAP, 2))(back_ids_keys, back_ids_turns).reshape((RELAY_SECTIONS, SECTION_TOKENS, 2))
    back_weights = jnp.clip(jnp.exp(math.log(1.0) - 1.3862944 * jax.random.uniform(splits[6], (RELAY_SECTIONS, SECTION_TOKENS, 2), jnp.float32) ** shard_levels(splits[6], (RELAY_SECTIONS, SECTION_TOKENS, 2), ((0, 8), (1, 8)), -0.2, 0.2)), 0.25, 1.0)
    upstream = bell_draw(splits[7], (RELAY_SECTIONS, SECTION_TOKENS, MODEL_WIDTH), 0.25, 1.5, ((0, 8), (1, 8), (2, 4)))
    window_expert = with_ends(jax.random.randint(splits[8], (RELAY_SECTIONS,), 0, EXPERTS), jax.random.fold_in(splits[8], 1), 0, EXPERTS - 1).astype(jnp.int32)
    w_gate = bell_draw(splits[9], (RELAY_SECTIONS, FF, MODEL_WIDTH), MODEL_WIDTH ** -0.5, 0.09375, ((0, 8), (1, 32)))
    w_up = bell_draw(splits[10], (RELAY_SECTIONS, FF, MODEL_WIDTH), MODEL_WIDTH ** -0.5, 0.09375, ((0, 8), (1, 32)))
    w_down = bell_draw(splits[11], (RELAY_SECTIONS, FF, MODEL_WIDTH), FF ** -0.5, 0.0625, ((0, 8), (1, 32)))
    return {"tokens_in": tokens_in, "route_ids": route_ids, "route_weights": route_weights, "stash": stash, "returned_batch_index": returned_batch_index, "back_ids": back_ids, "back_weights": back_weights, "upstream": upstream, "window_expert": window_expert, "w_gate": w_gate, "w_up": w_up, "w_down": w_down}


def routing(pair_ids, pair_weights, expert):
    matches = pair_ids == expert
    gate_share = jnp.sum(jnp.where(matches, pair_weights, jnp.float32(0.0)), axis=-1)
    routed = jnp.any(matches, axis=-1)
    counted = routed.astype(jnp.int32)
    slot_of = jnp.cumsum(counted, axis=-1).astype(jnp.int32) - counted
    return gate_share, routed, slot_of


def place_rows(values, routed, slot_of):
    group_of = jnp.arange(N_EXPERT, dtype=jnp.int32)[:, None] * jnp.ones_like(slot_of)
    target = jnp.where(routed, slot_of, CAP).astype(jnp.int32)
    buffer = jnp.zeros((N_EXPERT, CAP, values.shape[-1]), values.dtype)
    buffer = buffer.at[group_of, target].set(values, mode="drop")
    return buffer.reshape(N_EXPERT * CAP, values.shape[-1])


def collect(row_values, slot_of):
    shaped = row_values.reshape(N_EXPERT, CAP, row_values.shape[-1])
    index = jnp.clip(slot_of, 0, CAP - 1).astype(jnp.int32)[:, :, None]
    return jnp.take_along_axis(shaped, index, axis=1)


def project(rows, weight):
    return jnp.dot(rows, weight.T, preferred_element_type=jnp.float32)


def reference(tokens_in, route_ids, route_weights, stash, returned_batch_index, back_ids, back_weights, upstream, window_expert, w_gate, w_up, w_down):
    outs_fwd, outs_grad, outs_gate, outs_up, outs_down = [], [], [], [], []
    for section_num in range(N_SECTION):
        expert = window_expert[section_num]
        gate_w, up_w, down_w = w_gate[section_num], w_up[section_num], w_down[section_num]
        fwd_tokens = tokens_in[section_num].reshape(N_EXPERT, TOK_DEV, MODEL_WIDTH)
        fwd_gate, fwd_routed, fwd_slot = routing(route_ids[section_num].reshape(N_EXPERT, TOK_DEV, 2), route_weights[section_num].reshape(N_EXPERT, TOK_DEV, 2), expert)
        fwd_rows = place_rows(fwd_tokens, fwd_routed, fwd_slot)
        fwd_pre = project(fwd_rows, gate_w)
        fwd_up = project(fwd_rows, up_w)
        fwd_hidden = (fwd_pre * jax.nn.sigmoid(fwd_pre) * fwd_up).astype(jnp.bfloat16)
        fwd_sums = jnp.dot(fwd_hidden, down_w, preferred_element_type=jnp.float32)
        expert_out = (collect(fwd_sums, fwd_slot) * fwd_gate[:, :, None]).astype(jnp.bfloat16)
        mirror = N_SECTION - 1 - section_num
        held = stash[mirror].reshape(HELD_BATCHES, N_EXPERT, TOK_DEV, MODEL_WIDTH)
        picks = returned_batch_index[mirror].astype(jnp.int32)[None, :, None, None]
        back_input = jnp.take_along_axis(held, picks, axis=0)[0]
        back_gate, back_routed, back_slot = routing(back_ids[section_num].reshape(N_EXPERT, TOK_DEV, 2), back_weights[section_num].reshape(N_EXPERT, TOK_DEV, 2), expert)
        back_rows = place_rows(back_input, back_routed, back_slot)
        grad_tokens = (back_gate[:, :, None] * upstream[section_num].reshape(N_EXPERT, TOK_DEV, MODEL_WIDTH).astype(jnp.float32)).astype(jnp.bfloat16)
        grad_rows = place_rows(grad_tokens, back_routed, back_slot)
        pre_gate = project(back_rows, gate_w)
        pre_up = project(back_rows, up_w)
        sigmoid_pre = jax.nn.sigmoid(pre_gate)
        activated = pre_gate * sigmoid_pre
        back_hidden = (activated * pre_up).astype(jnp.bfloat16)
        hidden_grad = project(grad_rows, down_w)
        gate_grad = (hidden_grad * pre_up * sigmoid_pre * (1.0 + pre_gate * (1.0 - sigmoid_pre))).astype(jnp.bfloat16)
        up_grad = (hidden_grad * activated).astype(jnp.bfloat16)
        outs_down.append(jnp.dot(back_hidden.T, grad_rows, preferred_element_type=jnp.float32).astype(jnp.bfloat16))
        outs_gate.append(jnp.dot(gate_grad.T, back_rows, preferred_element_type=jnp.float32).astype(jnp.bfloat16))
        outs_up.append(jnp.dot(up_grad.T, back_rows, preferred_element_type=jnp.float32).astype(jnp.bfloat16))
        back_sums = jnp.dot(gate_grad, gate_w, preferred_element_type=jnp.float32) + jnp.dot(up_grad, up_w, preferred_element_type=jnp.float32)
        input_grad = (collect(back_sums, back_slot) * back_routed.astype(jnp.float32)[:, :, None]).astype(jnp.bfloat16)
        outs_fwd.append(expert_out.reshape(SECTION_TOKENS, MODEL_WIDTH))
        outs_grad.append(input_grad.reshape(SECTION_TOKENS, MODEL_WIDTH))
    return (jnp.stack(outs_fwd), jnp.stack(outs_grad), jnp.stack(outs_gate), jnp.stack(outs_up), jnp.stack(outs_down))
```

```python
import jax
import jax.numpy as jnp
from jax import lax
from jax.sharding import PartitionSpec as P

CAP = 64


def along_y(array, step):
    n = lax.axis_size("expert")
    return lax.ppermute(array, "expert", [(i, (i + 2 * step) % n) for i in range(n)])


def other_core(array):
    n = lax.axis_size("expert")
    return lax.ppermute(array, "expert", [(i, i ^ 1) for i in range(n)])


def along_mp(array, flip):
    n = lax.axis_size("mp")
    return lax.ppermute(array, "mp", [(i, i ^ flip) for i in range(n)])


def mirrored(array):
    n = lax.axis_size("section")
    return lax.ppermute(array, "section", [(i, n - 1 - i) for i in range(n)])


def routing(pair_ids, pair_weights, expert):
    matches = pair_ids == expert
    routed = jnp.any(matches, axis=1)
    counted = routed.astype(jnp.int32)
    slot_of = jnp.cumsum(counted) - counted
    gate_share = jnp.sum(jnp.where(matches, pair_weights, 0.0), axis=1)
    return (gate_share, jnp.where(routed, slot_of, CAP))


def picker_of(slot_or_cap):
    places = jnp.arange(CAP, dtype=jnp.int32)[:, None]
    return slot_or_cap[None, :] == places


def pack(picker, values):
    return jnp.dot(
        picker.astype(jnp.bfloat16), values, preferred_element_type=jnp.float32
    ).astype(jnp.bfloat16)


def unpack(picker, rows):
    return lax.dot_general(
        picker.astype(jnp.bfloat16),
        rows,
        (((0,), (0,)), ((), ())),
        preferred_element_type=jnp.float32,
    ).astype(jnp.bfloat16)


def swapped(flag, first, second):
    return (jnp.where(flag, second, first), jnp.where(flag, first, second))


def widen(block, place):
    one, two, three = (along_mp(block, 1), along_mp(block, 2), along_mp(block, 3))
    odd, high = (place & 1) == 1, (place & 2) == 2
    a0, a1 = swapped(odd, block, one)
    a2, a3 = swapped(odd, two, three)
    b0, b2 = swapped(high, a0, a2)
    b1, b3 = swapped(high, a1, a3)
    return jnp.concatenate([b0, b1, b2, b3], axis=1)


def ring_rows(block):
    half = block.shape[0] // 2
    behind = along_y(block, 1)
    ahead = along_y(block, -1)
    far_low = along_y(behind[:half], 1)
    far_high = along_y(ahead[half:], -1)
    return jnp.concatenate([block, behind, ahead, far_low, far_high], axis=0)


def project(rows, weight):
    return lax.dot_general(
        rows, weight, (((1,), (1,)), ((), ())), preferred_element_type=jnp.float32
    )


def outer_sum(left, right):
    return lax.dot_general(
        left, right, (((0,), (0,)), ((), ())), preferred_element_type=jnp.float32
    )


def spread(hidden, weight):
    return jnp.dot(hidden, weight, preferred_element_type=jnp.float32)


def scatter_sum(term, place):
    own, behind, ahead, far = (term[i * CAP : (i + 1) * CAP] for i in range(4))
    narrow = [block.astype(jnp.bfloat16) for block in (behind, ahead, far)]
    total = (
        own
        + along_y(narrow[0], -1).astype(jnp.float32)
        + along_y(narrow[1], 1).astype(jnp.float32)
        + along_y(narrow[2], 2).astype(jnp.float32)
    )
    width = total.shape[1] // 4

    def columns(array, index):
        return lax.dynamic_slice_in_dim(array, index * width, width, axis=1)

    low = total.astype(jnp.bfloat16)
    result = columns(total, place)
    for flip in (1, 2, 3):
        result = result + along_mp(columns(low, place ^ flip), flip).astype(jnp.float32)
    return result


def per_device(
    tokens_in,
    route_ids,
    route_weights,
    stash,
    returned_batch_index,
    back_ids,
    back_weights,
    upstream,
    window_expert,
    w_gate,
    w_up,
    w_down,
):
    expert = window_expert[0]
    place = lax.axis_index("mp")
    gate_w, up_w, down_w = (w_gate[0], w_up[0], w_down[0])
    fwd_gate, fwd_slot = routing(route_ids[0], route_weights[0], expert)
    fwd_pick = picker_of(fwd_slot)
    back_gate, back_slot = routing(back_ids[0], back_weights[0], expert)
    back_pick = picker_of(back_slot)

    fwd_buf = pack(fwd_pick, tokens_in[0])
    grad_tokens = (back_gate[:, None] * upstream[0].astype(jnp.float32)).astype(jnp.bfloat16)
    grad_buf = pack(back_pick, grad_tokens)
    held_rows = lax.dynamic_index_in_dim(
        stash[0], returned_batch_index[0, 0], axis=0, keepdims=False
    )
    back_buf = mirrored(pack(picker_of(mirrored(back_slot)), held_rows))

    fwd_rows = ring_rows(widen(fwd_buf, place))
    gate_x, up_x, down_x = (other_core(gate_w), other_core(up_w), other_core(down_w))
    grad_rows = ring_rows(widen(grad_buf, place))
    back_rows = ring_rows(widen(back_buf, place))

    fwd_term = 0.0
    for gate, up, down in ((gate_w, up_w, down_w), (gate_x, up_x, down_x)):
        fwd_pre = project(fwd_rows, gate)
        fwd_hidden = (fwd_pre * jax.nn.sigmoid(fwd_pre) * project(fwd_rows, up)).astype(
            jnp.bfloat16
        )
        fwd_term = fwd_term + spread(fwd_hidden, down)
    fwd_sum = scatter_sum(fwd_term, place)
    fwd_row_gate = jnp.sum(jnp.where(fwd_pick, fwd_gate[None, :], 0.0), axis=1)
    expert_out = unpack(fwd_pick, (fwd_sum * fwd_row_gate[:, None]).astype(jnp.bfloat16))

    grad_rows_x = other_core(grad_rows)
    back_rows_x = other_core(back_rows)
    back_term = 0.0
    kept = []
    for gate, up, down in ((gate_w, up_w, down_w), (gate_x, up_x, down_x)):
        hidden_grad = project(grad_rows, down)
        pre_gate = project(back_rows, gate)
        pre_up = project(back_rows, up)
        sigmoid_pre = jax.nn.sigmoid(pre_gate)
        activated = pre_gate * sigmoid_pre
        back_hidden = (activated * pre_up).astype(jnp.bfloat16)
        gate_grad = (
            hidden_grad * pre_up * sigmoid_pre * (1.0 + pre_gate * (1.0 - sigmoid_pre))
        ).astype(jnp.bfloat16)
        up_grad = (hidden_grad * activated).astype(jnp.bfloat16)
        kept.append((back_hidden, gate_grad, up_grad))
        back_term = back_term + (spread(gate_grad, gate) + spread(up_grad, up))
    back_sum = scatter_sum(back_term, place)
    input_grad = unpack(back_pick, back_sum.astype(jnp.bfloat16))

    back_hidden, gate_grad, up_grad = kept[0]
    back_hidden_x, gate_grad_x, up_grad_x = (other_core(array) for array in kept[1])
    grad_down = outer_sum(back_hidden, grad_rows) + outer_sum(back_hidden_x, grad_rows_x)
    grad_gate = outer_sum(gate_grad, back_rows) + outer_sum(gate_grad_x, back_rows_x)
    grad_up = outer_sum(up_grad, back_rows) + outer_sum(up_grad_x, back_rows_x)
    return (
        expert_out[None],
        input_grad[None],
        grad_gate.astype(jnp.bfloat16)[None],
        grad_up.astype(jnp.bfloat16)[None],
        grad_down.astype(jnp.bfloat16)[None],
    )


def solution(mesh):
    placed = (
        P("section", "expert", "mp"),
        P("section", "expert", None),
        P("section", "expert", None),
        P("section", None, "expert", "mp"),
        P("section", "expert"),
        P("section", "expert", None),
        P("section", "expert", None),
        P("section", "expert", "mp"),
        P("section"),
        P("section", ("expert", "mp"), None),
        P("section", ("expert", "mp"), None),
        P("section", ("expert", "mp"), None),
    )
    return jax.shard_map(
        per_device,
        mesh=mesh,
        in_specs=placed,
        out_specs=(
            P("section", "expert", "mp"),
            P("section", "expert", "mp"),
            P("section", ("expert", "mp"), None),
            P("section", ("expert", "mp"), None),
            P("section", ("expert", "mp"), None),
        ),
        check_vma=False,
    )
```

```python
import jax
import jax.numpy as jnp
from jax import lax
from jax.sharding import PartitionSpec as P

CAP = 64


def after(array, *others):
    return lax.optimization_barrier((array, *others))[0]


def along_y(array, step):
    n = lax.axis_size("expert")
    return lax.ppermute(array, "expert", [(i, (i + 2 * step) % n) for i in range(n)])


def other_core(array):
    n = lax.axis_size("expert")
    return lax.ppermute(array, "expert", [(i, i ^ 1) for i in range(n)])


def along_mp(array, flip):
    n = lax.axis_size("mp")
    return lax.ppermute(array, "mp", [(i, i ^ flip) for i in range(n)])


def mirrored(array):
    n = lax.axis_size("section")
    return lax.ppermute(array, "section", [(i, n - 1 - i) for i in range(n)])


def routing(pair_ids, pair_weights, expert):
    matches = pair_ids == expert
    routed = jnp.any(matches, axis=1)
    counted = routed.astype(jnp.int32)
    slot_of = jnp.cumsum(counted) - counted
    gate_share = jnp.sum(jnp.where(matches, pair_weights, 0.0), axis=1)
    return (gate_share, jnp.where(routed, slot_of, CAP))


def picker_of(slot_or_cap):
    places = jnp.arange(CAP, dtype=jnp.int32)[:, None]
    return slot_or_cap[None, :] == places


def pack(picker, values):
    return jnp.dot(
        picker.astype(jnp.bfloat16), values, preferred_element_type=jnp.float32
    ).astype(jnp.bfloat16)


def unpack(picker, rows):
    return lax.dot_general(
        picker.astype(jnp.bfloat16),
        rows,
        (((0,), (0,)), ((), ())),
        preferred_element_type=jnp.float32,
    ).astype(jnp.bfloat16)


def swapped(flag, first, second):
    return (jnp.where(flag, second, first), jnp.where(flag, first, second))


def widen(block, place):
    one, two, three = (along_mp(block, 1), along_mp(block, 2), along_mp(block, 3))
    odd, high = (place & 1) == 1, (place & 2) == 2
    a0, a1 = swapped(odd, block, one)
    a2, a3 = swapped(odd, two, three)
    b0, b2 = swapped(high, a0, a2)
    b1, b3 = swapped(high, a1, a3)
    return jnp.concatenate([b0, b1, b2, b3], axis=1)


def ring_near(block):
    return (block, along_y(block, 1), along_y(block, -1))


def ring_far(near):
    block, behind, ahead = near
    half = block.shape[0] // 2
    far_low = along_y(behind[:half], 1)
    far_high = along_y(ahead[half:], -1)
    return jnp.concatenate([block, behind, ahead, far_low, far_high], axis=0)


def project(rows, weight):
    return lax.dot_general(
        rows, weight, (((1,), (1,)), ((), ())), preferred_element_type=jnp.float32
    )


def outer_sum(left, right):
    return lax.dot_general(
        left, right, (((0,), (0,)), ((), ())), preferred_element_type=jnp.float32
    )


def spread(hidden, weight):
    return jnp.dot(hidden, weight, preferred_element_type=jnp.float32)


def scatter_y(term):
    own, behind, ahead, far = (term[i * CAP : (i + 1) * CAP] for i in range(4))
    behind, ahead, far = (block.astype(jnp.bfloat16) for block in (behind, ahead, far))
    return (own, along_y(behind, -1), along_y(ahead, 1), along_y(far, 2))


def scatter_mp(parts, place):
    total = parts[0]
    for part in parts[1:]:
        total = total + part.astype(jnp.float32)
    width = total.shape[1] // 4

    def columns(array, index):
        return lax.dynamic_slice_in_dim(array, index * width, width, axis=1)

    low = total.astype(jnp.bfloat16)
    result = columns(total, place)
    for flip in (1, 2, 3):
        result = result + along_mp(columns(low, place ^ flip), flip).astype(jnp.float32)
    return result


def per_device(
    tokens_in,
    route_ids,
    route_weights,
    stash,
    returned_batch_index,
    back_ids,
    back_weights,
    upstream,
    window_expert,
    w_gate,
    w_up,
    w_down,
):
    expert = window_expert[0]
    place = lax.axis_index("mp")
    gate_w, up_w, down_w = (w_gate[0], w_up[0], w_down[0])
    fwd_gate, fwd_slot = routing(route_ids[0], route_weights[0], expert)
    fwd_pick = picker_of(fwd_slot)
    back_gate, back_slot = routing(back_ids[0], back_weights[0], expert)
    back_pick = picker_of(back_slot)

    fwd_buf = pack(fwd_pick, tokens_in[0])
    grad_tokens = (back_gate[:, None] * upstream[0].astype(jnp.float32)).astype(jnp.bfloat16)
    grad_buf = pack(back_pick, grad_tokens)
    held_rows = lax.dynamic_index_in_dim(
        stash[0], returned_batch_index[0, 0], axis=0, keepdims=False
    )
    fwd_wide = widen(fwd_buf, place)
    fwd_near = ring_near(fwd_wide)
    grad_wide = widen(after(grad_buf, fwd_wide), place)
    back_buf = pack(back_pick, mirrored(after(held_rows, fwd_wide)))
    gate_x, up_x, down_x = (other_core(after(array, fwd_wide)) for array in (gate_w, up_w, down_w))
    fwd_rows = ring_far(fwd_near)
    grad_near = ring_near(after(grad_wide, *fwd_near))
    back_wide = widen(back_buf, place)
    grad_rows = ring_far(grad_near)
    back_near = ring_near(after(back_wide, *grad_near))
    back_rows = ring_far(back_near)

    fwd_term = 0.0
    for gate, up, down in ((gate_w, up_w, down_w), (gate_x, up_x, down_x)):
        fwd_pre = project(fwd_rows, gate)
        fwd_hidden = (fwd_pre * jax.nn.sigmoid(fwd_pre) * project(fwd_rows, up)).astype(
            jnp.bfloat16
        )
        fwd_term = fwd_term + spread(fwd_hidden, down)
    fwd_parts = scatter_y(after(fwd_term, *back_near))
    fwd_sum = scatter_mp(fwd_parts, place)
    fwd_row_gate = jnp.sum(jnp.where(fwd_pick, fwd_gate[None, :], 0.0), axis=1)
    expert_out = unpack(fwd_pick, (fwd_sum * fwd_row_gate[:, None]).astype(jnp.bfloat16))

    grad_rows_x = other_core(grad_rows)
    back_rows_x = other_core(back_rows)
    back_term = 0.0
    kept = []
    for gate, up, down in ((gate_w, up_w, down_w), (gate_x, up_x, down_x)):
        hidden_grad = project(grad_rows, down)
        pre_gate = project(back_rows, gate)
        pre_up = project(back_rows, up)
        sigmoid_pre = jax.nn.sigmoid(pre_gate)
        activated = pre_gate * sigmoid_pre
        back_hidden = (activated * pre_up).astype(jnp.bfloat16)
        gate_grad = (
            hidden_grad * pre_up * sigmoid_pre * (1.0 + pre_gate * (1.0 - sigmoid_pre))
        ).astype(jnp.bfloat16)
        up_grad = (hidden_grad * activated).astype(jnp.bfloat16)
        kept.append((back_hidden, gate_grad, up_grad))
        back_term = back_term + (spread(gate_grad, gate) + spread(up_grad, up))
    back_parts = scatter_y(back_term)
    back_hidden, gate_grad, up_grad = kept[0]
    back_hidden_x, gate_grad_x, up_grad_x = (other_core(array) for array in kept[1])
    grad_down = outer_sum(back_hidden, grad_rows) + outer_sum(back_hidden_x, grad_rows_x)
    grad_gate = outer_sum(gate_grad, back_rows) + outer_sum(gate_grad_x, back_rows_x)
    grad_up = outer_sum(up_grad, back_rows) + outer_sum(up_grad_x, back_rows_x)
    grads = tuple(array.astype(jnp.bfloat16) for array in (grad_gate, grad_up, grad_down))
    back_parts, grads = lax.optimization_barrier((back_parts, grads))
    back_sum = scatter_mp(back_parts, place)
    input_grad = unpack(back_pick, back_sum.astype(jnp.bfloat16))
    return (
        expert_out[None],
        input_grad[None],
        grads[0][None],
        grads[1][None],
        grads[2][None],
    )


def solution(mesh):
    placed = (
        P("section", "expert", "mp"),
        P("section", "expert", None),
        P("section", "expert", None),
        P("section", None, "expert", "mp"),
        P("section", "expert"),
        P("section", "expert", None),
        P("section", "expert", None),
        P("section", "expert", "mp"),
        P("section"),
        P("section", ("expert", "mp"), None),
        P("section", ("expert", "mp"), None),
        P("section", ("expert", "mp"), None),
    )
    return jax.shard_map(
        per_device,
        mesh=mesh,
        in_specs=placed,
        out_specs=(
            P("section", "expert", "mp"),
            P("section", "expert", "mp"),
            P("section", ("expert", "mp"), None),
            P("section", ("expert", "mp"), None),
            P("section", ("expert", "mp"), None),
        ),
        check_vma=False,
    )
```

```python
import jax
import jax.numpy as jnp
from jax import lax
from jax.experimental import pallas as pl
from jax.experimental.pallas import tpu as pltpu
from jax.sharding import PartitionSpec as P

CAP = 64


def together(*arrays):
    return lax.optimization_barrier(arrays)


def along_y(array, step):
    n = lax.axis_size("expert")
    return lax.ppermute(array, "expert", [(i, (i + 2 * step) % n) for i in range(n)])


def other_core(array):
    n = lax.axis_size("expert")
    return lax.ppermute(array, "expert", [(i, i ^ 1) for i in range(n)])


def along_mp(array, flip):
    n = lax.axis_size("mp")
    return lax.ppermute(array, "mp", [(i, i ^ flip) for i in range(n)])


def mirrored(array):
    n = lax.axis_size("section")
    return lax.ppermute(array, "section", [(i, n - 1 - i) for i in range(n)])


def routing(pair_ids, pair_weights, expert):
    matches = pair_ids == expert
    routed = jnp.any(matches, axis=1)
    counted = routed.astype(jnp.int32)
    slot_of = jnp.cumsum(counted) - counted
    gate_share = jnp.sum(jnp.where(matches, pair_weights, 0.0), axis=1)
    return (gate_share, jnp.where(routed, slot_of, CAP))


def picker_of(slot_or_cap):
    places = jnp.arange(CAP, dtype=jnp.int32)[:, None]
    return slot_or_cap[None, :] == places


def pack(picker, values):
    return jnp.dot(
        picker.astype(jnp.bfloat16), values, preferred_element_type=jnp.float32
    ).astype(jnp.bfloat16)


def unpack(picker, rows):
    return lax.dot_general(
        picker.astype(jnp.bfloat16),
        rows,
        (((0,), (0,)), ((), ())),
        preferred_element_type=jnp.float32,
    ).astype(jnp.bfloat16)


def swapped(flag, first, second):
    return (jnp.where(flag, second, first), jnp.where(flag, first, second))


def ask_mp(block):
    return (block, along_mp(block, 1), along_mp(block, 2), along_mp(block, 3))


def widen(blocks, place):
    block, one, two, three = blocks
    odd, high = (place & 1) == 1, (place & 2) == 2
    a0, a1 = swapped(odd, block, one)
    a2, a3 = swapped(odd, two, three)
    b0, b2 = swapped(high, a0, a2)
    b1, b3 = swapped(high, a1, a3)
    return jnp.concatenate([b0, b1, b2, b3], axis=1)


def ring_near(block):
    return (along_y(block, 1), along_y(block, -1))


def ring_far(behind, ahead):
    half = behind.shape[0] // 2
    return (along_y(behind[:half], 1), along_y(ahead[half:], -1))


def fetch(sources, target, sems, first):
    copies = []
    start = 0
    for index, source in enumerate(sources):
        rows = source.shape[0]
        copies.append(
            pltpu.make_async_copy(source, target.at[pl.ds(start, rows)], sems.at[first + index])
        )
        start += rows
    for copy in copies:
        copy.start()
    return copies


def arrive(copies):
    for copy in copies:
        copy.wait()


def times_rows(weight, rows):
    return lax.dot_general(
        weight, rows, (((1,), (1,)), ((), ())), preferred_element_type=jnp.float32
    )


def spread_kernel_part(pairs, own_ref, far_refs):
    width = own_ref.shape[1]
    step = min(width, 1024)
    for left in range(0, width, step):
        columns = slice(left, left + step)
        term = 0.0
        for hidden, weight in pairs:
            term = term + lax.dot_general(
                hidden,
                weight[:, columns],
                (((0,), (0,)), ((), ())),
                preferred_element_type=jnp.float32,
            )
        own_ref[:, columns] = term[:CAP]
        for index, ref in enumerate(far_refs):
            ref[:, columns] = term[CAP * (index + 1) : CAP * (index + 2)].astype(jnp.bfloat16)


def fwd_kernel(*refs):
    pieces = refs[:5]
    gate_own, up_own, down_own, gate_x, up_x, down_x = refs[5:11]
    own_ref, behind_ref, ahead_ref, far_ref = refs[11:15]
    rows, gate, up, down, sems = refs[15:]
    rows_in = fetch(pieces, rows, sems, 0)
    gate_in = fetch((gate_own, gate_x), gate, sems, 5)
    up_in = fetch((up_own, up_x), up, sems, 7)
    down_in = fetch((down_own, down_x), down, sems, 9)
    arrive(rows_in)
    arrive(gate_in)
    pre = times_rows(gate[...], rows[...])
    arrive(up_in)
    hidden = (pre * jax.nn.sigmoid(pre) * times_rows(up[...], rows[...])).astype(jnp.bfloat16)
    arrive(down_in)
    spread_kernel_part(((hidden, down),), own_ref, (behind_ref, ahead_ref, far_ref))


def grad_kernel(*refs):
    pieces = refs[:5]
    down_own, down_x, hidden_ref, rows_out, rows, down, sems = refs[5:]
    rows_in = fetch(pieces, rows, sems, 0)
    down_in = fetch((down_own, down_x), down, sems, 5)
    arrive(rows_in)
    keep = pltpu.make_async_copy(rows, rows_out, sems.at[7])
    keep.start()
    arrive(down_in)
    hidden_ref[...] = times_rows(down[...], rows[...])
    keep.wait()


def back_kernel(*refs):
    pieces = refs[:5]
    hidden_grad_ref, gate_own, up_own, gate_x, up_x = refs[5:10]
    own_ref, behind_ref, ahead_ref, far_ref, hidden_ref, gate_grad_ref, up_grad_ref = refs[10:17]
    rows_out, rows, gate, up, sems = refs[17:]
    rows_in = fetch(pieces, rows, sems, 0)
    gate_in = fetch((gate_own, gate_x), gate, sems, 5)
    up_in = fetch((up_own, up_x), up, sems, 7)
    arrive(rows_in)
    keep = pltpu.make_async_copy(rows, rows_out, sems.at[9])
    keep.start()
    arrive(gate_in)
    pre_gate = times_rows(gate[...], rows[...])
    arrive(up_in)
    pre_up = times_rows(up[...], rows[...])
    sigmoid_pre = jax.nn.sigmoid(pre_gate)
    activated = pre_gate * sigmoid_pre
    hidden_grad = hidden_grad_ref[...]
    hidden_ref[...] = (activated * pre_up).astype(jnp.bfloat16)
    gate_grad = (
        hidden_grad * pre_up * sigmoid_pre * (1.0 + pre_gate * (1.0 - sigmoid_pre))
    ).astype(jnp.bfloat16)
    up_grad = (hidden_grad * activated).astype(jnp.bfloat16)
    gate_grad_ref[...] = gate_grad
    up_grad_ref[...] = up_grad
    spread_kernel_part(
        ((gate_grad, gate), (up_grad, up)), own_ref, (behind_ref, ahead_ref, far_ref)
    )
    keep.wait()


ANY = pl.BlockSpec(memory_space=pl.ANY)
VMEM = pl.BlockSpec(memory_space=pltpu.VMEM)
LIMIT = 30 * 2**20


def block_shapes(width):
    narrow = jax.ShapeDtypeStruct((CAP, width), jnp.bfloat16)
    return (jax.ShapeDtypeStruct((CAP, width), jnp.float32), narrow, narrow, narrow)


def rows_shape(width):
    return jax.ShapeDtypeStruct((4 * CAP, width), jnp.bfloat16)


def run_fwd(pieces, weights):
    units, width = weights[0].shape
    return pl.pallas_call(
        fwd_kernel,
        out_shape=block_shapes(width),
        in_specs=[ANY] * 11,
        out_specs=(VMEM,) * 4,
        scratch_shapes=[pltpu.VMEM((4 * CAP, width), jnp.bfloat16)]
        + [pltpu.VMEM((2 * units, width), jnp.bfloat16)] * 3
        + [pltpu.SemaphoreType.DMA((11,))],
        compiler_params=pltpu.CompilerParams(vmem_limit_bytes=LIMIT),
        cost_estimate=pl.CostEstimate(
            flops=6 * 4 * CAP * 2 * units * width,
            bytes_accessed=2 * width * (6 * units + 8 * CAP),
            transcendentals=0,
        ),
    )(*pieces, *weights)


def run_grad(pieces, weights):
    units, width = weights[0].shape
    return pl.pallas_call(
        grad_kernel,
        out_shape=(
            jax.ShapeDtypeStruct((2 * units, 4 * CAP), jnp.float32),
            rows_shape(width),
        ),
        in_specs=[ANY] * 7,
        out_specs=(VMEM, ANY),
        scratch_shapes=[
            pltpu.VMEM((4 * CAP, width), jnp.bfloat16),
            pltpu.VMEM((2 * units, width), jnp.bfloat16),
            pltpu.SemaphoreType.DMA((8,)),
        ],
        compiler_params=pltpu.CompilerParams(vmem_limit_bytes=LIMIT),
        cost_estimate=pl.CostEstimate(
            flops=2 * 4 * CAP * 2 * units * width,
            bytes_accessed=2 * width * (2 * units + 8 * CAP),
            transcendentals=0,
        ),
    )(*pieces, *weights)


def run_back(pieces, hidden_grad, weights):
    units, width = weights[0].shape
    hidden = jax.ShapeDtypeStruct((2 * units, 4 * CAP), jnp.bfloat16)
    return pl.pallas_call(
        back_kernel,
        out_shape=block_shapes(width) + (hidden, hidden, hidden, rows_shape(width)),
        in_specs=[ANY] * 5 + [VMEM] + [ANY] * 4,
        out_specs=(VMEM,) * 7 + (ANY,),
        scratch_shapes=[pltpu.VMEM((4 * CAP, width), jnp.bfloat16)]
        + [pltpu.VMEM((2 * units, width), jnp.bfloat16)] * 2
        + [pltpu.SemaphoreType.DMA((11,))],
        compiler_params=pltpu.CompilerParams(vmem_limit_bytes=LIMIT),
        cost_estimate=pl.CostEstimate(
            flops=8 * 4 * CAP * 2 * units * width,
            bytes_accessed=2 * width * (4 * units + 12 * CAP),
            transcendentals=0,
        ),
    )(*pieces, hidden_grad, *weights)


def outer_sum(left, right):
    return jnp.dot(left, right, preferred_element_type=jnp.float32)


def add_parts(own, parts):
    total = own
    for part in parts:
        total = total + part.astype(jnp.float32)
    return total


def split_mp(total, place):
    width = total.shape[1] // 4

    def columns(array, index):
        return lax.dynamic_slice_in_dim(array, index * width, width, axis=1)

    low = total.astype(jnp.bfloat16)
    return (columns(total, place),) + tuple(columns(low, place ^ flip) for flip in (1, 2, 3))


def send_mp(blocks):
    return tuple(along_mp(block, flip) for flip, block in zip((1, 2, 3), blocks))


def per_device(
    tokens_in,
    route_ids,
    route_weights,
    stash,
    returned_batch_index,
    back_ids,
    back_weights,
    upstream,
    window_expert,
    w_gate,
    w_up,
    w_down,
):
    expert = window_expert[0]
    place = lax.axis_index("mp")
    gate_w, up_w, down_w = (w_gate[0], w_up[0], w_down[0])
    fwd_gate, fwd_slot = routing(route_ids[0], route_weights[0], expert)
    fwd_pick = picker_of(fwd_slot)
    back_gate, back_slot = routing(back_ids[0], back_weights[0], expert)
    back_pick = picker_of(back_slot)

    fwd_buf = pack(fwd_pick, tokens_in[0])
    grad_tokens = (back_gate[:, None] * upstream[0].astype(jnp.float32)).astype(jnp.bfloat16)
    grad_buf = pack(back_pick, grad_tokens)
    held_rows = lax.dynamic_index_in_dim(
        stash[0], returned_batch_index[0, 0], axis=0, keepdims=False
    )
    held_rows, fwd_buf, grad_buf = together(held_rows, fwd_buf, grad_buf)
    fwd_blocks = together(*ask_mp(fwd_buf))

    fwd_wide, grad_buf, held_rows = together(widen(fwd_blocks, place), grad_buf, held_rows)
    fwd_near = ring_near(fwd_wide)
    *fwd_near, held_rows, one, two, three, four = together(
        *fwd_near, mirrored(held_rows), *ask_mp(grad_buf)
    )
    weights = (gate_w, up_w, down_w)

    grad_wide, back_buf, *fwd_near = together(
        widen((one, two, three, four), place), pack(back_pick, held_rows), *fwd_near
    )
    fwd_far = ring_far(*fwd_near)
    grad_near = ring_near(grad_wide)
    *fwd_far, b0, b1, one, two, three, four = together(*fwd_far, *grad_near, *ask_mp(back_buf))
    grad_near = (b0, b1)
    weights_x = tuple(other_core(array) for array in weights)

    back_wide, *grad_near = together(widen((one, two, three, four), place), *grad_near)
    grad_far = ring_far(*grad_near)
    back_near = ring_near(back_wide)
    fwd_terms = run_fwd((fwd_wide, *fwd_near, *fwd_far), weights + weights_x)
    f0, f1, b0, b1, *fwd_terms = together(*grad_far, *back_near, *fwd_terms)
    grad_far, back_near = (f0, f1), (b0, b1)

    back_far = ring_far(*back_near)
    fwd_far_part = along_y(fwd_terms[3], 2)
    hidden_grad, grad_rows = run_grad(
        (grad_wide, *grad_near, *grad_far), (down_w, weights_x[2])
    )
    f0, f1, fwd_far_part, hidden_grad, grad_rows, *fwd_terms = together(
        *back_far, fwd_far_part, hidden_grad, grad_rows, *fwd_terms
    )
    back_far = (f0, f1)

    fwd_parts = (along_y(fwd_terms[1], -1), along_y(fwd_terms[2], 1))
    grad_rows_x = other_core(grad_rows)
    back_terms = run_back(
        (back_wide, *back_near, *back_far),
        hidden_grad,
        (gate_w, up_w, weights_x[0], weights_x[1]),
    )
    p0, p1, grad_rows_x, *back_terms = together(*fwd_parts, grad_rows_x, *back_terms)
    hidden_all, back_rows = back_terms[4:7], back_terms[7]

    fwd_total = add_parts(fwd_terms[0], (p0, p1, fwd_far_part))
    fwd_here, *fwd_sent = split_mp(fwd_total, place)
    fwd_sent = send_mp(fwd_sent)
    back_parts = (
        along_y(back_terms[1], -1),
        along_y(back_terms[2], 1),
        along_y(back_terms[3], 2),
    )
    units = gate_w.shape[0]
    back_rows_x = other_core(back_rows)
    hidden_x = tuple(other_core(array[units:]) for array in hidden_all)
    grads = []
    for hidden, other, rows, rows_x in zip(
        hidden_all,
        hidden_x,
        (grad_rows, back_rows, back_rows),
        (grad_rows_x, back_rows_x, back_rows_x),
    ):
        grads.append(
            (outer_sum(hidden[:units], rows) + outer_sum(other, rows_x)).astype(jnp.bfloat16)
        )
    p0, p1, p2, s0, s1, s2, fwd_here, *grads = together(
        *back_parts, *fwd_sent, fwd_here, *grads
    )
    fwd_sum = add_parts(fwd_here, (s0, s1, s2))
    fwd_row_gate = jnp.sum(jnp.where(fwd_pick, fwd_gate[None, :], 0.0), axis=1)
    expert_out = unpack(fwd_pick, (fwd_sum * fwd_row_gate[:, None]).astype(jnp.bfloat16))

    back_here, *back_sent = split_mp(add_parts(back_terms[0], (p0, p1, p2)), place)
    back_sum = add_parts(back_here, send_mp(back_sent))
    input_grad = unpack(back_pick, back_sum.astype(jnp.bfloat16))
    grad_down, grad_gate, grad_up = grads
    return (
        expert_out[None],
        input_grad[None],
        grad_gate[None],
        grad_up[None],
        grad_down[None],
    )


def solution(mesh):
    placed = (
        P("section", "expert", "mp"),
        P("section", "expert", None),
        P("section", "expert", None),
        P("section", None, "expert", "mp"),
        P("section", "expert"),
        P("section", "expert", None),
        P("section", "expert", None),
        P("section", "expert", "mp"),
        P("section"),
        P("section", ("expert", "mp"), None),
        P("section", ("expert", "mp"), None),
        P("section", ("expert", "mp"), None),
    )
    return jax.shard_map(
        per_device,
        mesh=mesh,
        in_specs=placed,
        out_specs=(
            P("section", "expert", "mp"),
            P("section", "expert", "mp"),
            P("section", ("expert", "mp"), None),
            P("section", ("expert", "mp"), None),
            P("section", ("expert", "mp"), None),
        ),
        check_vma=False,
    )
```

```python
import jax
import jax.numpy as jnp
from jax import lax
from jax.experimental import pallas as pl
from jax.experimental.pallas import tpu as pltpu
from jax.sharding import PartitionSpec as P

CAP = 64


def together(*arrays):
    return lax.optimization_barrier(arrays)


def along_y(array, step):
    n = lax.axis_size("expert")
    return lax.ppermute(array, "expert", [(i, (i + 2 * step) % n) for i in range(n)])


def other_core(array):
    n = lax.axis_size("expert")
    return lax.ppermute(array, "expert", [(i, i ^ 1) for i in range(n)])


def along_mp(array, flip):
    n = lax.axis_size("mp")
    return lax.ppermute(array, "mp", [(i, i ^ flip) for i in range(n)])


def mirrored(array):
    n = lax.axis_size("section")
    return lax.ppermute(array, "section", [(i, n - 1 - i) for i in range(n)])


def routing(pair_ids, pair_weights, expert):
    matches = pair_ids == expert
    routed = jnp.any(matches, axis=1)
    counted = routed.astype(jnp.int32)
    slot_of = jnp.cumsum(counted) - counted
    gate_share = jnp.sum(jnp.where(matches, pair_weights, 0.0), axis=1)
    return (gate_share, jnp.where(routed, slot_of, CAP))


def picker_of(slot_or_cap):
    places = jnp.arange(CAP, dtype=jnp.int32)[:, None]
    return slot_or_cap[None, :] == places


def pack(picker, values):
    return jnp.dot(
        picker.astype(jnp.bfloat16), values, preferred_element_type=jnp.float32
    ).astype(jnp.bfloat16)


def unpack(picker, rows):
    return lax.dot_general(
        picker.astype(jnp.bfloat16),
        rows,
        (((0,), (0,)), ((), ())),
        preferred_element_type=jnp.float32,
    ).astype(jnp.bfloat16)


def swapped(flag, first, second):
    return (jnp.where(flag, second, first), jnp.where(flag, first, second))


def beside(flag, here, there):
    first, second = swapped(flag, here, there)
    return jnp.concatenate([first, second], axis=1)


def widen_at_once(block, place):
    odd, high = (place & 1) == 1, (place & 2) == 2
    one, two, three = together(*(along_mp(block, flip) for flip in (1, 2, 3)))
    return beside(high, beside(odd, block, one), beside(odd, two, three))


def widen_by_steps(block, place):
    odd, high = (place & 1) == 1, (place & 2) == 2
    pair = beside(odd, block, along_mp(block, 1))
    return beside(high, pair, along_mp(pair, 2))


def ring_near(block):
    return (along_y(block, 1), along_y(block, -1))


def ring_far(behind, ahead):
    half = behind.shape[0] // 2
    return (along_y(behind[:half], 1), along_y(ahead[half:], -1))


def fetch(sources, target, sems, first):
    copies = []
    start = 0
    for index, source in enumerate(sources):
        rows = source.shape[0]
        copies.append(
            pltpu.make_async_copy(source, target.at[pl.ds(start, rows)], sems.at[first + index])
        )
        start += rows
    for copy in copies:
        copy.start()
    return copies


def arrive(copies):
    for copy in copies:
        copy.wait()


def times_rows(weight, rows):
    return lax.dot_general(
        weight, rows, (((1,), (1,)), ((), ())), preferred_element_type=jnp.float32
    )


def spread_kernel_part(pairs, own_ref, far_refs):
    width = own_ref.shape[1]
    step = min(width, 1024)
    for left in range(0, width, step):
        columns = slice(left, left + step)
        term = 0.0
        for hidden, weight in pairs:
            term = term + lax.dot_general(
                hidden,
                weight[:, columns],
                (((0,), (0,)), ((), ())),
                preferred_element_type=jnp.float32,
            )
        own_ref[:, columns] = term[:CAP]
        for index, ref in enumerate(far_refs):
            ref[:, columns] = term[CAP * (index + 1) : CAP * (index + 2)].astype(jnp.bfloat16)


def fwd_kernel(*refs):
    pieces = refs[:5]
    gate_own, up_own, down_own, gate_x, up_x, down_x = refs[5:11]
    own_ref, behind_ref, ahead_ref, far_ref = refs[11:15]
    rows, gate, up, down, sems = refs[15:]
    rows_in = fetch(pieces, rows, sems, 0)
    gate_in = fetch((gate_own, gate_x), gate, sems, 5)
    up_in = fetch((up_own, up_x), up, sems, 7)
    down_in = fetch((down_own, down_x), down, sems, 9)
    arrive(rows_in)
    arrive(gate_in)
    pre = times_rows(gate[...], rows[...])
    arrive(up_in)
    hidden = (pre * jax.nn.sigmoid(pre) * times_rows(up[...], rows[...])).astype(jnp.bfloat16)
    arrive(down_in)
    spread_kernel_part(((hidden, down),), own_ref, (behind_ref, ahead_ref, far_ref))


def grad_kernel(*refs):
    pieces = refs[:5]
    down_own, down_x, hidden_ref, rows_out, rows, down, sems = refs[5:]
    rows_in = fetch(pieces, rows, sems, 0)
    down_in = fetch((down_own, down_x), down, sems, 5)
    arrive(rows_in)
    keep = pltpu.make_async_copy(rows, rows_out, sems.at[7])
    keep.start()
    arrive(down_in)
    hidden_ref[...] = times_rows(down[...], rows[...])
    keep.wait()


def back_kernel(*refs):
    pieces = refs[:5]
    hidden_grad_ref, gate_own, up_own, gate_x, up_x = refs[5:10]
    own_ref, behind_ref, ahead_ref, far_ref, keep_ref, send_ref = refs[10:16]
    rows, gate, up, sems = refs[16:]
    units = gate_own.shape[0]
    rows_in = fetch(pieces, rows, sems, 0)
    gate_in = fetch((gate_own, gate_x), gate, sems, 5)
    up_in = fetch((up_own, up_x), up, sems, 7)
    arrive(rows_in)
    arrive(gate_in)
    pre_gate = times_rows(gate[...], rows[...])
    arrive(up_in)
    pre_up = times_rows(up[...], rows[...])
    sigmoid_pre = jax.nn.sigmoid(pre_gate)
    activated = pre_gate * sigmoid_pre
    hidden_grad = hidden_grad_ref[...]
    hidden = (activated * pre_up).astype(jnp.bfloat16)
    gate_grad = (
        hidden_grad * pre_up * sigmoid_pre * (1.0 + pre_gate * (1.0 - sigmoid_pre))
    ).astype(jnp.bfloat16)
    up_grad = (hidden_grad * activated).astype(jnp.bfloat16)
    for index, array in enumerate((hidden, gate_grad, up_grad)):
        keep_ref[units * index : units * (index + 1)] = array[:units]
        send_ref[units * index : units * (index + 1)] = array[units:]
    spread_kernel_part(
        ((gate_grad, gate), (up_grad, up)), own_ref, (behind_ref, ahead_ref, far_ref)
    )


HBM = pl.BlockSpec(memory_space=pltpu.HBM)
VMEM = pl.BlockSpec(memory_space=pltpu.VMEM)
LIMIT = 30 * 2**20


def block_shapes(width):
    narrow = jax.ShapeDtypeStruct((CAP, width), jnp.bfloat16)
    return (jax.ShapeDtypeStruct((CAP, width), jnp.float32), narrow, narrow, narrow)


def rows_shape(width):
    return jax.ShapeDtypeStruct((4 * CAP, width), jnp.bfloat16)


def run_fwd(pieces, weights):
    units, width = weights[0].shape
    return pl.pallas_call(
        fwd_kernel,
        out_shape=block_shapes(width),
        in_specs=[HBM] * 11,
        out_specs=(VMEM,) * 4,
        scratch_shapes=[pltpu.VMEM((4 * CAP, width), jnp.bfloat16)]
        + [pltpu.VMEM((2 * units, width), jnp.bfloat16)] * 3
        + [pltpu.SemaphoreType.DMA((11,))],
        compiler_params=pltpu.CompilerParams(vmem_limit_bytes=LIMIT),
        cost_estimate=pl.CostEstimate(
            flops=6 * 4 * CAP * 2 * units * width,
            bytes_accessed=2 * width * (6 * units + 8 * CAP),
            transcendentals=0,
        ),
    )(*pieces, *weights)


def run_grad(pieces, weights):
    units, width = weights[0].shape
    return pl.pallas_call(
        grad_kernel,
        out_shape=(
            jax.ShapeDtypeStruct((2 * units, 4 * CAP), jnp.float32),
            rows_shape(width),
        ),
        in_specs=[HBM] * 7,
        out_specs=(VMEM, HBM),
        scratch_shapes=[
            pltpu.VMEM((4 * CAP, width), jnp.bfloat16),
            pltpu.VMEM((2 * units, width), jnp.bfloat16),
            pltpu.SemaphoreType.DMA((8,)),
        ],
        compiler_params=pltpu.CompilerParams(vmem_limit_bytes=LIMIT),
        cost_estimate=pl.CostEstimate(
            flops=2 * 4 * CAP * 2 * units * width,
            bytes_accessed=2 * width * (2 * units + 8 * CAP),
            transcendentals=0,
        ),
    )(*pieces, *weights)


def run_back(pieces, hidden_grad, weights):
    units, width = weights[0].shape
    hidden = jax.ShapeDtypeStruct((3 * units, 4 * CAP), jnp.bfloat16)
    return pl.pallas_call(
        back_kernel,
        out_shape=block_shapes(width) + (hidden, hidden),
        in_specs=[HBM] * 5 + [VMEM] + [HBM] * 4,
        out_specs=(VMEM,) * 6,
        scratch_shapes=[pltpu.VMEM((4 * CAP, width), jnp.bfloat16)]
        + [pltpu.VMEM((2 * units, width), jnp.bfloat16)] * 2
        + [pltpu.SemaphoreType.DMA((9,))],
        compiler_params=pltpu.CompilerParams(vmem_limit_bytes=LIMIT),
        cost_estimate=pl.CostEstimate(
            flops=8 * 4 * CAP * 2 * units * width,
            bytes_accessed=2 * width * (4 * units + 12 * CAP),
            transcendentals=0,
        ),
    )(*pieces, hidden_grad, *weights)


def outer_sum(left, right):
    return jnp.dot(left, right, preferred_element_type=jnp.float32)


def add_parts(own, parts):
    total = own
    for part in parts:
        total = total + part.astype(jnp.float32)
    return total


def far_halves(far):
    half = far.shape[0] // 2
    return (along_y(far[:half], 1), along_y(far[half:], -1))


def near_with_far(behind, ahead, from_behind, from_ahead):
    half = from_behind.shape[0]

    def plus(block, start, extra):
        padded = jnp.pad(extra, ((start, block.shape[0] - half - start), (0, 0)))
        return (block.astype(jnp.float32) + padded.astype(jnp.float32)).astype(jnp.bfloat16)

    return (along_y(plus(behind, half, from_ahead), -1), along_y(plus(ahead, 0, from_behind), 1))


def halves(total):
    middle = total.shape[1] // 2
    return (total[:, :middle], total[:, middle:])


def sum_mp_step(total, flag, flip):
    keep, give = swapped(flag, *halves(total))
    return keep + along_mp(give.astype(jnp.bfloat16), flip).astype(jnp.float32)


def sum_mp_at_once(total, place):
    width = total.shape[1] // 4

    def columns(array, index):
        return lax.dynamic_slice_in_dim(array, index * width, width, axis=1)

    low = total.astype(jnp.bfloat16)
    parts = tuple(along_mp(columns(low, place ^ flip), flip) for flip in (1, 2, 3))
    return add_parts(columns(total, place), parts)


def per_device(
    tokens_in,
    route_ids,
    route_weights,
    stash,
    returned_batch_index,
    back_ids,
    back_weights,
    upstream,
    window_expert,
    w_gate,
    w_up,
    w_down,
):
    expert = window_expert[0]
    place = lax.axis_index("mp")
    odd, high = (place & 1) == 1, (place & 2) == 2
    gate_w, up_w, down_w = (w_gate[0], w_up[0], w_down[0])
    units = gate_w.shape[0]

    fwd_gate, fwd_slot = routing(route_ids[0], route_weights[0], expert)
    fwd_pick = picker_of(fwd_slot)
    fwd_buf = pack(fwd_pick, tokens_in[0])
    back_gate, back_slot = routing(back_ids[0], back_weights[0], expert)
    held_rows = lax.dynamic_index_in_dim(
        stash[0], returned_batch_index[0, 0], axis=0, keepdims=False
    )
    fwd_wide, held_slot, gate_x = together(
        widen_at_once(fwd_buf, place), mirrored(back_slot), other_core(gate_w)
    )

    back_pick = picker_of(back_slot)
    grad_tokens = (back_gate[:, None] * upstream[0].astype(jnp.float32)).astype(jnp.bfloat16)
    grad_tokens, held_rows, up_w = together(grad_tokens, held_rows, up_w)
    fwd_behind, fwd_ahead, grad_wide, back_buf, up_x = together(
        *ring_near(fwd_wide),
        widen_by_steps(pack(back_pick, grad_tokens), place),
        mirrored(pack(picker_of(held_slot), held_rows)),
        other_core(up_w),
    )

    fwd_far_0, fwd_far_1, grad_behind, grad_ahead, back_wide, down_w = together(
        *ring_far(fwd_behind, fwd_ahead),
        *ring_near(grad_wide),
        widen_by_steps(back_buf, place),
        down_w,
    )

    down_x = other_core(down_w)
    fwd_terms = run_fwd(
        (fwd_wide, fwd_behind, fwd_ahead, fwd_far_0, fwd_far_1),
        (gate_w, up_w, down_w, gate_x, up_x, down_x),
    )
    grad_far_0, grad_far_1, back_behind, back_ahead, down_x, *fwd_terms = together(
        *ring_far(grad_behind, grad_ahead), *ring_near(back_wide), down_x, *fwd_terms
    )
    fwd_own, fwd_to_behind, fwd_to_ahead, fwd_to_far = fwd_terms

    hidden_grad, grad_rows = run_grad(
        (grad_wide, grad_behind, grad_ahead, grad_far_0, grad_far_1), (down_w, down_x)
    )
    back_far_0, back_far_1, f0, f1, hidden_grad, grad_rows_x = together(
        *ring_far(back_behind, back_ahead),
        *far_halves(fwd_to_far),
        hidden_grad,
        other_core(grad_rows),
    )

    back_pieces = (back_wide, back_behind, back_ahead, back_far_0, back_far_1)
    back_terms = run_back(back_pieces, hidden_grad, (gate_w, up_w, gate_x, up_x))
    back_rows = jnp.concatenate(back_pieces, axis=0)
    p0, p1, back_rows_x, *back_terms = together(
        *near_with_far(fwd_to_behind, fwd_to_ahead, f0, f1), other_core(back_rows), *back_terms
    )
    back_own, back_to_behind, back_to_ahead, back_to_far, hidden_keep, hidden_send = back_terms

    fwd_total = add_parts(fwd_own, (p0, p1))
    f0, f1, fwd_half, hidden_x = together(
        *far_halves(back_to_far),
        sum_mp_step(fwd_total, high, 2),
        other_core(hidden_send),
    )
    grads = []
    for index, (rows, rows_x) in enumerate(
        ((grad_rows, grad_rows_x), (back_rows, back_rows_x), (back_rows, back_rows_x))
    ):
        part = slice(units * index, units * (index + 1))
        grads.append(
            (outer_sum(hidden_keep[part], rows) + outer_sum(hidden_x[part], rows_x)).astype(
                jnp.bfloat16
            )
        )
    p0, p1, fwd_sum, *grads = together(
        *near_with_far(back_to_behind, back_to_ahead, f0, f1),
        sum_mp_step(fwd_half, odd, 1),
        *grads,
    )
    fwd_row_gate = jnp.sum(jnp.where(fwd_pick, fwd_gate[None, :], 0.0), axis=1)
    expert_out = unpack(fwd_pick, (fwd_sum * fwd_row_gate[:, None]).astype(jnp.bfloat16))

    back_sum = sum_mp_at_once(add_parts(back_own, (p0, p1)), place)
    input_grad = unpack(back_pick, back_sum.astype(jnp.bfloat16))
    grad_down, grad_gate, grad_up = grads
    return (
        expert_out[None],
        input_grad[None],
        grad_gate[None],
        grad_up[None],
        grad_down[None],
    )


def solution(mesh):
    placed = (
        P("section", "expert", "mp"),
        P("section", "expert", None),
        P("section", "expert", None),
        P("section", None, "expert", "mp"),
        P("section", "expert"),
        P("section", "expert", None),
        P("section", "expert", None),
        P("section", "expert", "mp"),
        P("section"),
        P("section", ("expert", "mp"), None),
        P("section", ("expert", "mp"), None),
        P("section", ("expert", "mp"), None),
    )
    return jax.shard_map(
        per_device,
        mesh=mesh,
        in_specs=placed,
        out_specs=(
            P("section", "expert", "mp"),
            P("section", "expert", "mp"),
            P("section", ("expert", "mp"), None),
            P("section", ("expert", "mp"), None),
            P("section", ("expert", "mp"), None),
        ),
        check_vma=False,
    )
```

```python
import jax
import jax.numpy as jnp
from jax import lax
from jax.experimental import pallas as pl
from jax.experimental.pallas import tpu as pltpu
from jax.sharding import PartitionSpec as P

CAP = 64


def together(*arrays):
    return lax.optimization_barrier(arrays)


def along_y(array, step):
    n = lax.axis_size("expert")
    return lax.ppermute(array, "expert", [(i, (i + 2 * step) % n) for i in range(n)])


def other_core(array):
    n = lax.axis_size("expert")
    return lax.ppermute(array, "expert", [(i, i ^ 1) for i in range(n)])


def along_mp(array, flip):
    n = lax.axis_size("mp")
    return lax.ppermute(array, "mp", [(i, i ^ flip) for i in range(n)])


def mirrored(array):
    n = lax.axis_size("section")
    return lax.ppermute(array, "section", [(i, n - 1 - i) for i in range(n)])


def routing(pair_ids, pair_weights, expert):
    matches = pair_ids == expert
    routed = jnp.any(matches, axis=1)
    counted = routed.astype(jnp.int32)
    slot_of = jnp.cumsum(counted) - counted
    gate_share = jnp.sum(jnp.where(matches, pair_weights, 0.0), axis=1)
    return (gate_share, jnp.where(routed, slot_of, CAP))


def picker_of(slot_or_cap):
    places = jnp.arange(CAP, dtype=jnp.int32)[:, None]
    return slot_or_cap[None, :] == places


def pack(picker, values):
    return jnp.dot(
        picker.astype(jnp.bfloat16), values, preferred_element_type=jnp.float32
    ).astype(jnp.bfloat16)


def unpack(picker, rows):
    return lax.dot_general(
        picker.astype(jnp.bfloat16),
        rows,
        (((0,), (0,)), ((), ())),
        preferred_element_type=jnp.float32,
    ).astype(jnp.bfloat16)


def swapped(flag, first, second):
    return (jnp.where(flag, second, first), jnp.where(flag, first, second))


def beside(flag, here, there):
    first, second = swapped(flag, here, there)
    return jnp.concatenate([first, second], axis=1)


def widen(block, others, place):
    one, two, three = others
    odd, high = (place & 1) == 1, (place & 2) == 2
    return beside(high, beside(odd, block, one), beside(odd, two, three))


def ask_mp(block):
    return tuple(along_mp(block, flip) for flip in (1, 2, 3))


def both_ways(to_ahead, to_behind):
    return (along_y(to_ahead, 1), along_y(to_behind, -1))


def stacked(*arrays):
    return jnp.concatenate(arrays, axis=0)


def fetch(sources, target, sems, first):
    copies = []
    into = 0
    for index, (ref, start, rows) in enumerate(sources):
        copies.append(
            pltpu.make_async_copy(
                ref.at[pl.ds(start, rows)],
                target.at[pl.ds(into, rows)],
                sems.at[first + index],
            )
        )
        into += rows
    for copy in copies:
        copy.start()
    return copies


def whole(*refs):
    return tuple((ref, 0, ref.shape[0]) for ref in refs)


def arrive(copies):
    for copy in copies:
        copy.wait()


def times_rows(weight, rows):
    return lax.dot_general(
        weight, rows, (((1,), (1,)), ((), ())), preferred_element_type=jnp.float32
    )


def spread_kernel_part(pairs, own_ref, far_refs):
    width = own_ref.shape[1]
    step = min(width, 1024)
    for left in range(0, width, step):
        columns = slice(left, left + step)
        term = 0.0
        for hidden, weight in pairs:
            term = term + lax.dot_general(
                hidden,
                weight[:, columns],
                (((0,), (0,)), ((), ())),
                preferred_element_type=jnp.float32,
            )
        own_ref[:, columns] = term[:CAP]
        for index, ref in enumerate(far_refs):
            ref[:, columns] = term[CAP * (index + 1) : CAP * (index + 2)].astype(jnp.bfloat16)


def fwd_kernel(*refs):
    wide, behind, ahead, low, high = refs[:5]
    gate_own, up_own, down_own, gate_x, up_x, down_x = refs[5:11]
    own_ref, behind_ref, ahead_ref, far_ref = refs[11:15]
    rows, gate, up, down, sems = refs[15:]
    half = CAP // 2
    rows_in = fetch(whole(wide, behind, ahead) + ((low, 0, half), (high, 0, half)), rows, sems, 0)
    gate_in = fetch(whole(gate_own, gate_x), gate, sems, 5)
    up_in = fetch(whole(up_own, up_x), up, sems, 7)
    down_in = fetch(whole(down_own, down_x), down, sems, 9)
    arrive(rows_in)
    arrive(gate_in)
    pre = times_rows(gate[...], rows[...])
    arrive(up_in)
    hidden = (pre * jax.nn.sigmoid(pre) * times_rows(up[...], rows[...])).astype(jnp.bfloat16)
    arrive(down_in)
    spread_kernel_part(((hidden, down),), own_ref, (behind_ref, ahead_ref, far_ref))


def later_rows(refs):
    wide, behind, ahead, low, high = refs
    half = CAP // 2
    return whole(wide) + (
        (behind, half, CAP),
        (ahead, half, CAP),
        (low, 0, half),
        (high, 0, half),
    )


def grad_kernel(*refs):
    down_own, down_x, hidden_ref, rows_out, rows, down, sems = refs[5:]
    rows_in = fetch(later_rows(refs[:5]), rows, sems, 0)
    down_in = fetch(whole(down_own, down_x), down, sems, 5)
    arrive(rows_in)
    keep = pltpu.make_async_copy(rows, rows_out, sems.at[7])
    keep.start()
    arrive(down_in)
    hidden_ref[...] = times_rows(down[...], rows[...])
    keep.wait()


def back_kernel(*refs):
    hidden_grad_ref, gate_own, up_own, gate_x, up_x = refs[5:10]
    own_ref, behind_ref, ahead_ref, far_ref, keep_ref, send_ref, rows_out = refs[10:17]
    rows, gate, up, sems = refs[17:]
    units = gate_own.shape[0]
    rows_in = fetch(later_rows(refs[:5]), rows, sems, 0)
    gate_in = fetch(whole(gate_own, gate_x), gate, sems, 5)
    up_in = fetch(whole(up_own, up_x), up, sems, 7)
    arrive(rows_in)
    rows_back = pltpu.make_async_copy(rows, rows_out, sems.at[9])
    rows_back.start()
    arrive(gate_in)
    pre_gate = times_rows(gate[...], rows[...])
    arrive(up_in)
    pre_up = times_rows(up[...], rows[...])
    sigmoid_pre = jax.nn.sigmoid(pre_gate)
    activated = pre_gate * sigmoid_pre
    hidden_grad = hidden_grad_ref[...]
    hidden = (activated * pre_up).astype(jnp.bfloat16)
    gate_grad = (
        hidden_grad * pre_up * sigmoid_pre * (1.0 + pre_gate * (1.0 - sigmoid_pre))
    ).astype(jnp.bfloat16)
    up_grad = (hidden_grad * activated).astype(jnp.bfloat16)
    for index, array in enumerate((hidden, gate_grad, up_grad)):
        keep_ref[units * index : units * (index + 1)] = array[:units]
        send_ref[units * index : units * (index + 1)] = array[units:]
    spread_kernel_part(
        ((gate_grad, gate), (up_grad, up)), own_ref, (behind_ref, ahead_ref, far_ref)
    )
    rows_back.wait()


def weight_kernel(hidden_ref, hidden_x_ref, grad_ref, grad_x_ref, back_ref, back_x_ref, *outs):
    units = outs[0].shape[0]
    for index, out in enumerate(outs):
        part = slice(units * index, units * (index + 1))
        rows, rows_x = (grad_ref, grad_x_ref) if index == 0 else (back_ref, back_x_ref)
        total = jnp.dot(hidden_ref[part], rows[...], preferred_element_type=jnp.float32)
        total = total + jnp.dot(
            hidden_x_ref[part], rows_x[...], preferred_element_type=jnp.float32
        )
        out[...] = total.astype(jnp.bfloat16)


HBM = pl.BlockSpec(memory_space=pltpu.HBM)
VMEM = pl.BlockSpec(memory_space=pltpu.VMEM)
LIMIT = 56 * 2**20
PARAMS = pltpu.CompilerParams(vmem_limit_bytes=LIMIT)
SMALL = pl.CostEstimate(flops=1, bytes_accessed=1, transcendentals=0)


def block_shapes(width):
    narrow = jax.ShapeDtypeStruct((CAP, width), jnp.bfloat16)
    return (jax.ShapeDtypeStruct((CAP, width), jnp.float32), narrow, narrow, narrow)


def rows_shape(width):
    return jax.ShapeDtypeStruct((4 * CAP, width), jnp.bfloat16)


def scratch(units, width, weights, sems):
    return (
        [pltpu.VMEM((4 * CAP, width), jnp.bfloat16)]
        + [pltpu.VMEM((2 * units, width), jnp.bfloat16)] * weights
        + [pltpu.SemaphoreType.DMA((sems,))]
    )


def run_fwd(pieces, weights):
    units, width = weights[0].shape
    return pl.pallas_call(
        fwd_kernel,
        out_shape=block_shapes(width),
        in_specs=[HBM] * 11,
        out_specs=(VMEM,) * 4,
        scratch_shapes=scratch(units, width, 3, 11),
        compiler_params=PARAMS,
        cost_estimate=SMALL,
    )(*pieces, *weights)


def run_grad(pieces, weights):
    units, width = weights[0].shape
    return pl.pallas_call(
        grad_kernel,
        out_shape=(
            jax.ShapeDtypeStruct((2 * units, 4 * CAP), jnp.float32),
            rows_shape(width),
        ),
        in_specs=[HBM] * 7,
        out_specs=(VMEM, HBM),
        scratch_shapes=scratch(units, width, 1, 8),
        compiler_params=PARAMS,
        cost_estimate=SMALL,
    )(*pieces, *weights)


def run_back(pieces, hidden_grad, weights):
    units, width = weights[0].shape
    hidden = jax.ShapeDtypeStruct((3 * units, 4 * CAP), jnp.bfloat16)
    return pl.pallas_call(
        back_kernel,
        out_shape=block_shapes(width) + (hidden, hidden, rows_shape(width)),
        in_specs=[HBM] * 5 + [VMEM] + [HBM] * 4,
        out_specs=(VMEM,) * 6 + (HBM,),
        scratch_shapes=scratch(units, width, 2, 10),
        compiler_params=PARAMS,
        cost_estimate=SMALL,
    )(*pieces, hidden_grad, *weights)


def run_weights(hidden, hidden_x, grad_rows, grad_rows_x, back_rows, back_rows_x):
    units, width = hidden.shape[0] // 3, grad_rows.shape[1]
    step = min(width, 512)
    held = pl.BlockSpec(hidden.shape, lambda i: (0, 0))
    rows = pl.BlockSpec((grad_rows.shape[0], step), lambda i: (0, i))
    return pl.pallas_call(
        weight_kernel,
        grid=(width // step,),
        out_shape=(jax.ShapeDtypeStruct((units, width), jnp.bfloat16),) * 3,
        in_specs=[held] * 2 + [rows] * 4,
        out_specs=(pl.BlockSpec((units, step), lambda i: (0, i)),) * 3,
        compiler_params=PARAMS,
        cost_estimate=SMALL,
    )(hidden, hidden_x, grad_rows, grad_rows_x, back_rows, back_rows_x)


def add_parts(own, parts):
    total = own
    for part in parts:
        total = total + part.astype(jnp.float32)
    return total


def near_with_far(behind, ahead, from_behind, from_ahead):
    half = from_behind.shape[0]

    def plus(block, start, extra):
        padded = jnp.pad(extra, ((start, block.shape[0] - half - start), (0, 0)))
        return (block.astype(jnp.float32) + padded.astype(jnp.float32)).astype(jnp.bfloat16)

    return both_ways(plus(ahead, 0, from_behind), plus(behind, half, from_ahead))


def split_mp(total, place):
    width = total.shape[1] // 4

    def columns(array, index):
        return lax.dynamic_slice_in_dim(array, index * width, width, axis=1)

    low = total.astype(jnp.bfloat16)
    return (columns(total, place),) + tuple(columns(low, place ^ flip) for flip in (1, 2, 3))


def send_mp(blocks):
    return tuple(along_mp(block, flip) for flip, block in zip((1, 2, 3), blocks))


def per_device(
    tokens_in,
    route_ids,
    route_weights,
    stash,
    returned_batch_index,
    back_ids,
    back_weights,
    upstream,
    window_expert,
    w_gate,
    w_up,
    w_down,
):
    expert = window_expert[0]
    place = lax.axis_index("mp")
    half = CAP // 2
    gate_w, up_w, down_w = (w_gate[0], w_up[0], w_down[0])

    fwd_gate, fwd_slot = routing(route_ids[0], route_weights[0], expert)
    fwd_pick = picker_of(fwd_slot)
    back_gate, back_slot = routing(back_ids[0], back_weights[0], expert)
    back_pick = picker_of(back_slot)
    grad_tokens = (back_gate[:, None] * upstream[0].astype(jnp.float32)).astype(jnp.bfloat16)
    bufs = stacked(pack(fwd_pick, tokens_in[0]), pack(back_pick, grad_tokens))
    held_rows = lax.dynamic_index_in_dim(
        stash[0], returned_batch_index[0, 0], axis=0, keepdims=False
    )
    bufs, back_slot, gate_w, up_w, down_w, held_rows = together(
        bufs, back_slot, gate_w, up_w, down_w, held_rows
    )
    one, two, three, held_slot, gate_x, up_w, down_w, held_rows = together(
        *ask_mp(bufs), mirrored(back_slot), other_core(gate_w), up_w, down_w, held_rows
    )

    wide = widen(bufs, (one, two, three), place)
    fwd_wide, grad_wide = wide[:CAP], wide[CAP:]
    fwd_behind, fwd_ahead, back_buf, up_x, down_x, grad_wide = together(
        *both_ways(fwd_wide, fwd_wide),
        mirrored(pack(picker_of(held_slot), held_rows)),
        other_core(up_w),
        other_core(down_w),
        grad_wide,
    )

    cw, ccw, one, two, three = together(
        *both_ways(stacked(fwd_behind[:half], grad_wide), stacked(fwd_ahead[half:], grad_wide)),
        *ask_mp(back_buf),
    )

    fwd_terms = run_fwd(
        (fwd_wide, fwd_behind, fwd_ahead, cw, ccw), (gate_w, up_w, down_w, gate_x, up_x, down_x)
    )
    grad_pieces = (grad_wide, cw, ccw)
    back_wide = widen(back_buf, (one, two, three), place)
    cw, ccw, *fwd_terms = together(
        *both_ways(stacked(cw[half:CAP], back_wide), stacked(ccw[CAP:], back_wide)), *fwd_terms
    )
    fwd_own, fwd_to_behind, fwd_to_ahead, fwd_to_far = fwd_terms

    hidden_grad, grad_rows = run_grad((*grad_pieces, cw, ccw), (down_w, down_x))
    back_pieces = (back_wide, cw, ccw)
    cw, ccw, hidden_grad, grad_rows = together(
        *both_ways(
            stacked(cw[half:CAP], fwd_to_far[:half]), stacked(ccw[CAP:], fwd_to_far[half:])
        ),
        hidden_grad,
        grad_rows,
    )

    back_terms = run_back((*back_pieces, cw, ccw), hidden_grad, (gate_w, up_w, gate_x, up_x))
    p0, p1, grad_rows_x, *back_terms = together(
        *near_with_far(fwd_to_behind, fwd_to_ahead, cw[half:], ccw[half:]),
        other_core(grad_rows),
        *back_terms,
    )
    back_own, back_to_behind, back_to_ahead, back_to_far = back_terms[:4]
    hidden_keep, hidden_send, back_rows = back_terms[4:]

    fwd_total = add_parts(fwd_own, (p0, p1))
    f0, f1, hidden_x, back_rows_x, *fwd_blocks = together(
        *both_ways(back_to_far[:half], back_to_far[half:]),
        other_core(hidden_send),
        other_core(back_rows),
        *split_mp(fwd_total, place),
    )

    p0, p1, one, two, three, *grads = together(
        *near_with_far(back_to_behind, back_to_ahead, f0, f1),
        *send_mp(fwd_blocks[1:]),
        *run_weights(hidden_keep, hidden_x, grad_rows, grad_rows_x, back_rows, back_rows_x),
    )
    grad_down, grad_gate, grad_up = grads

    back_here, *back_sent = split_mp(add_parts(back_own, (p0, p1)), place)
    back_sent = send_mp(back_sent)
    fwd_sum = add_parts(fwd_blocks[0], (one, two, three))
    fwd_row_gate = jnp.sum(jnp.where(fwd_pick, fwd_gate[None, :], 0.0), axis=1)
    expert_out = unpack(fwd_pick, (fwd_sum * fwd_row_gate[:, None]).astype(jnp.bfloat16))
    input_grad = unpack(back_pick, add_parts(back_here, back_sent).astype(jnp.bfloat16))
    return (
        expert_out[None],
        input_grad[None],
        grad_gate[None],
        grad_up[None],
        grad_down[None],
    )


def solution(mesh):
    placed = (
        P("section", "expert", "mp"),
        P("section", "expert", None),
        P("section", "expert", None),
        P("section", None, "expert", "mp"),
        P("section", "expert"),
        P("section", "expert", None),
        P("section", "expert", None),
        P("section", "expert", "mp"),
        P("section"),
        P("section", ("expert", "mp"), None),
        P("section", ("expert", "mp"), None),
        P("section", ("expert", "mp"), None),
    )
    return jax.shard_map(
        per_device,
        mesh=mesh,
        in_specs=placed,
        out_specs=(
            P("section", "expert", "mp"),
            P("section", "expert", "mp"),
            P("section", ("expert", "mp"), None),
            P("section", ("expert", "mp"), None),
            P("section", ("expert", "mp"), None),
        ),
        check_vma=False,
    )
```

```python
import jax
import jax.numpy as jnp
from jax import lax
from jax.experimental import pallas as pl
from jax.experimental.pallas import tpu as pltpu
from jax.sharding import PartitionSpec as P

CAP = 64


def together(*arrays):
    return lax.optimization_barrier(arrays)


def along_y(array, step):
    n = lax.axis_size("expert")
    return lax.ppermute(array, "expert", [(i, (i + 2 * step) % n) for i in range(n)])


def other_core(array):
    n = lax.axis_size("expert")
    return lax.ppermute(array, "expert", [(i, i ^ 1) for i in range(n)])


def along_mp(array, flip):
    n = lax.axis_size("mp")
    return lax.ppermute(array, "mp", [(i, i ^ flip) for i in range(n)])


def mirrored(array):
    sections, places = (lax.axis_size("section"), lax.axis_size("mp"))
    last = sections * places - 1
    return lax.ppermute(array, ("section", "mp"), [(i, last - i) for i in range(last + 1)])


def routing(pair_ids, pair_weights, expert):
    matches = pair_ids == expert
    routed = jnp.any(matches, axis=1)
    counted = routed.astype(jnp.int32)
    slot_of = jnp.cumsum(counted) - counted
    gate_share = jnp.sum(jnp.where(matches, pair_weights, 0.0), axis=1)
    return (gate_share, jnp.where(routed, slot_of, CAP))


def picker_of(slot_or_cap):
    places = jnp.arange(CAP, dtype=jnp.int32)[:, None]
    return slot_or_cap[None, :] == places


def pack(picker, values):
    return jnp.dot(
        picker.astype(jnp.bfloat16), values, preferred_element_type=jnp.float32
    ).astype(jnp.bfloat16)


def unpack(picker, rows):
    return lax.dot_general(
        picker.astype(jnp.bfloat16),
        rows,
        (((0,), (0,)), ((), ())),
        preferred_element_type=jnp.float32,
    ).astype(jnp.bfloat16)


def swapped(flag, first, second):
    return (jnp.where(flag, second, first), jnp.where(flag, first, second))


def beside(flag, here, there):
    first, second = swapped(flag, here, there)
    return jnp.concatenate([first, second], axis=1)


def widen(block, others, place):
    one, two, three = others
    odd, high = (place & 1) == 1, (place & 2) == 2
    return beside(high, beside(odd, block, one), beside(odd, two, three))


def ask_mp(block):
    return tuple(along_mp(block, flip) for flip in (1, 2, 3))


def both_ways(to_ahead, to_behind):
    return (along_y(to_ahead, 1), along_y(to_behind, -1))


def stacked(*arrays):
    return jnp.concatenate(arrays, axis=0)


def fetch(sources, target, sems, first):
    copies = []
    into = 0
    for index, (ref, start, rows) in enumerate(sources):
        copies.append(
            pltpu.make_async_copy(
                ref.at[pl.ds(start, rows)],
                target.at[pl.ds(into, rows)],
                sems.at[first + index],
            )
        )
        into += rows
    for copy in copies:
        copy.start()
    return copies


def whole(*refs):
    return tuple((ref, 0, ref.shape[0]) for ref in refs)


def arrive(copies):
    for copy in copies:
        copy.wait()


def times_rows(weight, rows):
    return lax.dot_general(
        weight, rows, (((1,), (1,)), ((), ())), preferred_element_type=jnp.float32
    )


def spread_kernel_part(pairs, own_ref, far_refs):
    width = own_ref.shape[1]
    step = min(width, 1024)
    for left in range(0, width, step):
        columns = slice(left, left + step)
        term = 0.0
        for hidden, weight in pairs:
            term = term + lax.dot_general(
                hidden,
                weight[:, columns],
                (((0,), (0,)), ((), ())),
                preferred_element_type=jnp.float32,
            )
        own_ref[:, columns] = term[:CAP]
        for index, ref in enumerate(far_refs):
            ref[:, columns] = term[CAP * (index + 1) : CAP * (index + 2)].astype(jnp.bfloat16)


def fwd_kernel(*refs):
    wide, behind, ahead, low, high = refs[:5]
    gate_own, up_own, down_own, gate_x, up_x, down_x = refs[5:11]
    own_ref, behind_ref, ahead_ref, far_ref = refs[11:15]
    rows, gate, up, down, sems = refs[15:]
    half = CAP // 2
    rows_in = fetch(whole(wide, behind, ahead) + ((low, 0, half), (high, 0, half)), rows, sems, 0)
    gate_in = fetch(whole(gate_own, gate_x), gate, sems, 5)
    up_in = fetch(whole(up_own, up_x), up, sems, 7)
    down_in = fetch(whole(down_own, down_x), down, sems, 9)
    arrive(rows_in)
    arrive(gate_in)
    pre = times_rows(gate[...], rows[...])
    arrive(up_in)
    hidden = (pre * jax.nn.sigmoid(pre) * times_rows(up[...], rows[...])).astype(jnp.bfloat16)
    arrive(down_in)
    spread_kernel_part(((hidden, down),), own_ref, (behind_ref, ahead_ref, far_ref))


def later_rows(refs):
    wide, behind, ahead, low, high = refs
    half = CAP // 2
    return whole(wide) + (
        (behind, half, CAP),
        (ahead, half, CAP),
        (low, 0, half),
        (high, 0, half),
    )


def grad_kernel(*refs):
    down_own, down_x, hidden_ref, rows_out, rows, down, sems = refs[5:]
    rows_in = fetch(later_rows(refs[:5]), rows, sems, 0)
    down_in = fetch(whole(down_own, down_x), down, sems, 5)
    arrive(rows_in)
    keep = pltpu.make_async_copy(rows, rows_out, sems.at[7])
    keep.start()
    arrive(down_in)
    hidden_ref[...] = times_rows(down[...], rows[...])
    keep.wait()


def back_kernel(*refs):
    hidden_grad_ref, gate_own, up_own, gate_x, up_x = refs[5:10]
    own_ref, behind_ref, ahead_ref, far_ref, first_ref, keep_ref, send_ref, rows_out = refs[10:18]
    rows, gate, up, sems = refs[18:]
    units = gate_own.shape[0]
    rows_in = fetch(later_rows(refs[:5]), rows, sems, 0)
    gate_in = fetch(whole(gate_own, gate_x), gate, sems, 5)
    up_in = fetch(whole(up_own, up_x), up, sems, 7)
    arrive(rows_in)
    rows_back = pltpu.make_async_copy(rows, rows_out, sems.at[9])
    rows_back.start()
    arrive(gate_in)
    pre_gate = times_rows(gate[...], rows[...])
    arrive(up_in)
    pre_up = times_rows(up[...], rows[...])
    sigmoid_pre = jax.nn.sigmoid(pre_gate)
    activated = pre_gate * sigmoid_pre
    hidden_grad = hidden_grad_ref[...]
    hidden = (activated * pre_up).astype(jnp.bfloat16)
    gate_grad = (
        hidden_grad * pre_up * sigmoid_pre * (1.0 + pre_gate * (1.0 - sigmoid_pre))
    ).astype(jnp.bfloat16)
    up_grad = (hidden_grad * activated).astype(jnp.bfloat16)
    first_ref[...] = hidden[:units]
    keep_ref[:units] = gate_grad[:units]
    keep_ref[units:] = up_grad[:units]
    send_ref[:units] = hidden[units:]
    send_ref[units : 2 * units] = gate_grad[units:]
    send_ref[2 * units :] = up_grad[units:]
    spread_kernel_part(
        ((gate_grad, gate), (up_grad, up)), own_ref, (behind_ref, ahead_ref, far_ref)
    )
    rows_back.wait()


def weight_kernel(hidden_ref, hidden_x_ref, rows_ref, rows_x_ref, *outs):
    units = outs[0].shape[0]
    for index, out in enumerate(outs):
        part = slice(units * index, units * (index + 1))
        total = jnp.dot(hidden_ref[part], rows_ref[...], preferred_element_type=jnp.float32)
        total = total + jnp.dot(
            hidden_x_ref[part], rows_x_ref[...], preferred_element_type=jnp.float32
        )
        out[...] = total.astype(jnp.bfloat16)


HBM = pl.BlockSpec(memory_space=pltpu.HBM)
VMEM = pl.BlockSpec(memory_space=pltpu.VMEM)
PARAMS = pltpu.CompilerParams(vmem_limit_bytes=30 * 2**20)
SMALL = pl.CostEstimate(flops=1, bytes_accessed=1, transcendentals=0)


def block_shapes(width):
    narrow = jax.ShapeDtypeStruct((CAP, width), jnp.bfloat16)
    return (jax.ShapeDtypeStruct((CAP, width), jnp.float32), narrow, narrow, narrow)


def rows_shape(width):
    return jax.ShapeDtypeStruct((4 * CAP, width), jnp.bfloat16)


def scratch(units, width, weights, sems):
    return (
        [pltpu.VMEM((4 * CAP, width), jnp.bfloat16)]
        + [pltpu.VMEM((2 * units, width), jnp.bfloat16)] * weights
        + [pltpu.SemaphoreType.DMA((sems,))]
    )


def run_fwd(pieces, weights):
    units, width = weights[0].shape
    return pl.pallas_call(
        fwd_kernel,
        out_shape=block_shapes(width),
        in_specs=[HBM] * 11,
        out_specs=(VMEM,) * 4,
        scratch_shapes=scratch(units, width, 3, 11),
        compiler_params=PARAMS,
        cost_estimate=SMALL,
    )(*pieces, *weights)


def run_grad(pieces, weights):
    units, width = weights[0].shape
    return pl.pallas_call(
        grad_kernel,
        out_shape=(
            jax.ShapeDtypeStruct((2 * units, 4 * CAP), jnp.float32),
            rows_shape(width),
        ),
        in_specs=[HBM] * 7,
        out_specs=(VMEM, HBM),
        scratch_shapes=scratch(units, width, 1, 8),
        compiler_params=PARAMS,
        cost_estimate=SMALL,
    )(*pieces, *weights)


def run_back(pieces, hidden_grad, weights):
    units, width = weights[0].shape

    def hidden(count):
        return jax.ShapeDtypeStruct((count * units, 4 * CAP), jnp.bfloat16)

    return pl.pallas_call(
        back_kernel,
        out_shape=block_shapes(width) + (hidden(1), hidden(2), hidden(3), rows_shape(width)),
        in_specs=[HBM] * 5 + [VMEM] + [HBM] * 4,
        out_specs=(VMEM,) * 7 + (HBM,),
        scratch_shapes=scratch(units, width, 2, 10),
        compiler_params=pltpu.CompilerParams(vmem_limit_bytes=56 * 2**20),
        cost_estimate=SMALL,
    )(*pieces, hidden_grad, *weights)


def run_weights(units, hidden, hidden_x, rows, rows_x):
    width = rows.shape[1]
    step = min(width, 512)
    outs = hidden.shape[0] // units
    held = pl.BlockSpec(hidden.shape, lambda i: (0, 0))
    columns = pl.BlockSpec((rows.shape[0], step), lambda i: (0, i))
    return pl.pallas_call(
        weight_kernel,
        grid=(width // step,),
        out_shape=(jax.ShapeDtypeStruct((units, width), jnp.bfloat16),) * outs,
        in_specs=[held] * 2 + [columns] * 2,
        out_specs=(pl.BlockSpec((units, step), lambda i: (0, i)),) * outs,
        compiler_params=PARAMS,
        cost_estimate=SMALL,
    )(hidden, hidden_x, rows, rows_x)


def add_parts(own, parts):
    total = own
    for part in parts:
        total = total + part.astype(jnp.float32)
    return total


def near_with_far(behind, ahead, from_behind, from_ahead):
    half = from_behind.shape[0]

    def plus(block, start, extra):
        padded = jnp.pad(extra, ((start, block.shape[0] - half - start), (0, 0)))
        return (block.astype(jnp.float32) + padded.astype(jnp.float32)).astype(jnp.bfloat16)

    return both_ways(plus(ahead, 0, from_behind), plus(behind, half, from_ahead))


def split_mp(total, place):
    width = total.shape[1] // 4

    def columns(array, index):
        return lax.dynamic_slice_in_dim(array, index * width, width, axis=1)

    low = total.astype(jnp.bfloat16)
    return (columns(total, place),) + tuple(columns(low, place ^ flip) for flip in (1, 2, 3))


def send_mp(blocks):
    return tuple(along_mp(block, flip) for flip, block in zip((1, 2, 3), blocks))


def per_device(
    tokens_in,
    route_ids,
    route_weights,
    stash,
    returned_batch_index,
    back_ids,
    back_weights,
    upstream,
    window_expert,
    w_gate,
    w_up,
    w_down,
):
    expert = window_expert[0]
    place = lax.axis_index("mp")
    half = CAP // 2
    gate_w, up_w, down_w = (w_gate[0], w_up[0], w_down[0])

    fwd_gate, fwd_slot = routing(route_ids[0], route_weights[0], expert)
    fwd_pick = picker_of(fwd_slot)
    fwd_buf = pack(fwd_pick, tokens_in[0])
    held_rows = lax.dynamic_index_in_dim(
        stash[0], returned_batch_index[0, 0], axis=0, keepdims=False
    )
    fwd_buf, back_ids, back_weights = together(fwd_buf, back_ids, back_weights)
    back_gate, back_slot = routing(back_ids[0], back_weights[0], expert)
    back_pick = picker_of(back_slot)
    grad_tokens = (back_gate[:, None] * upstream[0].astype(jnp.float32)).astype(jnp.bfloat16)
    one, two, three, held_rows, gate_x, grad_buf = together(
        *ask_mp(fwd_buf), mirrored(held_rows), other_core(gate_w), pack(back_pick, grad_tokens)
    )

    fwd_wide = widen(fwd_buf, (one, two, three), place)
    fwd_behind, fwd_ahead, one, two, three, held_rows = together(
        *both_ways(fwd_wide, fwd_wide), *ask_mp(grad_buf), held_rows
    )

    grad_wide = widen(grad_buf, (one, two, three), place)
    back_buf = pack(back_pick, held_rows)
    cw, ccw, one, two, three, up_w, down_w = together(
        *both_ways(stacked(fwd_behind[:half], grad_wide), stacked(fwd_ahead[half:], grad_wide)),
        *ask_mp(back_buf),
        up_w,
        down_w,
    )

    up_x, down_x = (other_core(up_w), other_core(down_w))
    fwd_terms = run_fwd(
        (fwd_wide, fwd_behind, fwd_ahead, cw, ccw), (gate_w, up_w, down_w, gate_x, up_x, down_x)
    )
    grad_pieces = (grad_wide, cw, ccw)
    back_wide = widen(back_buf, (one, two, three), place ^ 3)
    cw, ccw, down_x, up_x, *fwd_terms = together(
        *both_ways(stacked(cw[half:CAP], back_wide), stacked(ccw[CAP:], back_wide)),
        down_x,
        up_x,
        *fwd_terms,
    )
    fwd_own, fwd_to_behind, fwd_to_ahead, fwd_to_far = fwd_terms

    hidden_grad, grad_rows = run_grad((*grad_pieces, cw, ccw), (down_w, down_x))
    back_pieces = (back_wide, cw, ccw)
    cw, ccw, hidden_grad, grad_rows = together(
        *both_ways(
            stacked(cw[half:CAP], fwd_to_far[:half]), stacked(ccw[CAP:], fwd_to_far[half:])
        ),
        hidden_grad,
        grad_rows,
    )

    back_terms = run_back((*back_pieces, cw, ccw), hidden_grad, (gate_w, up_w, gate_x, up_x))
    p0, p1, grad_rows_x, *back_terms = together(
        *near_with_far(fwd_to_behind, fwd_to_ahead, cw[half:], ccw[half:]),
        other_core(grad_rows),
        *back_terms,
    )
    back_own, back_to_behind, back_to_ahead, back_to_far = back_terms[:4]
    hidden, pair_grads, hidden_send, back_rows = back_terms[4:]

    fwd_total = add_parts(fwd_own, (p0, p1))
    f0, f1, hidden_x, back_rows_x, *fwd_blocks = together(
        *both_ways(back_to_far[:half], back_to_far[half:]),
        other_core(hidden_send),
        other_core(back_rows),
        *split_mp(fwd_total, place),
    )

    units = gate_w.shape[0]
    p0, p1, one, two, three, grad_down = together(
        *near_with_far(back_to_behind, back_to_ahead, f0, f1),
        *send_mp(fwd_blocks[1:]),
        *run_weights(units, hidden, hidden_x[:units], grad_rows, grad_rows_x),
    )

    back_here, *back_sent = split_mp(add_parts(back_own, (p0, p1)), place)
    grad_gate, grad_up, *back_sent = together(
        *run_weights(units, pair_grads, hidden_x[units:], back_rows, back_rows_x),
        *send_mp(back_sent),
    )
    fwd_sum = add_parts(fwd_blocks[0], (one, two, three))
    fwd_row_gate = jnp.sum(jnp.where(fwd_pick, fwd_gate[None, :], 0.0), axis=1)
    expert_out = unpack(fwd_pick, (fwd_sum * fwd_row_gate[:, None]).astype(jnp.bfloat16))
    input_grad = unpack(back_pick, add_parts(back_here, back_sent).astype(jnp.bfloat16))
    return (
        expert_out[None],
        input_grad[None],
        grad_gate[None],
        grad_up[None],
        grad_down[None],
    )


def solution(mesh):
    placed = (
        P("section", "expert", "mp"),
        P("section", "expert", None),
        P("section", "expert", None),
        P("section", None, "expert", "mp"),
        P("section", "expert"),
        P("section", "expert", None),
        P("section", "expert", None),
        P("section", "expert", "mp"),
        P("section"),
        P("section", ("expert", "mp"), None),
        P("section", ("expert", "mp"), None),
        P("section", ("expert", "mp"), None),
    )
    return jax.shard_map(
        per_device,
        mesh=mesh,
        in_specs=placed,
        out_specs=(
            P("section", "expert", "mp"),
            P("section", "expert", "mp"),
            P("section", ("expert", "mp"), None),
            P("section", ("expert", "mp"), None),
            P("section", ("expert", "mp"), None),
        ),
        check_vma=False,
    )
```

```python
import jax
import jax.numpy as jnp
from jax import lax
from jax.experimental import pallas as pl
from jax.experimental.pallas import tpu as pltpu
from jax.sharding import PartitionSpec as P

CAP = 64


def together(*arrays):
    return lax.optimization_barrier(arrays)


def along_y(array, step):
    n = lax.axis_size("expert")
    return lax.ppermute(array, "expert", [(i, (i + 2 * step) % n) for i in range(n)])


def other_core(array):
    n = lax.axis_size("expert")
    return lax.ppermute(array, "expert", [(i, i ^ 1) for i in range(n)])


def along_mp(array, flip):
    n = lax.axis_size("mp")
    return lax.ppermute(array, "mp", [(i, i ^ flip) for i in range(n)])


def mirrored(array):
    sections, places = (lax.axis_size("section"), lax.axis_size("mp"))
    last = sections * places - 1
    return lax.ppermute(array, ("section", "mp"), [(i, last - i) for i in range(last + 1)])


def routing(pair_ids, pair_weights, expert):
    matches = pair_ids == expert
    routed = jnp.any(matches, axis=1)
    counted = routed.astype(jnp.int32)
    slot_of = jnp.cumsum(counted) - counted
    gate_share = jnp.sum(jnp.where(matches, pair_weights, 0.0), axis=1)
    return (gate_share, jnp.where(routed, slot_of, CAP))


def picker_of(slot_or_cap):
    places = jnp.arange(CAP, dtype=jnp.int32)[:, None]
    return slot_or_cap[None, :] == places


def pack(picker, values):
    return jnp.dot(
        picker.astype(jnp.bfloat16), values, preferred_element_type=jnp.float32
    ).astype(jnp.bfloat16)


def unpack(picker, rows):
    return lax.dot_general(
        picker.astype(jnp.bfloat16),
        rows,
        (((0,), (0,)), ((), ())),
        preferred_element_type=jnp.float32,
    ).astype(jnp.bfloat16)


def swapped(flag, first, second):
    return (jnp.where(flag, second, first), jnp.where(flag, first, second))


def beside(flag, here, there):
    first, second = swapped(flag, here, there)
    return jnp.concatenate([first, second], axis=1)


def widen(block, others, place):
    one, two, three = others
    odd, high = (place & 1) == 1, (place & 2) == 2
    return beside(high, beside(odd, block, one), beside(odd, two, three))


def ask_mp(block):
    return tuple(along_mp(block, flip) for flip in (1, 2, 3))


def both_ways(to_ahead, to_behind):
    return (along_y(to_ahead, 1), along_y(to_behind, -1))


def stacked(*arrays):
    return jnp.concatenate(arrays, axis=0)


def fetch(sources, target, sems, first):
    copies = []
    into = 0
    for index, (ref, start, rows) in enumerate(sources):
        copies.append(
            pltpu.make_async_copy(
                ref.at[pl.ds(start, rows)],
                target.at[pl.ds(into, rows)],
                sems.at[first + index],
            )
        )
        into += rows
    for copy in copies:
        copy.start()
    return copies


def whole(*refs):
    return tuple((ref, 0, ref.shape[0]) for ref in refs)


def arrive(copies):
    for copy in copies:
        copy.wait()


def times_rows(weight, rows):
    return lax.dot_general(
        weight, rows, (((1,), (1,)), ((), ())), preferred_element_type=jnp.float32
    )


def spread_kernel_part(pairs, own_ref, far_refs):
    width = own_ref.shape[1]
    step = min(width, 1024)
    for left in range(0, width, step):
        columns = slice(left, left + step)
        term = 0.0
        for hidden, weight in pairs:
            term = term + lax.dot_general(
                hidden,
                weight[:, columns],
                (((0,), (0,)), ((), ())),
                preferred_element_type=jnp.float32,
            )
        own_ref[:, columns] = term[:CAP]
        start = CAP
        for ref in far_refs:
            rows = ref.shape[0]
            ref[:, columns] = term[start : start + rows].astype(jnp.bfloat16)
            start += rows


def fwd_kernel(*refs):
    wide, behind, ahead, low, high = refs[:5]
    gate_own, up_own, down_own, gate_x, up_x, down_x = refs[5:11]
    own_ref, *far_refs = refs[11:16]
    rows, gate, up, down, sems = refs[16:]
    half = CAP // 2
    rows_in = fetch(whole(wide, behind, ahead) + ((low, 0, half), (high, 0, half)), rows, sems, 0)
    gate_in = fetch(whole(gate_own, gate_x), gate, sems, 5)
    up_in = fetch(whole(up_own, up_x), up, sems, 7)
    down_in = fetch(whole(down_own, down_x), down, sems, 9)
    arrive(rows_in)
    arrive(gate_in)
    pre = times_rows(gate[...], rows[...])
    arrive(up_in)
    hidden = (pre * jax.nn.sigmoid(pre) * times_rows(up[...], rows[...])).astype(jnp.bfloat16)
    arrive(down_in)
    spread_kernel_part(((hidden, down),), own_ref, far_refs)


def later_rows(refs):
    sent, behind, ahead, low, high = refs
    half = CAP // 2
    return (
        (sent, half, CAP),
        (behind, half, CAP),
        (ahead, half, CAP),
        (low, 0, half),
        (high, 0, half),
    )


def grad_kernel(*refs):
    down_own, down_x, hidden_ref, rows_out, rows, down, sems = refs[5:]
    rows_in = fetch(later_rows(refs[:5]), rows, sems, 0)
    down_in = fetch(whole(down_own, down_x), down, sems, 5)
    arrive(rows_in)
    keep = pltpu.make_async_copy(rows, rows_out, sems.at[7])
    keep.start()
    arrive(down_in)
    hidden_ref[...] = times_rows(down[...], rows[...])
    keep.wait()


def chunk_copies(sources, target, columns, sems):
    copies = []
    into = 0
    for index, (ref, start, rows) in enumerate(sources):
        copies.append(
            pltpu.make_async_copy(
                ref.at[pl.ds(start, rows), columns],
                target.at[pl.ds(into, rows), columns],
                sems.at[index],
            )
        )
        into += rows
    return copies


def back_kernel(*refs):
    pieces = later_rows(refs[:5])
    hidden_grad_ref, gate_own, up_own, gate_x, up_x = refs[5:10]
    block_outs, first_out, keep_out, send_out, rows_out = refs[10:15], *refs[15:19]
    rows, gate, up, block_own, block_far, hidden_all, in_sems, out_sems, rows_sem = refs[19:]
    units = gate_own.shape[0]
    width = rows.shape[1]
    step = width // CHUNKS
    loads = []
    for chunk in range(CHUNKS):
        columns = pl.ds(chunk * step, step)
        loads.append(
            chunk_copies(pieces, rows, columns, in_sems.at[chunk, 0])
            + chunk_copies(whole(gate_own, gate_x), gate, columns, in_sems.at[chunk, 1])
            + chunk_copies(whole(up_own, up_x), up, columns, in_sems.at[chunk, 2])
        )
    for copies in loads:
        for copy in copies:
            copy.start()
    pre_gate, pre_up = 0.0, 0.0
    for chunk, copies in enumerate(loads):
        columns = slice(chunk * step, (chunk + 1) * step)
        arrive(copies)
        pre_gate = pre_gate + times_rows(gate[:, columns], rows[:, columns])
        pre_up = pre_up + times_rows(up[:, columns], rows[:, columns])
    rows_back = pltpu.make_async_copy(rows, rows_out, rows_sem.at[0])
    rows_back.start()
    sigmoid_pre = jax.nn.sigmoid(pre_gate)
    activated = pre_gate * sigmoid_pre
    hidden_grad = hidden_grad_ref[...]
    hidden = (activated * pre_up).astype(jnp.bfloat16)
    gate_grad = (
        hidden_grad * pre_up * sigmoid_pre * (1.0 + pre_gate * (1.0 - sigmoid_pre))
    ).astype(jnp.bfloat16)
    up_grad = (hidden_grad * activated).astype(jnp.bfloat16)
    ordered = (
        hidden[:units],
        gate_grad[:units],
        up_grad[:units],
        hidden[units:],
        gate_grad[units:],
        up_grad[units:],
    )
    for index, array in enumerate(ordered):
        hidden_all[units * index : units * (index + 1)] = array
    stores = []
    for index, (out, start) in enumerate(((first_out, 0), (keep_out, 1), (send_out, 3))):
        part = pl.ds(units * start, out.shape[0])
        stores.append(pltpu.make_async_copy(hidden_all.at[part], out, rows_sem.at[index + 1]))
        stores[-1].start()
    for chunk in range(CHUNKS):
        columns = slice(chunk * step, (chunk + 1) * step)
        term = 0.0
        for array, weight in ((gate_grad, gate), (up_grad, up)):
            term = term + lax.dot_general(
                array,
                weight[:, columns],
                (((0,), (0,)), ((), ())),
                preferred_element_type=jnp.float32,
            )
        block_own[:, columns] = term[:CAP]
        block_far[:, columns] = term[CAP:].astype(jnp.bfloat16)
        columns = pl.ds(chunk * step, step)
        start = 0
        for index, out in enumerate(block_outs):
            source = block_own if index == 0 else block_far.at[pl.ds(start, out.shape[0])]
            start += out.shape[0] if index else 0
            stores.append(
                pltpu.make_async_copy(
                    source.at[:, columns], out.at[:, columns], out_sems.at[chunk, index]
                )
            )
            stores[-1].start()
    rows_back.wait()
    arrive(stores)


def weight_kernel(hidden_ref, hidden_x_ref, rows_ref, rows_x_ref, *outs):
    units = outs[0].shape[0]
    for index, out in enumerate(outs):
        part = slice(units * index, units * (index + 1))
        total = jnp.dot(hidden_ref[part], rows_ref[...], preferred_element_type=jnp.float32)
        total = total + jnp.dot(
            hidden_x_ref[part], rows_x_ref[...], preferred_element_type=jnp.float32
        )
        out[...] = total.astype(jnp.bfloat16)


HBM = pl.BlockSpec(memory_space=pltpu.HBM)
VMEM = pl.BlockSpec(memory_space=pltpu.VMEM)
CHUNKS = 4
PARAMS = pltpu.CompilerParams(vmem_limit_bytes=30 * 2**20)
SMALL = pl.CostEstimate(flops=1, bytes_accessed=1, transcendentals=0)


def block_shapes(width):
    sent = (CAP, CAP, CAP // 2, CAP // 2)
    return (jax.ShapeDtypeStruct((CAP, width), jnp.float32),) + tuple(
        jax.ShapeDtypeStruct((rows, width), jnp.bfloat16) for rows in sent
    )


def rows_shape(width):
    return jax.ShapeDtypeStruct((4 * CAP, width), jnp.bfloat16)


def scratch(units, width, weights, sems):
    return (
        [pltpu.VMEM((4 * CAP, width), jnp.bfloat16)]
        + [pltpu.VMEM((2 * units, width), jnp.bfloat16)] * weights
        + [pltpu.SemaphoreType.DMA((sems,))]
    )


def run_fwd(pieces, weights):
    units, width = weights[0].shape
    return pl.pallas_call(
        fwd_kernel,
        out_shape=block_shapes(width),
        in_specs=[HBM] * 11,
        out_specs=(VMEM,) * 5,
        scratch_shapes=scratch(units, width, 3, 11),
        compiler_params=PARAMS,
        cost_estimate=SMALL,
    )(*pieces, *weights)


def run_grad(pieces, weights):
    units, width = weights[0].shape
    return pl.pallas_call(
        grad_kernel,
        out_shape=(
            jax.ShapeDtypeStruct((2 * units, 4 * CAP), jnp.float32),
            rows_shape(width),
        ),
        in_specs=[HBM] * 7,
        out_specs=(VMEM, HBM),
        scratch_shapes=scratch(units, width, 1, 8),
        compiler_params=PARAMS,
        cost_estimate=SMALL,
    )(*pieces, *weights)


def run_back(pieces, hidden_grad, weights):
    units, width = weights[0].shape

    def hidden(count):
        return jax.ShapeDtypeStruct((count * units, 4 * CAP), jnp.bfloat16)

    return pl.pallas_call(
        back_kernel,
        out_shape=block_shapes(width) + (hidden(1), hidden(2), hidden(3), rows_shape(width)),
        in_specs=[HBM] * 5 + [VMEM] + [HBM] * 4,
        out_specs=(HBM,) * 9,
        scratch_shapes=[
            pltpu.VMEM((4 * CAP, width), jnp.bfloat16),
            pltpu.VMEM((2 * units, width), jnp.bfloat16),
            pltpu.VMEM((2 * units, width), jnp.bfloat16),
            pltpu.VMEM((CAP, width), jnp.float32),
            pltpu.VMEM((3 * CAP, width), jnp.bfloat16),
            pltpu.VMEM((6 * units, 4 * CAP), jnp.bfloat16),
            pltpu.SemaphoreType.DMA((CHUNKS, 3, 5)),
            pltpu.SemaphoreType.DMA((CHUNKS, 5)),
            pltpu.SemaphoreType.DMA((4,)),
        ],
        compiler_params=pltpu.CompilerParams(vmem_limit_bytes=56 * 2**20),
        cost_estimate=SMALL,
    )(*pieces, hidden_grad, *weights)


def run_weights(units, hidden, hidden_x, rows, rows_x):
    width = rows.shape[1]
    step = min(width, 1024)
    outs = hidden.shape[0] // units
    held = pl.BlockSpec(hidden.shape, lambda i: (0, 0))
    columns = pl.BlockSpec((rows.shape[0], step), lambda i: (0, i))
    return pl.pallas_call(
        weight_kernel,
        grid=(width // step,),
        out_shape=(jax.ShapeDtypeStruct((units, width), jnp.bfloat16),) * outs,
        in_specs=[held] * 2 + [columns] * 2,
        out_specs=(pl.BlockSpec((units, step), lambda i: (0, i)),) * outs,
        compiler_params=PARAMS,
        cost_estimate=SMALL,
    )(hidden, hidden_x, rows, rows_x)


def add_parts(own, parts):
    total = own
    for part in parts:
        total = total + part.astype(jnp.float32)
    return total


def near_with_far(behind, ahead, from_behind, from_ahead):
    half = from_behind.shape[0]

    def plus(block, start, extra):
        padded = jnp.pad(extra, ((start, block.shape[0] - half - start), (0, 0)))
        return (block.astype(jnp.float32) + padded.astype(jnp.float32)).astype(jnp.bfloat16)

    return both_ways(plus(ahead, 0, from_behind), plus(behind, half, from_ahead))


def split_mp(total, place):
    width = total.shape[1] // 4

    def columns(array, index):
        return lax.dynamic_slice_in_dim(array, index * width, width, axis=1)

    low = total.astype(jnp.bfloat16)
    return (columns(total, place),) + tuple(columns(low, place ^ flip) for flip in (1, 2, 3))


def send_mp(blocks):
    return tuple(along_mp(block, flip) for flip, block in zip((1, 2, 3), blocks))


def per_device(
    tokens_in,
    route_ids,
    route_weights,
    stash,
    returned_batch_index,
    back_ids,
    back_weights,
    upstream,
    window_expert,
    w_gate,
    w_up,
    w_down,
):
    expert = window_expert[0]
    place = lax.axis_index("mp")
    half = CAP // 2
    gate_w, up_w, down_w = (w_gate[0], w_up[0], w_down[0])

    fwd_gate, fwd_slot = routing(route_ids[0], route_weights[0], expert)
    fwd_pick = picker_of(fwd_slot)
    fwd_buf = pack(fwd_pick, tokens_in[0])
    held_rows = lax.dynamic_index_in_dim(
        stash[0], returned_batch_index[0, 0], axis=0, keepdims=False
    )
    fwd_buf, back_ids, back_weights = together(fwd_buf, back_ids, back_weights)
    back_gate, back_slot = routing(back_ids[0], back_weights[0], expert)
    back_pick = picker_of(back_slot)
    grad_tokens = (back_gate[:, None] * upstream[0].astype(jnp.float32)).astype(jnp.bfloat16)
    held_rows = mirrored(held_rows)
    one, two, three, gate_x, grad_buf = together(
        *ask_mp(fwd_buf), other_core(gate_w), pack(back_pick, grad_tokens)
    )

    fwd_wide = widen(fwd_buf, (one, two, three), place)
    fwd_behind, fwd_ahead, one, two, three, held_rows = together(
        *both_ways(fwd_wide, fwd_wide), *ask_mp(grad_buf), held_rows
    )

    grad_wide = widen(grad_buf, (one, two, three), place)
    back_buf = pack(back_pick, held_rows)
    grad_sent = stacked(fwd_behind[:half], grad_wide)
    cw, ccw, one, two, three, up_w, down_w = together(
        *both_ways(grad_sent, stacked(fwd_ahead[half:], grad_wide)),
        *ask_mp(back_buf),
        up_w,
        down_w,
    )

    up_x, down_x = (other_core(up_w), other_core(down_w))
    fwd_terms = run_fwd(
        (fwd_wide, fwd_behind, fwd_ahead, cw, ccw), (gate_w, up_w, down_w, gate_x, up_x, down_x)
    )
    grad_pieces = (grad_sent, cw, ccw)
    back_wide = widen(back_buf, (one, two, three), place ^ 3)
    back_sent = stacked(cw[half:CAP], back_wide)
    cw, ccw, down_x, up_x, *fwd_terms = together(
        *both_ways(back_sent, stacked(ccw[CAP:], back_wide)),
        down_x,
        up_x,
        *fwd_terms,
    )
    fwd_own, fwd_to_behind, fwd_to_ahead, fwd_low, fwd_high = fwd_terms

    hidden_grad, grad_rows = run_grad((*grad_pieces, cw, ccw), (down_w, down_x))
    back_pieces = (back_sent, cw, ccw)
    cw, ccw, hidden_grad, grad_rows = together(
        *both_ways(stacked(cw[half:CAP], fwd_low), stacked(ccw[CAP:], fwd_high)),
        hidden_grad,
        grad_rows,
    )

    back_terms = run_back((*back_pieces, cw, ccw), hidden_grad, (gate_w, up_w, gate_x, up_x))
    p0, p1, grad_rows_x, *back_terms = together(
        *near_with_far(fwd_to_behind, fwd_to_ahead, cw[half:], ccw[half:]),
        other_core(grad_rows),
        *back_terms,
    )
    back_own, back_to_behind, back_to_ahead, back_low, back_high = back_terms[:5]
    hidden, pair_grads, hidden_send, back_rows = back_terms[5:]

    fwd_total = add_parts(fwd_own, (p0, p1))
    f0, f1, hidden_x, back_rows_x, *fwd_blocks = together(
        *both_ways(back_low, back_high),
        other_core(hidden_send),
        other_core(back_rows),
        *split_mp(fwd_total, place),
    )

    units = gate_w.shape[0]
    p0, p1, one, two, three, grad_down, pair_grads = together(
        *near_with_far(back_to_behind, back_to_ahead, f0, f1),
        *send_mp(fwd_blocks[1:]),
        *run_weights(units, hidden, hidden_x[:units], grad_rows, grad_rows_x),
        pair_grads,
    )

    back_here, *back_sent = split_mp(add_parts(back_own, (p0, p1)), place)
    grad_gate, grad_up, *back_sent = together(
        *run_weights(units, pair_grads, hidden_x[units:], back_rows, back_rows_x),
        *send_mp(back_sent),
    )
    fwd_sum = add_parts(fwd_blocks[0], (one, two, three))
    fwd_row_gate = jnp.sum(jnp.where(fwd_pick, fwd_gate[None, :], 0.0), axis=1)
    expert_out = unpack(fwd_pick, (fwd_sum * fwd_row_gate[:, None]).astype(jnp.bfloat16))
    input_grad = unpack(back_pick, add_parts(back_here, back_sent).astype(jnp.bfloat16))
    return (
        expert_out[None],
        input_grad[None],
        grad_gate[None],
        grad_up[None],
        grad_down[None],
    )


def solution(mesh):
    placed = (
        P("section", "expert", "mp"),
        P("section", "expert", None),
        P("section", "expert", None),
        P("section", None, "expert", "mp"),
        P("section", "expert"),
        P("section", "expert", None),
        P("section", "expert", None),
        P("section", "expert", "mp"),
        P("section"),
        P("section", ("expert", "mp"), None),
        P("section", ("expert", "mp"), None),
        P("section", ("expert", "mp"), None),
    )
    return jax.shard_map(
        per_device,
        mesh=mesh,
        in_specs=placed,
        out_specs=(
            P("section", "expert", "mp"),
            P("section", "expert", "mp"),
            P("section", ("expert", "mp"), None),
            P("section", ("expert", "mp"), None),
            P("section", ("expert", "mp"), None),
        ),
        check_vma=False,
    )
```

```python
import jax
import jax.numpy as jnp
from jax import lax
from jax.experimental import pallas as pl
from jax.experimental.pallas import tpu as pltpu
from jax.sharding import PartitionSpec as P

CAP = 64


def together(*arrays):
    return lax.optimization_barrier(arrays)


def along_y(array, step):
    n = lax.axis_size("expert")
    return lax.ppermute(array, "expert", [(i, (i + 2 * step) % n) for i in range(n)])


def other_core(array):
    n = lax.axis_size("expert")
    return lax.ppermute(array, "expert", [(i, i ^ 1) for i in range(n)])


def along_mp(array, flip):
    n = lax.axis_size("mp")
    return lax.ppermute(array, "mp", [(i, i ^ flip) for i in range(n)])


def mirrored(array):
    sections, places = (lax.axis_size("section"), lax.axis_size("mp"))
    last = sections * places - 1
    return lax.ppermute(array, ("section", "mp"), [(i, last - i) for i in range(last + 1)])


def routing(pair_ids, pair_weights, expert):
    matches = pair_ids == expert
    routed = jnp.any(matches, axis=1)
    counted = routed.astype(jnp.int32)
    slot_of = jnp.cumsum(counted) - counted
    gate_share = jnp.sum(jnp.where(matches, pair_weights, 0.0), axis=1)
    return (gate_share, jnp.where(routed, slot_of, CAP))


def picker_of(slot_or_cap):
    places = jnp.arange(CAP, dtype=jnp.int32)[:, None]
    return slot_or_cap[None, :] == places


def pack(picker, values):
    return jnp.dot(
        picker.astype(jnp.bfloat16), values, preferred_element_type=jnp.float32
    ).astype(jnp.bfloat16)


def unpack(picker, rows):
    return lax.dot_general(
        picker.astype(jnp.bfloat16),
        rows,
        (((0,), (0,)), ((), ())),
        preferred_element_type=jnp.float32,
    ).astype(jnp.bfloat16)


def swapped(flag, first, second):
    return (jnp.where(flag, second, first), jnp.where(flag, first, second))


def beside(flag, here, there):
    first, second = swapped(flag, here, there)
    return jnp.concatenate([first, second], axis=1)


def widen(block, others, place):
    one, two, three = others
    odd, high = (place & 1) == 1, (place & 2) == 2
    return beside(high, beside(odd, block, one), beside(odd, two, three))


def ask_mp(block):
    return tuple(along_mp(block, flip) for flip in (1, 2, 3))


def both_ways(to_ahead, to_behind):
    return (along_y(to_ahead, 1), along_y(to_behind, -1))


def stacked(*arrays):
    return jnp.concatenate(arrays, axis=0)


def fetch(sources, target, sems, first):
    copies = []
    into = 0
    for index, (ref, start, rows) in enumerate(sources):
        copies.append(
            pltpu.make_async_copy(
                ref.at[pl.ds(start, rows)],
                target.at[pl.ds(into, rows)],
                sems.at[first + index],
            )
        )
        into += rows
    for copy in copies:
        copy.start()
    return copies


def whole(*refs):
    return tuple((ref, 0, ref.shape[0]) for ref in refs)


def arrive(copies):
    for copy in copies:
        copy.wait()


def times_rows(weight, rows):
    return lax.dot_general(
        weight, rows, (((1,), (1,)), ((), ())), preferred_element_type=jnp.float32
    )


def spread_kernel_part(pairs, own_ref, far_refs):
    width = own_ref.shape[1]
    step = min(width, 1024)
    for left in range(0, width, step):
        columns = slice(left, left + step)
        term = 0.0
        for hidden, weight in pairs:
            term = term + lax.dot_general(
                hidden,
                weight[:, columns],
                (((0,), (0,)), ((), ())),
                preferred_element_type=jnp.float32,
            )
        own_ref[:, columns] = term[:CAP]
        start = CAP
        for ref in far_refs:
            rows = ref.shape[0]
            ref[:, columns] = term[start : start + rows].astype(jnp.bfloat16)
            start += rows


def fwd_kernel(*refs):
    wide, behind, ahead, low, high = refs[:5]
    gate_own, up_own, down_own, gate_x, up_x, down_x = refs[5:11]
    own_ref, *far_refs = refs[11:16]
    rows, gate, up, down, sems = refs[16:]
    half = CAP // 2
    rows_in = fetch(whole(wide, behind, ahead) + ((low, 0, half), (high, 0, half)), rows, sems, 0)
    gate_in = fetch(whole(gate_own, gate_x), gate, sems, 5)
    up_in = fetch(whole(up_own, up_x), up, sems, 7)
    down_in = fetch(whole(down_own, down_x), down, sems, 9)
    arrive(rows_in)
    arrive(gate_in)
    pre = times_rows(gate[...], rows[...])
    arrive(up_in)
    hidden = (pre * jax.nn.sigmoid(pre) * times_rows(up[...], rows[...])).astype(jnp.bfloat16)
    arrive(down_in)
    spread_kernel_part(((hidden, down),), own_ref, far_refs)


def later_rows(refs):
    sent, behind, ahead, low, high = refs
    half = CAP // 2
    return (
        (sent, half, CAP),
        (behind, half, CAP),
        (ahead, half, CAP),
        (low, 0, half),
        (high, 0, half),
    )


def grad_kernel(*refs):
    down_own, down_x, hidden_ref, rows_out, rows, down, sems = refs[5:]
    rows_in = fetch(later_rows(refs[:5]), rows, sems, 0)
    down_in = fetch(whole(down_own, down_x), down, sems, 5)
    arrive(rows_in)
    keep = pltpu.make_async_copy(rows, rows_out, sems.at[7])
    keep.start()
    arrive(down_in)
    hidden_ref[...] = times_rows(down[...], rows[...])
    keep.wait()


def chunk_copies(sources, target, columns, sems):
    copies = []
    into = 0
    for index, (ref, start, rows) in enumerate(sources):
        copies.append(
            pltpu.make_async_copy(
                ref.at[pl.ds(start, rows), columns],
                target.at[pl.ds(into, rows), columns],
                sems.at[index],
            )
        )
        into += rows
    return copies


def back_kernel(*refs):
    pieces = later_rows(refs[:5])
    hidden_grad_ref, gate_own, up_own, gate_x, up_x = refs[5:10]
    block_outs, first_out, keep_out, send_out, rows_out = refs[10:15], *refs[15:19]
    rows, gate, up, block_own, block_far, hidden_all, in_sems, out_sems, rows_sem = refs[19:]
    units = gate_own.shape[0]
    width = rows.shape[1]
    step = width // CHUNKS
    loads = []
    for chunk in range(CHUNKS):
        columns = pl.ds(chunk * step, step)
        loads.append(
            chunk_copies(pieces, rows, columns, in_sems.at[chunk, 0])
            + chunk_copies(whole(gate_own, gate_x), gate, columns, in_sems.at[chunk, 1])
            + chunk_copies(whole(up_own, up_x), up, columns, in_sems.at[chunk, 2])
        )
    for copies in loads:
        for copy in copies:
            copy.start()
    pre_gate, pre_up = 0.0, 0.0
    for chunk, copies in enumerate(loads):
        columns = slice(chunk * step, (chunk + 1) * step)
        arrive(copies)
        pre_gate = pre_gate + times_rows(gate[:, columns], rows[:, columns])
        pre_up = pre_up + times_rows(up[:, columns], rows[:, columns])
    rows_back = pltpu.make_async_copy(rows, rows_out, rows_sem.at[0])
    rows_back.start()
    sigmoid_pre = jax.nn.sigmoid(pre_gate)
    activated = pre_gate * sigmoid_pre
    hidden_grad = hidden_grad_ref[...]
    hidden = (activated * pre_up).astype(jnp.bfloat16)
    gate_grad = (
        hidden_grad * pre_up * sigmoid_pre * (1.0 + pre_gate * (1.0 - sigmoid_pre))
    ).astype(jnp.bfloat16)
    up_grad = (hidden_grad * activated).astype(jnp.bfloat16)
    ordered = (
        hidden[:units],
        gate_grad[:units],
        up_grad[:units],
        hidden[units:],
        gate_grad[units:],
        up_grad[units:],
    )
    for index, array in enumerate(ordered):
        hidden_all[units * index : units * (index + 1)] = array
    stores = []
    for index, (out, start) in enumerate(((first_out, 0), (keep_out, 1), (send_out, 3))):
        part = pl.ds(units * start, out.shape[0])
        stores.append(pltpu.make_async_copy(hidden_all.at[part], out, rows_sem.at[index + 1]))
        stores[-1].start()
    for chunk in range(CHUNKS):
        columns = slice(chunk * step, (chunk + 1) * step)
        term = 0.0
        for array, weight in ((gate_grad, gate), (up_grad, up)):
            term = term + lax.dot_general(
                array,
                weight[:, columns],
                (((0,), (0,)), ((), ())),
                preferred_element_type=jnp.float32,
            )
        block_own[:, columns] = term[:CAP]
        block_far[:, columns] = term[CAP:].astype(jnp.bfloat16)
        columns = pl.ds(chunk * step, step)
        start = 0
        for index, out in enumerate(block_outs):
            source = block_own if index == 0 else block_far.at[pl.ds(start, out.shape[0])]
            start += out.shape[0] if index else 0
            stores.append(
                pltpu.make_async_copy(
                    source.at[:, columns], out.at[:, columns], out_sems.at[chunk, index]
                )
            )
            stores[-1].start()
    rows_back.wait()
    arrive(stores)


def weight_kernel(hidden_ref, hidden_x_ref, rows_ref, rows_x_ref, *outs):
    units = outs[0].shape[0]
    for index, out in enumerate(outs):
        part = slice(units * index, units * (index + 1))
        total = jnp.dot(hidden_ref[part], rows_ref[...], preferred_element_type=jnp.float32)
        total = total + jnp.dot(
            hidden_x_ref[part], rows_x_ref[...], preferred_element_type=jnp.float32
        )
        out[...] = total.astype(jnp.bfloat16)


HBM = pl.BlockSpec(memory_space=pltpu.HBM)
VMEM = pl.BlockSpec(memory_space=pltpu.VMEM)
CHUNKS = 4
PARAMS = pltpu.CompilerParams(vmem_limit_bytes=30 * 2**20)
SMALL = pl.CostEstimate(flops=1, bytes_accessed=1, transcendentals=0)


def block_shapes(width):
    sent = (CAP, CAP, CAP // 2, CAP // 2)
    return (jax.ShapeDtypeStruct((CAP, width), jnp.float32),) + tuple(
        jax.ShapeDtypeStruct((rows, width), jnp.bfloat16) for rows in sent
    )


def rows_shape(width):
    return jax.ShapeDtypeStruct((4 * CAP, width), jnp.bfloat16)


def scratch(units, width, weights, sems):
    return (
        [pltpu.VMEM((4 * CAP, width), jnp.bfloat16)]
        + [pltpu.VMEM((2 * units, width), jnp.bfloat16)] * weights
        + [pltpu.SemaphoreType.DMA((sems,))]
    )


def run_fwd(pieces, weights):
    units, width = weights[0].shape
    return pl.pallas_call(
        fwd_kernel,
        out_shape=block_shapes(width),
        in_specs=[HBM] * 11,
        out_specs=(VMEM,) * 5,
        scratch_shapes=scratch(units, width, 3, 11),
        compiler_params=PARAMS,
        cost_estimate=SMALL,
    )(*pieces, *weights)


def run_grad(pieces, weights):
    units, width = weights[0].shape
    return pl.pallas_call(
        grad_kernel,
        out_shape=(
            jax.ShapeDtypeStruct((2 * units, 4 * CAP), jnp.float32),
            rows_shape(width),
        ),
        in_specs=[HBM] * 7,
        out_specs=(VMEM, HBM),
        scratch_shapes=scratch(units, width, 1, 8),
        compiler_params=PARAMS,
        cost_estimate=SMALL,
    )(*pieces, *weights)


def run_back(pieces, hidden_grad, weights):
    units, width = weights[0].shape

    def hidden(count):
        return jax.ShapeDtypeStruct((count * units, 4 * CAP), jnp.bfloat16)

    return pl.pallas_call(
        back_kernel,
        out_shape=block_shapes(width) + (hidden(1), hidden(2), hidden(3), rows_shape(width)),
        in_specs=[HBM] * 5 + [VMEM] + [HBM] * 4,
        out_specs=(HBM,) * 9,
        scratch_shapes=[
            pltpu.VMEM((4 * CAP, width), jnp.bfloat16),
            pltpu.VMEM((2 * units, width), jnp.bfloat16),
            pltpu.VMEM((2 * units, width), jnp.bfloat16),
            pltpu.VMEM((CAP, width), jnp.float32),
            pltpu.VMEM((3 * CAP, width), jnp.bfloat16),
            pltpu.VMEM((6 * units, 4 * CAP), jnp.bfloat16),
            pltpu.SemaphoreType.DMA((CHUNKS, 3, 5)),
            pltpu.SemaphoreType.DMA((CHUNKS, 5)),
            pltpu.SemaphoreType.DMA((4,)),
        ],
        compiler_params=pltpu.CompilerParams(vmem_limit_bytes=56 * 2**20),
        cost_estimate=SMALL,
    )(*pieces, hidden_grad, *weights)


def run_weights(units, hidden, hidden_x, rows, rows_x):
    width = rows.shape[1]
    step = min(width, 1024)
    outs = hidden.shape[0] // units
    held = pl.BlockSpec(hidden.shape, lambda i: (0, 0))
    columns = pl.BlockSpec((rows.shape[0], step), lambda i: (0, i))
    return pl.pallas_call(
        weight_kernel,
        grid=(width // step,),
        out_shape=(jax.ShapeDtypeStruct((units, width), jnp.bfloat16),) * outs,
        in_specs=[held] * 2 + [columns] * 2,
        out_specs=(pl.BlockSpec((units, step), lambda i: (0, i)),) * outs,
        compiler_params=PARAMS,
        cost_estimate=SMALL,
    )(hidden, hidden_x, rows, rows_x)


def add_parts(own, parts):
    total = own
    for part in parts:
        total = total + part.astype(jnp.float32)
    return total


def near_with_far(behind, ahead, from_behind, from_ahead):
    half = from_behind.shape[0]

    def plus(block, start, extra):
        padded = jnp.pad(extra, ((start, block.shape[0] - half - start), (0, 0)))
        return (block.astype(jnp.float32) + padded.astype(jnp.float32)).astype(jnp.bfloat16)

    return both_ways(plus(ahead, 0, from_behind), plus(behind, half, from_ahead))


def split_mp(total, place):
    width = total.shape[1] // 4

    def columns(array, index):
        return lax.dynamic_slice_in_dim(array, index * width, width, axis=1)

    low = total.astype(jnp.bfloat16)
    return (columns(total, place),) + tuple(columns(low, place ^ flip) for flip in (1, 2, 3))


def send_mp(blocks):
    return tuple(along_mp(block, flip) for flip, block in zip((1, 2, 3), blocks))


def per_device(
    tokens_in,
    route_ids,
    route_weights,
    stash,
    returned_batch_index,
    back_ids,
    back_weights,
    upstream,
    window_expert,
    w_gate,
    w_up,
    w_down,
):
    expert = window_expert[0]
    place = lax.axis_index("mp")
    half = CAP // 2
    gate_w, up_w, down_w = (w_gate[0], w_up[0], w_down[0])

    fwd_gate, fwd_slot = routing(route_ids[0], route_weights[0], expert)
    fwd_pick = picker_of(fwd_slot)
    fwd_buf = pack(fwd_pick, tokens_in[0])
    held_rows = lax.dynamic_index_in_dim(
        stash[0], returned_batch_index[0, 0], axis=0, keepdims=False
    )
    fwd_buf, back_ids, back_weights = together(fwd_buf, back_ids, back_weights)
    back_gate, back_slot = routing(back_ids[0], back_weights[0], expert)
    back_pick = picker_of(back_slot)
    grad_tokens = (back_gate[:, None] * upstream[0].astype(jnp.float32)).astype(jnp.bfloat16)
    held_rows = mirrored(held_rows)
    one, two, three, gate_x, grad_buf = together(
        *ask_mp(fwd_buf), other_core(gate_w), pack(back_pick, grad_tokens)
    )

    fwd_wide = widen(fwd_buf, (one, two, three), place)
    back_buf, one, two, three = together(pack(back_pick, held_rows), *ask_mp(grad_buf))
    back_one, fwd_behind, fwd_ahead, one, two, three, back_buf = together(
        along_mp(back_buf, 1), *both_ways(fwd_wide, fwd_wide), one, two, three, back_buf
    )

    grad_wide = widen(grad_buf, (one, two, three), place)
    grad_sent = stacked(fwd_behind[:half], grad_wide)
    cw, ccw, two, three, up_x, down_w = together(
        *both_ways(grad_sent, stacked(fwd_ahead[half:], grad_wide)),
        *(along_mp(back_buf, flip) for flip in (2, 3)),
        other_core(up_w),
        down_w,
    )
    one = back_one

    down_x = other_core(down_w)
    fwd_terms = run_fwd(
        (fwd_wide, fwd_behind, fwd_ahead, cw, ccw), (gate_w, up_w, down_w, gate_x, up_x, down_x)
    )
    grad_pieces = (grad_sent, cw, ccw)
    back_wide = widen(back_buf, (one, two, three), place ^ 3)
    back_sent = stacked(cw[half:CAP], back_wide)
    cw, ccw, down_x, *fwd_terms = together(
        *both_ways(back_sent, stacked(ccw[CAP:], back_wide)),
        down_x,
        *fwd_terms,
    )
    fwd_own, fwd_to_behind, fwd_to_ahead, fwd_low, fwd_high = fwd_terms

    hidden_grad, grad_rows = run_grad((*grad_pieces, cw, ccw), (down_w, down_x))
    back_pieces = (back_sent, cw, ccw)
    cw, ccw, hidden_grad, grad_rows = together(
        *both_ways(stacked(cw[half:CAP], fwd_low), stacked(ccw[CAP:], fwd_high)),
        hidden_grad,
        grad_rows,
    )

    back_terms = run_back((*back_pieces, cw, ccw), hidden_grad, (gate_w, up_w, gate_x, up_x))
    p0, p1, grad_rows_x, *back_terms = together(
        *near_with_far(fwd_to_behind, fwd_to_ahead, cw[half:], ccw[half:]),
        other_core(grad_rows),
        *back_terms,
    )
    back_own, back_to_behind, back_to_ahead, back_low, back_high = back_terms[:5]
    hidden, pair_grads, hidden_send, back_rows = back_terms[5:]

    fwd_total = add_parts(fwd_own, (p0, p1))
    f0, f1, hidden_x, back_rows_x, *fwd_blocks = together(
        *both_ways(back_low, back_high),
        other_core(hidden_send),
        other_core(back_rows),
        *split_mp(fwd_total, place),
    )

    units = gate_w.shape[0]
    p0, p1, one, two, three, grad_down, pair_grads = together(
        *near_with_far(back_to_behind, back_to_ahead, f0, f1),
        *send_mp(fwd_blocks[1:]),
        *run_weights(units, hidden, hidden_x[:units], grad_rows, grad_rows_x),
        pair_grads,
    )

    back_here, *back_sent = split_mp(add_parts(back_own, (p0, p1)), place)
    grad_gate, grad_up, *back_sent = together(
        *run_weights(units, pair_grads, hidden_x[units:], back_rows, back_rows_x),
        *send_mp(back_sent),
    )
    fwd_sum = add_parts(fwd_blocks[0], (one, two, three))
    fwd_row_gate = jnp.sum(jnp.where(fwd_pick, fwd_gate[None, :], 0.0), axis=1)
    expert_out = unpack(fwd_pick, (fwd_sum * fwd_row_gate[:, None]).astype(jnp.bfloat16))
    input_grad = unpack(back_pick, add_parts(back_here, back_sent).astype(jnp.bfloat16))
    return (
        expert_out[None],
        input_grad[None],
        grad_gate[None],
        grad_up[None],
        grad_down[None],
    )


def solution(mesh):
    placed = (
        P("section", "expert", "mp"),
        P("section", "expert", None),
        P("section", "expert", None),
        P("section", None, "expert", "mp"),
        P("section", "expert"),
        P("section", "expert", None),
        P("section", "expert", None),
        P("section", "expert", "mp"),
        P("section"),
        P("section", ("expert", "mp"), None),
        P("section", ("expert", "mp"), None),
        P("section", ("expert", "mp"), None),
    )
    return jax.shard_map(
        per_device,
        mesh=mesh,
        in_specs=placed,
        out_specs=(
            P("section", "expert", "mp"),
            P("section", "expert", "mp"),
            P("section", ("expert", "mp"), None),
            P("section", ("expert", "mp"), None),
            P("section", ("expert", "mp"), None),
        ),
        check_vma=False,
    )
```

```python
import jax
import jax.numpy as jnp
from jax import lax
from jax.experimental import pallas as pl
from jax.experimental.pallas import tpu as pltpu
from jax.sharding import PartitionSpec as P

CAP = 64


def together(*arrays):
    return lax.optimization_barrier(arrays)


def along_y(array, step):
    n = lax.axis_size("expert")
    return lax.ppermute(array, "expert", [(i, (i + 2 * step) % n) for i in range(n)])


def other_core(array):
    n = lax.axis_size("expert")
    return lax.ppermute(array, "expert", [(i, i ^ 1) for i in range(n)])


def along_mp(array, flip):
    n = lax.axis_size("mp")
    return lax.ppermute(array, "mp", [(i, i ^ flip) for i in range(n)])


def mirrored(array):
    sections, places = (lax.axis_size("section"), lax.axis_size("mp"))
    last = sections * places - 1
    return lax.ppermute(array, ("section", "mp"), [(i, last - i) for i in range(last + 1)])


def routing(pair_ids, pair_weights, expert):
    matches = pair_ids == expert
    routed = jnp.any(matches, axis=1)
    counted = routed.astype(jnp.int32)
    slot_of = jnp.cumsum(counted) - counted
    gate_share = jnp.sum(jnp.where(matches, pair_weights, 0.0), axis=1)
    return (gate_share, jnp.where(routed, slot_of, CAP))


def picker_of(slot_or_cap):
    places = jnp.arange(CAP, dtype=jnp.int32)[:, None]
    return slot_or_cap[None, :] == places


def pack(picker, values):
    return jnp.dot(
        picker.astype(jnp.bfloat16), values, preferred_element_type=jnp.float32
    ).astype(jnp.bfloat16)


def unpack(picker, rows):
    return lax.dot_general(
        picker.astype(jnp.bfloat16),
        rows,
        (((0,), (0,)), ((), ())),
        preferred_element_type=jnp.float32,
    ).astype(jnp.bfloat16)


def swapped(flag, first, second):
    return (jnp.where(flag, second, first), jnp.where(flag, first, second))


def beside(flag, here, there):
    first, second = swapped(flag, here, there)
    return jnp.concatenate([first, second], axis=1)


def widen(block, others, place):
    three, two, one = others
    odd, high = (place & 1) == 1, (place & 2) == 2
    return beside(high, beside(odd, block, one), beside(odd, two, three))


def ask_mp(block):
    three, two, one = (along_mp(block, flip) for flip in (3, 2, 1))
    return (three, two, one)


def both_ways(to_ahead, to_behind):
    return (along_y(to_ahead, 1), along_y(to_behind, -1))


def stacked(*arrays):
    return jnp.concatenate(arrays, axis=0)


def fetch(sources, target, sems, first):
    copies = []
    into = 0
    for index, (ref, start, rows) in enumerate(sources):
        copies.append(
            pltpu.make_async_copy(
                ref.at[pl.ds(start, rows)],
                target.at[pl.ds(into, rows)],
                sems.at[first + index],
            )
        )
        into += rows
    for copy in copies:
        copy.start()
    return copies


def whole(*refs):
    return tuple((ref, 0, ref.shape[0]) for ref in refs)


def arrive(copies):
    for copy in copies:
        copy.wait()


def times_rows(weight, rows):
    return lax.dot_general(
        weight, rows, (((1,), (1,)), ((), ())), preferred_element_type=jnp.float32
    )


def spread_kernel_part(pairs, own_ref, far_refs):
    width = own_ref.shape[1]
    step = min(width, 1024)
    for left in range(0, width, step):
        columns = slice(left, left + step)
        term = 0.0
        for hidden, weight in pairs:
            term = term + lax.dot_general(
                hidden,
                weight[:, columns],
                (((0,), (0,)), ((), ())),
                preferred_element_type=jnp.float32,
            )
        own_ref[:, columns] = term[:CAP]
        start = CAP
        for ref in far_refs:
            rows = ref.shape[0]
            ref[:, columns] = term[start : start + rows].astype(jnp.bfloat16)
            start += rows


def fwd_kernel(*refs):
    wide, behind, ahead, low, high = refs[:5]
    gate_own, up_own, down_own, gate_x, up_x, down_x = refs[5:11]
    own_ref, *far_refs = refs[11:16]
    rows, gate, up, down, sems = refs[16:]
    half = CAP // 2
    rows_in = fetch(whole(wide, behind, ahead) + ((low, 0, half), (high, 0, half)), rows, sems, 0)
    gate_in = fetch(whole(gate_own, gate_x), gate, sems, 5)
    up_in = fetch(whole(up_own, up_x), up, sems, 7)
    down_in = fetch(whole(down_own, down_x), down, sems, 9)
    arrive(rows_in)
    arrive(gate_in)
    pre = times_rows(gate[...], rows[...])
    arrive(up_in)
    hidden = (pre * jax.nn.sigmoid(pre) * times_rows(up[...], rows[...])).astype(jnp.bfloat16)
    arrive(down_in)
    spread_kernel_part(((hidden, down),), own_ref, far_refs)


def later_rows(refs):
    sent, behind, ahead, low, high = refs
    half = CAP // 2
    return (
        (sent, half, CAP),
        (behind, half, CAP),
        (ahead, half, CAP),
        (low, 0, half),
        (high, 0, half),
    )


def grad_kernel(*refs):
    down_own, down_x, hidden_ref, rows_out, rows, down, sems = refs[5:]
    rows_in = fetch(later_rows(refs[:5]), rows, sems, 0)
    down_in = fetch(whole(down_own, down_x), down, sems, 5)
    arrive(rows_in)
    keep = pltpu.make_async_copy(rows, rows_out, sems.at[7])
    keep.start()
    arrive(down_in)
    hidden_ref[...] = times_rows(down[...], rows[...])
    keep.wait()


def chunk_copies(sources, target, columns, sems):
    copies = []
    into = 0
    for index, (ref, start, rows) in enumerate(sources):
        copies.append(
            pltpu.make_async_copy(
                ref.at[pl.ds(start, rows), columns],
                target.at[pl.ds(into, rows), columns],
                sems.at[index],
            )
        )
        into += rows
    return copies


def back_kernel(*refs):
    pieces = later_rows(refs[:5])
    hidden_grad_ref, gate_own, up_own, gate_x, up_x = refs[5:10]
    block_outs, first_out, keep_out, send_out, rows_out = refs[10:15], *refs[15:19]
    rows, gate, up, block_own, block_far, hidden_all, in_sems, out_sems, rows_sem = refs[19:]
    units = gate_own.shape[0]
    width = rows.shape[1]
    step = width // CHUNKS
    loads = []
    for chunk in range(CHUNKS):
        columns = pl.ds(chunk * step, step)
        loads.append(
            chunk_copies(pieces, rows, columns, in_sems.at[chunk, 0])
            + chunk_copies(whole(gate_own, gate_x), gate, columns, in_sems.at[chunk, 1])
            + chunk_copies(whole(up_own, up_x), up, columns, in_sems.at[chunk, 2])
        )
    for copies in loads:
        for copy in copies:
            copy.start()
    pre_gate, pre_up = 0.0, 0.0
    for chunk, copies in enumerate(loads):
        columns = slice(chunk * step, (chunk + 1) * step)
        arrive(copies)
        pre_gate = pre_gate + times_rows(gate[:, columns], rows[:, columns])
        pre_up = pre_up + times_rows(up[:, columns], rows[:, columns])
    rows_back = pltpu.make_async_copy(rows, rows_out, rows_sem.at[0])
    rows_back.start()
    sigmoid_pre = jax.nn.sigmoid(pre_gate)
    activated = pre_gate * sigmoid_pre
    hidden_grad = hidden_grad_ref[...]
    hidden = (activated * pre_up).astype(jnp.bfloat16)
    gate_grad = (
        hidden_grad * pre_up * sigmoid_pre * (1.0 + pre_gate * (1.0 - sigmoid_pre))
    ).astype(jnp.bfloat16)
    up_grad = (hidden_grad * activated).astype(jnp.bfloat16)
    ordered = (
        hidden[:units],
        gate_grad[:units],
        up_grad[:units],
        hidden[units:],
        gate_grad[units:],
        up_grad[units:],
    )
    for index, array in enumerate(ordered):
        hidden_all[units * index : units * (index + 1)] = array
    stores = []
    for index, (out, start) in enumerate(((first_out, 0), (keep_out, 1), (send_out, 3))):
        part = pl.ds(units * start, out.shape[0])
        stores.append(pltpu.make_async_copy(hidden_all.at[part], out, rows_sem.at[index + 1]))
        stores[-1].start()
    for chunk in range(CHUNKS):
        columns = slice(chunk * step, (chunk + 1) * step)
        term = 0.0
        for array, weight in ((gate_grad, gate), (up_grad, up)):
            term = term + lax.dot_general(
                array,
                weight[:, columns],
                (((0,), (0,)), ((), ())),
                preferred_element_type=jnp.float32,
            )
        block_own[:, columns] = term[:CAP]
        block_far[:, columns] = term[CAP:].astype(jnp.bfloat16)
        columns = pl.ds(chunk * step, step)
        start = 0
        for index, out in enumerate(block_outs):
            source = block_own if index == 0 else block_far.at[pl.ds(start, out.shape[0])]
            start += out.shape[0] if index else 0
            stores.append(
                pltpu.make_async_copy(
                    source.at[:, columns], out.at[:, columns], out_sems.at[chunk, index]
                )
            )
            stores[-1].start()
    rows_back.wait()
    arrive(stores)


def weight_kernel(hidden_ref, hidden_x_ref, rows_ref, rows_x_ref, *outs):
    units = outs[0].shape[0]
    for index, out in enumerate(outs):
        part = slice(units * index, units * (index + 1))
        total = jnp.dot(hidden_ref[part], rows_ref[...], preferred_element_type=jnp.float32)
        total = total + jnp.dot(
            hidden_x_ref[part], rows_x_ref[...], preferred_element_type=jnp.float32
        )
        out[...] = total.astype(jnp.bfloat16)


HBM = pl.BlockSpec(memory_space=pltpu.HBM)
VMEM = pl.BlockSpec(memory_space=pltpu.VMEM)
CHUNKS = 4
PARAMS = pltpu.CompilerParams(vmem_limit_bytes=22 * 2**20)
SMALL = pl.CostEstimate(flops=1, bytes_accessed=1, transcendentals=0)


def block_shapes(width):
    sent = (CAP, CAP, CAP // 2, CAP // 2)
    return (jax.ShapeDtypeStruct((CAP, width), jnp.float32),) + tuple(
        jax.ShapeDtypeStruct((rows, width), jnp.bfloat16) for rows in sent
    )


def rows_shape(width):
    return jax.ShapeDtypeStruct((4 * CAP, width), jnp.bfloat16)


def scratch(units, width, weights, sems):
    return (
        [pltpu.VMEM((4 * CAP, width), jnp.bfloat16)]
        + [pltpu.VMEM((2 * units, width), jnp.bfloat16)] * weights
        + [pltpu.SemaphoreType.DMA((sems,))]
    )


def run_fwd(pieces, weights):
    units, width = weights[0].shape
    return pl.pallas_call(
        fwd_kernel,
        out_shape=block_shapes(width),
        in_specs=[HBM] * 11,
        out_specs=(VMEM,) * 5,
        scratch_shapes=scratch(units, width, 3, 11),
        compiler_params=PARAMS,
        cost_estimate=SMALL,
    )(*pieces, *weights)


def run_grad(pieces, weights):
    units, width = weights[0].shape
    return pl.pallas_call(
        grad_kernel,
        out_shape=(
            jax.ShapeDtypeStruct((2 * units, 4 * CAP), jnp.float32),
            rows_shape(width),
        ),
        in_specs=[HBM] * 7,
        out_specs=(VMEM, HBM),
        scratch_shapes=scratch(units, width, 1, 8),
        compiler_params=PARAMS,
        cost_estimate=SMALL,
    )(*pieces, *weights)


def run_back(pieces, hidden_grad, weights):
    units, width = weights[0].shape

    def hidden(count):
        return jax.ShapeDtypeStruct((count * units, 4 * CAP), jnp.bfloat16)

    return pl.pallas_call(
        back_kernel,
        out_shape=block_shapes(width) + (hidden(1), hidden(2), hidden(3), rows_shape(width)),
        in_specs=[HBM] * 5 + [VMEM] + [HBM] * 4,
        out_specs=(HBM,) * 9,
        scratch_shapes=[
            pltpu.VMEM((4 * CAP, width), jnp.bfloat16),
            pltpu.VMEM((2 * units, width), jnp.bfloat16),
            pltpu.VMEM((2 * units, width), jnp.bfloat16),
            pltpu.VMEM((CAP, width), jnp.float32),
            pltpu.VMEM((3 * CAP, width), jnp.bfloat16),
            pltpu.VMEM((6 * units, 4 * CAP), jnp.bfloat16),
            pltpu.SemaphoreType.DMA((CHUNKS, 3, 5)),
            pltpu.SemaphoreType.DMA((CHUNKS, 5)),
            pltpu.SemaphoreType.DMA((4,)),
        ],
        compiler_params=pltpu.CompilerParams(vmem_limit_bytes=56 * 2**20),
        cost_estimate=SMALL,
    )(*pieces, hidden_grad, *weights)


def run_weights(units, hidden, hidden_x, rows, rows_x):
    width = rows.shape[1]
    step = min(width, 1024)
    outs = hidden.shape[0] // units
    held = pl.BlockSpec(hidden.shape, lambda i: (0, 0))
    columns = pl.BlockSpec((rows.shape[0], step), lambda i: (0, i))
    return pl.pallas_call(
        weight_kernel,
        grid=(width // step,),
        out_shape=(jax.ShapeDtypeStruct((units, width), jnp.bfloat16),) * outs,
        in_specs=[held] * 2 + [columns] * 2,
        out_specs=(pl.BlockSpec((units, step), lambda i: (0, i)),) * outs,
        compiler_params=PARAMS,
        cost_estimate=SMALL,
    )(hidden, hidden_x, rows, rows_x)


def add_parts(own, parts):
    total = own
    for part in parts:
        total = total + part.astype(jnp.float32)
    return total


def near_with_far(behind, ahead, from_behind, from_ahead):
    half = from_behind.shape[0]

    def plus(block, start, extra):
        padded = jnp.pad(extra, ((start, block.shape[0] - half - start), (0, 0)))
        return (block.astype(jnp.float32) + padded.astype(jnp.float32)).astype(jnp.bfloat16)

    return both_ways(plus(ahead, 0, from_behind), plus(behind, half, from_ahead))


def split_mp(total, place):
    width = total.shape[1] // 4

    def columns(array, index):
        return lax.dynamic_slice_in_dim(array, index * width, width, axis=1)

    low = total.astype(jnp.bfloat16)
    return (columns(total, place),) + tuple(columns(low, place ^ flip) for flip in (1, 2, 3))


def send_mp(blocks):
    three, two, one = (along_mp(blocks[flip - 1], flip) for flip in (3, 2, 1))
    return (three, two, one)


def per_device(
    tokens_in,
    route_ids,
    route_weights,
    stash,
    returned_batch_index,
    back_ids,
    back_weights,
    upstream,
    window_expert,
    w_gate,
    w_up,
    w_down,
):
    expert = window_expert[0]
    place = lax.axis_index("mp")
    half = CAP // 2
    gate_w, up_w, down_w = (w_gate[0], w_up[0], w_down[0])

    fwd_gate, fwd_slot = routing(route_ids[0], route_weights[0], expert)
    fwd_pick = picker_of(fwd_slot)
    fwd_buf = pack(fwd_pick, tokens_in[0])
    held_rows = lax.dynamic_index_in_dim(
        stash[0], returned_batch_index[0, 0], axis=0, keepdims=False
    )
    fwd_buf, back_ids, back_weights = together(fwd_buf, back_ids, back_weights)
    back_gate, back_slot = routing(back_ids[0], back_weights[0], expert)
    back_pick = picker_of(back_slot)
    grad_tokens = (back_gate[:, None] * upstream[0].astype(jnp.float32)).astype(jnp.bfloat16)
    held_rows = mirrored(held_rows)
    three, two, one, gate_x, grad_buf = together(
        *ask_mp(fwd_buf), other_core(gate_w), pack(back_pick, grad_tokens)
    )

    fwd_wide = widen(fwd_buf, (three, two, one), place)
    three, two, one = ask_mp(grad_buf)
    back_buf, three = together(pack(back_pick, held_rows), three)
    fwd_behind, fwd_ahead, three, two, one, back_one, back_buf = together(
        *both_ways(fwd_wide, fwd_wide), three, two, one, along_mp(back_buf, 1), back_buf
    )

    grad_wide = widen(grad_buf, (three, two, one), place)
    grad_sent = stacked(fwd_behind[:half], grad_wide)
    cw, ccw, three, two, up_x, down_w = together(
        *both_ways(grad_sent, stacked(fwd_ahead[half:], grad_wide)),
        *(along_mp(back_buf, flip) for flip in (3, 2)),
        other_core(up_w),
        down_w,
    )

    down_x = other_core(down_w)
    fwd_terms = run_fwd(
        (fwd_wide, fwd_behind, fwd_ahead, cw, ccw), (gate_w, up_w, down_w, gate_x, up_x, down_x)
    )
    grad_pieces = (grad_sent, cw, ccw)
    back_wide = widen(back_buf, (three, two, back_one), place ^ 3)
    back_sent = stacked(cw[half:CAP], back_wide)
    cw, ccw, down_x, *fwd_terms = together(
        *both_ways(back_sent, stacked(ccw[CAP:], back_wide)),
        down_x,
        *fwd_terms,
    )
    fwd_own, fwd_to_behind, fwd_to_ahead, fwd_low, fwd_high = fwd_terms

    hidden_grad, grad_rows = run_grad((*grad_pieces, cw, ccw), (down_w, down_x))
    back_pieces = (back_sent, cw, ccw)
    cw, ccw, hidden_grad, grad_rows = together(
        *both_ways(stacked(cw[half:CAP], fwd_low), stacked(ccw[CAP:], fwd_high)),
        hidden_grad,
        grad_rows,
    )

    back_terms = run_back((*back_pieces, cw, ccw), hidden_grad, (gate_w, up_w, gate_x, up_x))
    p0, p1, grad_rows_x, *back_terms = together(
        *near_with_far(fwd_to_behind, fwd_to_ahead, cw[half:], ccw[half:]),
        other_core(grad_rows),
        *back_terms,
    )
    back_own, back_to_behind, back_to_ahead, back_low, back_high = back_terms[:5]
    hidden, pair_grads, hidden_send, back_rows = back_terms[5:]

    fwd_total = add_parts(fwd_own, (p0, p1))
    f0, f1, hidden_x, back_rows_x, *fwd_blocks = together(
        *both_ways(back_low, back_high),
        other_core(hidden_send),
        other_core(back_rows),
        *split_mp(fwd_total, place),
    )

    units = gate_w.shape[0]
    p0, p1, one, two, three, grad_down, pair_grads = together(
        *near_with_far(back_to_behind, back_to_ahead, f0, f1),
        *send_mp(fwd_blocks[1:]),
        *run_weights(units, hidden, hidden_x[:units], grad_rows, grad_rows_x),
        pair_grads,
    )

    back_here, *back_sent = split_mp(add_parts(back_own, (p0, p1)), place)
    grad_gate, grad_up, *back_sent = together(
        *run_weights(units, pair_grads, hidden_x[units:], back_rows, back_rows_x),
        *send_mp(back_sent),
    )
    fwd_sum = add_parts(fwd_blocks[0], (one, two, three))
    fwd_row_gate = jnp.sum(jnp.where(fwd_pick, fwd_gate[None, :], 0.0), axis=1)
    expert_out = unpack(fwd_pick, (fwd_sum * fwd_row_gate[:, None]).astype(jnp.bfloat16))
    input_grad = unpack(back_pick, add_parts(back_here, back_sent).astype(jnp.bfloat16))
    return (
        expert_out[None],
        input_grad[None],
        grad_gate[None],
        grad_up[None],
        grad_down[None],
    )


def solution(mesh):
    placed = (
        P("section", "expert", "mp"),
        P("section", "expert", None),
        P("section", "expert", None),
        P("section", None, "expert", "mp"),
        P("section", "expert"),
        P("section", "expert", None),
        P("section", "expert", None),
        P("section", "expert", "mp"),
        P("section"),
        P("section", ("expert", "mp"), None),
        P("section", ("expert", "mp"), None),
        P("section", ("expert", "mp"), None),
    )
    return jax.shard_map(
        per_device,
        mesh=mesh,
        in_specs=placed,
        out_specs=(
            P("section", "expert", "mp"),
            P("section", "expert", "mp"),
            P("section", ("expert", "mp"), None),
            P("section", ("expert", "mp"), None),
            P("section", ("expert", "mp"), None),
        ),
        check_vma=False,
    )
```

```python
import jax
import jax.numpy as jnp
from jax import lax
from jax.experimental import pallas as pl
from jax.experimental.pallas import tpu as pltpu
from jax.sharding import PartitionSpec as P

CAP = 64


def together(*arrays):
    return lax.optimization_barrier(arrays)


def along_y(array, step):
    n = lax.axis_size("expert")
    return lax.ppermute(array, "expert", [(i, (i + 2 * step) % n) for i in range(n)])


def other_core(array):
    n = lax.axis_size("expert")
    return lax.ppermute(array, "expert", [(i, i ^ 1) for i in range(n)])


def along_mp(array, flip):
    n = lax.axis_size("mp")
    return lax.ppermute(array, "mp", [(i, i ^ flip) for i in range(n)])


def mirrored(array):
    sections, places = (lax.axis_size("section"), lax.axis_size("mp"))
    last = sections * places - 1
    return lax.ppermute(array, ("section", "mp"), [(i, last - i) for i in range(last + 1)])


def routing(pair_ids, pair_weights, expert):
    matches = pair_ids == expert
    routed = jnp.any(matches, axis=1)
    counted = routed.astype(jnp.int32)
    slot_of = jnp.cumsum(counted) - counted
    gate_share = jnp.sum(jnp.where(matches, pair_weights, 0.0), axis=1)
    return (gate_share, jnp.where(routed, slot_of, CAP))


def picker_of(slot_or_cap):
    places = jnp.arange(CAP, dtype=jnp.int32)[:, None]
    return slot_or_cap[None, :] == places


def pack(picker, values):
    return jnp.dot(
        picker.astype(jnp.bfloat16), values, preferred_element_type=jnp.float32
    ).astype(jnp.bfloat16)


def unpack(picker, rows):
    return lax.dot_general(
        picker.astype(jnp.bfloat16),
        rows,
        (((0,), (0,)), ((), ())),
        preferred_element_type=jnp.float32,
    ).astype(jnp.bfloat16)


def swapped(flag, first, second):
    return (jnp.where(flag, second, first), jnp.where(flag, first, second))


def beside(flag, here, there):
    first, second = swapped(flag, here, there)
    return jnp.concatenate([first, second], axis=1)


def widen(block, others, place):
    three, two, one = others
    odd, high = (place & 1) == 1, (place & 2) == 2
    return beside(high, beside(odd, block, one), beside(odd, two, three))


def ask_mp(block):
    three, two, one = (along_mp(block, flip) for flip in (3, 2, 1))
    return (three, two, one)


def both_ways(to_ahead, to_behind):
    return (along_y(to_ahead, 1), along_y(to_behind, -1))


def stacked(*arrays):
    return jnp.concatenate(arrays, axis=0)


def fetch(sources, target, sems, first):
    copies = []
    into = 0
    for index, (ref, start, rows) in enumerate(sources):
        copies.append(
            pltpu.make_async_copy(
                ref.at[pl.ds(start, rows)],
                target.at[pl.ds(into, rows)],
                sems.at[first + index],
            )
        )
        into += rows
    for copy in copies:
        copy.start()
    return copies


def whole(*refs):
    return tuple((ref, 0, ref.shape[0]) for ref in refs)


def arrive(copies):
    for copy in copies:
        copy.wait()


def times_rows(weight, rows):
    return lax.dot_general(
        weight, rows, (((1,), (1,)), ((), ())), preferred_element_type=jnp.float32
    )


def spread_kernel_part(pairs, own_ref, far_refs):
    width = own_ref.shape[1]
    step = min(width, 1024)
    for left in range(0, width, step):
        columns = slice(left, left + step)
        term = 0.0
        for hidden, weight in pairs:
            term = term + lax.dot_general(
                hidden,
                weight[:, columns],
                (((0,), (0,)), ((), ())),
                preferred_element_type=jnp.float32,
            )
        own_ref[:, columns] = term[:CAP]
        start = CAP
        for ref in far_refs:
            rows = ref.shape[0]
            ref[:, columns] = term[start : start + rows].astype(jnp.bfloat16)
            start += rows


def fwd_kernel(*refs):
    wide, behind, ahead, low, high = refs[:5]
    gate_own, up_own, down_own, gate_x, up_x, down_x = refs[5:11]
    own_ref, *far_refs = refs[11:16]
    rows, gate, up, down, sems = refs[16:]
    half = CAP // 2
    rows_in = fetch(whole(wide, behind, ahead) + ((low, 0, half), (high, 0, half)), rows, sems, 0)
    gate_in = fetch(whole(gate_own, gate_x), gate, sems, 5)
    up_in = fetch(whole(up_own, up_x), up, sems, 7)
    down_in = fetch(whole(down_own, down_x), down, sems, 9)
    arrive(rows_in)
    arrive(gate_in)
    pre = times_rows(gate[...], rows[...])
    arrive(up_in)
    hidden = (pre * jax.nn.sigmoid(pre) * times_rows(up[...], rows[...])).astype(jnp.bfloat16)
    arrive(down_in)
    spread_kernel_part(((hidden, down),), own_ref, far_refs)


def later_rows(refs):
    sent, behind, ahead, low, high = refs
    half = CAP // 2
    return (
        (sent, half, CAP),
        (behind, half, CAP),
        (ahead, half, CAP),
        (low, 0, half),
        (high, 0, half),
    )


def grad_kernel(*refs):
    down_own, down_x, hidden_ref, rows_out, rows, down, sems = refs[5:]
    rows_in = fetch(later_rows(refs[:5]), rows, sems, 0)
    down_in = fetch(whole(down_own, down_x), down, sems, 5)
    arrive(rows_in)
    keep = pltpu.make_async_copy(rows, rows_out, sems.at[7])
    keep.start()
    arrive(down_in)
    hidden_ref[...] = times_rows(down[...], rows[...])
    keep.wait()


def chunk_copies(sources, target, columns, sems):
    copies = []
    into = 0
    for index, (ref, start, rows) in enumerate(sources):
        copies.append(
            pltpu.make_async_copy(
                ref.at[pl.ds(start, rows), columns],
                target.at[pl.ds(into, rows), columns],
                sems.at[index],
            )
        )
        into += rows
    return copies


def back_kernel(*refs):
    pieces = later_rows(refs[:5])
    hidden_grad_ref, gate_own, up_own, gate_x, up_x = refs[5:10]
    block_outs, first_out, keep_out, send_out, rows_out = refs[10:15], *refs[15:19]
    rows, gate, up, block_own, block_far, hidden_all, in_sems, out_sems, rows_sem = refs[19:]
    units = gate_own.shape[0]
    width = rows.shape[1]
    step = width // CHUNKS
    loads = []
    for chunk in range(CHUNKS):
        columns = pl.ds(chunk * step, step)
        loads.append(
            chunk_copies(pieces, rows, columns, in_sems.at[chunk, 0])
            + chunk_copies(whole(gate_own, gate_x), gate, columns, in_sems.at[chunk, 1])
            + chunk_copies(whole(up_own, up_x), up, columns, in_sems.at[chunk, 2])
        )
    for copies in loads:
        for copy in copies:
            copy.start()
    pre_gate, pre_up = 0.0, 0.0
    for chunk, copies in enumerate(loads):
        columns = slice(chunk * step, (chunk + 1) * step)
        arrive(copies)
        pre_gate = pre_gate + times_rows(gate[:, columns], rows[:, columns])
        pre_up = pre_up + times_rows(up[:, columns], rows[:, columns])
    rows_back = pltpu.make_async_copy(rows, rows_out, rows_sem.at[0])
    rows_back.start()
    sigmoid_pre = jax.nn.sigmoid(pre_gate)
    activated = pre_gate * sigmoid_pre
    hidden_grad = hidden_grad_ref[...]
    hidden = (activated * pre_up).astype(jnp.bfloat16)
    gate_grad = (
        hidden_grad * pre_up * sigmoid_pre * (1.0 + pre_gate * (1.0 - sigmoid_pre))
    ).astype(jnp.bfloat16)
    up_grad = (hidden_grad * activated).astype(jnp.bfloat16)
    ordered = (
        hidden[:units],
        gate_grad[:units],
        up_grad[:units],
        hidden[units:],
        gate_grad[units:],
        up_grad[units:],
    )
    for index, array in enumerate(ordered):
        hidden_all[units * index : units * (index + 1)] = array
    stores = []
    for index, (out, start) in enumerate(((first_out, 0), (keep_out, 1), (send_out, 3))):
        part = pl.ds(units * start, out.shape[0])
        stores.append(pltpu.make_async_copy(hidden_all.at[part], out, rows_sem.at[index + 1]))
        stores[-1].start()
    for chunk in range(CHUNKS):
        columns = slice(chunk * step, (chunk + 1) * step)
        term = 0.0
        for array, weight in ((gate_grad, gate), (up_grad, up)):
            term = term + lax.dot_general(
                array,
                weight[:, columns],
                (((0,), (0,)), ((), ())),
                preferred_element_type=jnp.float32,
            )
        block_own[:, columns] = term[:CAP]
        block_far[:, columns] = term[CAP:].astype(jnp.bfloat16)
        columns = pl.ds(chunk * step, step)
        start = 0
        for index, out in enumerate(block_outs):
            source = block_own if index == 0 else block_far.at[pl.ds(start, out.shape[0])]
            start += out.shape[0] if index else 0
            stores.append(
                pltpu.make_async_copy(
                    source.at[:, columns], out.at[:, columns], out_sems.at[chunk, index]
                )
            )
            stores[-1].start()
    rows_back.wait()
    arrive(stores)


def weight_kernel(hidden_ref, hidden_x_ref, rows_ref, rows_x_ref, *outs):
    units = outs[0].shape[0]
    for index, out in enumerate(outs):
        part = slice(units * index, units * (index + 1))
        total = jnp.dot(hidden_ref[part], rows_ref[...], preferred_element_type=jnp.float32)
        total = total + jnp.dot(
            hidden_x_ref[part], rows_x_ref[...], preferred_element_type=jnp.float32
        )
        out[...] = total.astype(jnp.bfloat16)


HBM = pl.BlockSpec(memory_space=pltpu.HBM)
VMEM = pl.BlockSpec(memory_space=pltpu.VMEM)
CHUNKS = 4
PARAMS = pltpu.CompilerParams(vmem_limit_bytes=22 * 2**20)
SMALL = pl.CostEstimate(flops=1, bytes_accessed=1, transcendentals=0)


def block_shapes(width):
    sent = (CAP, CAP, CAP // 2, CAP // 2)
    return (jax.ShapeDtypeStruct((CAP, width), jnp.float32),) + tuple(
        jax.ShapeDtypeStruct((rows, width), jnp.bfloat16) for rows in sent
    )


def rows_shape(width):
    return jax.ShapeDtypeStruct((4 * CAP, width), jnp.bfloat16)


def scratch(units, width, weights, sems):
    return (
        [pltpu.VMEM((4 * CAP, width), jnp.bfloat16)]
        + [pltpu.VMEM((2 * units, width), jnp.bfloat16)] * weights
        + [pltpu.SemaphoreType.DMA((sems,))]
    )


def run_fwd(pieces, weights):
    units, width = weights[0].shape
    return pl.pallas_call(
        fwd_kernel,
        out_shape=block_shapes(width),
        in_specs=[HBM] * 11,
        out_specs=(VMEM,) * 5,
        scratch_shapes=scratch(units, width, 3, 11),
        compiler_params=PARAMS,
        cost_estimate=SMALL,
    )(*pieces, *weights)


def run_grad(pieces, weights):
    units, width = weights[0].shape
    return pl.pallas_call(
        grad_kernel,
        out_shape=(
            jax.ShapeDtypeStruct((2 * units, 4 * CAP), jnp.float32),
            rows_shape(width),
        ),
        in_specs=[HBM] * 7,
        out_specs=(VMEM, HBM),
        scratch_shapes=scratch(units, width, 1, 8),
        compiler_params=PARAMS,
        cost_estimate=SMALL,
    )(*pieces, *weights)


def run_back(pieces, hidden_grad, weights):
    units, width = weights[0].shape

    def hidden(count):
        return jax.ShapeDtypeStruct((count * units, 4 * CAP), jnp.bfloat16)

    return pl.pallas_call(
        back_kernel,
        out_shape=block_shapes(width) + (hidden(1), hidden(2), hidden(3), rows_shape(width)),
        in_specs=[HBM] * 5 + [VMEM] + [HBM] * 4,
        out_specs=(HBM,) * 9,
        scratch_shapes=[
            pltpu.VMEM((4 * CAP, width), jnp.bfloat16),
            pltpu.VMEM((2 * units, width), jnp.bfloat16),
            pltpu.VMEM((2 * units, width), jnp.bfloat16),
            pltpu.VMEM((CAP, width), jnp.float32),
            pltpu.VMEM((3 * CAP, width), jnp.bfloat16),
            pltpu.VMEM((6 * units, 4 * CAP), jnp.bfloat16),
            pltpu.SemaphoreType.DMA((CHUNKS, 3, 5)),
            pltpu.SemaphoreType.DMA((CHUNKS, 5)),
            pltpu.SemaphoreType.DMA((4,)),
        ],
        compiler_params=pltpu.CompilerParams(vmem_limit_bytes=30 * 2**20),
        cost_estimate=SMALL,
    )(*pieces, hidden_grad, *weights)


def run_weights(units, hidden, hidden_x, rows, rows_x):
    width = rows.shape[1]
    step = min(width, 1024)
    outs = hidden.shape[0] // units
    held = pl.BlockSpec(hidden.shape, lambda i: (0, 0))
    columns = pl.BlockSpec((rows.shape[0], step), lambda i: (0, i))
    return pl.pallas_call(
        weight_kernel,
        grid=(width // step,),
        out_shape=(jax.ShapeDtypeStruct((units, width), jnp.bfloat16),) * outs,
        in_specs=[held] * 2 + [columns] * 2,
        out_specs=(pl.BlockSpec((units, step), lambda i: (0, i)),) * outs,
        compiler_params=PARAMS,
        cost_estimate=SMALL,
    )(hidden, hidden_x, rows, rows_x)


def add_parts(own, parts):
    total = own
    for part in parts:
        total = total + part.astype(jnp.float32)
    return total


def near_with_far(behind, ahead, from_behind, from_ahead):
    half = from_behind.shape[0]

    def plus(block, start, extra):
        padded = jnp.pad(extra, ((start, block.shape[0] - half - start), (0, 0)))
        return (block.astype(jnp.float32) + padded.astype(jnp.float32)).astype(jnp.bfloat16)

    return both_ways(plus(ahead, 0, from_behind), plus(behind, half, from_ahead))


def split_mp(total, place):
    width = total.shape[1] // 4

    def columns(array, index):
        return lax.dynamic_slice_in_dim(array, index * width, width, axis=1)

    low = total.astype(jnp.bfloat16)
    return (columns(total, place),) + tuple(columns(low, place ^ flip) for flip in (1, 2, 3))


def send_mp(blocks):
    three, two, one = (along_mp(blocks[flip - 1], flip) for flip in (3, 2, 1))
    return (three, two, one)


def per_device(
    tokens_in,
    route_ids,
    route_weights,
    stash,
    returned_batch_index,
    back_ids,
    back_weights,
    upstream,
    window_expert,
    w_gate,
    w_up,
    w_down,
):
    expert = window_expert[0]
    place = lax.axis_index("mp")
    half = CAP // 2
    gate_w, up_w, down_w = (w_gate[0], w_up[0], w_down[0])

    fwd_gate, fwd_slot = routing(route_ids[0], route_weights[0], expert)
    fwd_pick = picker_of(fwd_slot)
    fwd_buf = pack(fwd_pick, tokens_in[0])
    held_rows = lax.dynamic_index_in_dim(
        stash[0], returned_batch_index[0, 0], axis=0, keepdims=False
    )
    fwd_buf, back_ids, back_weights = together(fwd_buf, back_ids, back_weights)
    back_gate, back_slot = routing(back_ids[0], back_weights[0], expert)
    back_pick = picker_of(back_slot)
    grad_tokens = (back_gate[:, None] * upstream[0].astype(jnp.float32)).astype(jnp.bfloat16)
    held_rows = mirrored(held_rows)
    three, two, one, gate_x, grad_buf = together(
        *ask_mp(fwd_buf), other_core(gate_w), pack(back_pick, grad_tokens)
    )

    fwd_wide = widen(fwd_buf, (three, two, one), place)
    three, two, one = ask_mp(grad_buf)
    back_buf, three = together(pack(back_pick, held_rows), three)
    fwd_behind, fwd_ahead, three, two, one, back_one, back_buf = together(
        *both_ways(fwd_wide, fwd_wide), three, two, one, along_mp(back_buf, 1), back_buf
    )

    grad_wide = widen(grad_buf, (three, two, one), place)
    grad_sent = stacked(fwd_behind[:half], grad_wide)
    cw, ccw, three, two, up_x, down_w = together(
        *both_ways(grad_sent, stacked(fwd_ahead[half:], grad_wide)),
        *(along_mp(back_buf, flip) for flip in (3, 2)),
        other_core(up_w),
        down_w,
    )

    down_x = other_core(down_w)
    fwd_terms = run_fwd(
        (fwd_wide, fwd_behind, fwd_ahead, cw, ccw), (gate_w, up_w, down_w, gate_x, up_x, down_x)
    )
    grad_pieces = (grad_sent, cw, ccw)
    back_wide = widen(back_buf, (three, two, back_one), place ^ 3)
    back_sent = stacked(cw[half:CAP], back_wide)
    cw, ccw, down_x, *fwd_terms = together(
        *both_ways(back_sent, stacked(ccw[CAP:], back_wide)),
        down_x,
        *fwd_terms,
    )
    fwd_own, fwd_to_behind, fwd_to_ahead, fwd_low, fwd_high = fwd_terms

    hidden_grad, grad_rows = run_grad((*grad_pieces, cw, ccw), (down_w, down_x))
    back_pieces = (back_sent, cw, ccw)
    cw, ccw, hidden_grad, grad_rows = together(
        *both_ways(stacked(cw[half:CAP], fwd_low), stacked(ccw[CAP:], fwd_high)),
        hidden_grad,
        grad_rows,
    )

    back_terms = run_back((*back_pieces, cw, ccw), hidden_grad, (gate_w, up_w, gate_x, up_x))
    p0, p1, grad_rows_x, *back_terms = together(
        *near_with_far(fwd_to_behind, fwd_to_ahead, cw[half:], ccw[half:]),
        other_core(grad_rows),
        *back_terms,
    )
    back_own, back_to_behind, back_to_ahead, back_low, back_high = back_terms[:5]
    hidden, pair_grads, hidden_send, back_rows = back_terms[5:]

    fwd_total = add_parts(fwd_own, (p0, p1))
    f0, f1, hidden_x, back_rows_x, *fwd_blocks = together(
        *both_ways(back_low, back_high),
        other_core(hidden_send),
        other_core(back_rows),
        *split_mp(fwd_total, place),
    )

    units = gate_w.shape[0]
    p0, p1, one, two, three, grad_down, pair_grads = together(
        *near_with_far(back_to_behind, back_to_ahead, f0, f1),
        *send_mp(fwd_blocks[1:]),
        *run_weights(units, hidden, hidden_x[:units], grad_rows, grad_rows_x),
        pair_grads,
    )

    back_here, *back_sent = split_mp(add_parts(back_own, (p0, p1)), place)
    grad_gate, grad_up, *back_sent = together(
        *run_weights(units, pair_grads, hidden_x[units:], back_rows, back_rows_x),
        *send_mp(back_sent),
    )
    fwd_sum = add_parts(fwd_blocks[0], (one, two, three))
    fwd_row_gate = jnp.sum(jnp.where(fwd_pick, fwd_gate[None, :], 0.0), axis=1)
    expert_out = unpack(fwd_pick, (fwd_sum * fwd_row_gate[:, None]).astype(jnp.bfloat16))
    input_grad = unpack(back_pick, add_parts(back_here, back_sent).astype(jnp.bfloat16))
    return (
        expert_out[None],
        input_grad[None],
        grad_gate[None],
        grad_up[None],
        grad_down[None],
    )


def solution(mesh):
    placed = (
        P("section", "expert", "mp"),
        P("section", "expert", None),
        P("section", "expert", None),
        P("section", None, "expert", "mp"),
        P("section", "expert"),
        P("section", "expert", None),
        P("section", "expert", None),
        P("section", "expert", "mp"),
        P("section"),
        P("section", ("expert", "mp"), None),
        P("section", ("expert", "mp"), None),
        P("section", ("expert", "mp"), None),
    )
    return jax.shard_map(
        per_device,
        mesh=mesh,
        in_specs=placed,
        out_specs=(
            P("section", "expert", "mp"),
            P("section", "expert", "mp"),
            P("section", ("expert", "mp"), None),
            P("section", ("expert", "mp"), None),
            P("section", ("expert", "mp"), None),
        ),
        check_vma=False,
    )
```

```python
import jax
import jax.numpy as jnp
from jax import lax
from jax.experimental import pallas as pl
from jax.experimental.pallas import tpu as pltpu
from jax.sharding import PartitionSpec as P

CAP = 64


def together(*arrays):
    return lax.optimization_barrier(arrays)


def along_y(array, step):
    n = lax.axis_size("expert")
    return lax.ppermute(array, "expert", [(i, (i + 2 * step) % n) for i in range(n)])


def other_core(array):
    n = lax.axis_size("expert")
    return lax.ppermute(array, "expert", [(i, i ^ 1) for i in range(n)])


def along_mp(array, flip):
    n = lax.axis_size("mp")
    return lax.ppermute(array, "mp", [(i, i ^ flip) for i in range(n)])


def mirrored(array):
    sections, places = (lax.axis_size("section"), lax.axis_size("mp"))
    last = sections * places - 1
    return lax.ppermute(array, ("section", "mp"), [(i, last - i) for i in range(last + 1)])


def routing(pair_ids, pair_weights, expert):
    matches = pair_ids == expert
    routed = jnp.any(matches, axis=1)
    counted = routed.astype(jnp.int32)
    slot_of = jnp.cumsum(counted) - counted
    gate_share = jnp.sum(jnp.where(matches, pair_weights, 0.0), axis=1)
    return (gate_share, jnp.where(routed, slot_of, CAP))


def picker_of(slot_or_cap):
    places = jnp.arange(CAP, dtype=jnp.int32)[:, None]
    return slot_or_cap[None, :] == places


def pack(picker, values):
    return jnp.dot(
        picker.astype(jnp.bfloat16), values, preferred_element_type=jnp.float32
    ).astype(jnp.bfloat16)


def unpack(picker, rows):
    return lax.dot_general(
        picker.astype(jnp.bfloat16),
        rows,
        (((0,), (0,)), ((), ())),
        preferred_element_type=jnp.float32,
    ).astype(jnp.bfloat16)


def swapped(flag, first, second):
    return (jnp.where(flag, second, first), jnp.where(flag, first, second))


def beside(flag, here, there):
    first, second = swapped(flag, here, there)
    return jnp.concatenate([first, second], axis=1)


def widen(block, others, place):
    three, two, one = others
    odd, high = (place & 1) == 1, (place & 2) == 2
    return beside(high, beside(odd, block, one), beside(odd, two, three))


def ask_mp(block):
    three, two, one = (along_mp(block, flip) for flip in (3, 2, 1))
    return (three, two, one)


def both_ways(to_ahead, to_behind):
    return (along_y(to_ahead, 1), along_y(to_behind, -1))


def stacked(*arrays):
    return jnp.concatenate(arrays, axis=0)


def fetch(sources, target, sems, first):
    copies = []
    into = 0
    for index, (ref, start, rows) in enumerate(sources):
        copies.append(
            pltpu.make_async_copy(
                ref.at[pl.ds(start, rows)],
                target.at[pl.ds(into, rows)],
                sems.at[first + index],
            )
        )
        into += rows
    for copy in copies:
        copy.start()
    return copies


def whole(*refs):
    return tuple((ref, 0, ref.shape[0]) for ref in refs)


def arrive(copies):
    for copy in copies:
        copy.wait()


def times_rows(weight, rows):
    return lax.dot_general(
        weight, rows, (((1,), (1,)), ((), ())), preferred_element_type=jnp.float32
    )


def spread_kernel_part(pairs, own_ref, far_refs):
    width = own_ref.shape[1]
    step = min(width, 1024)
    for left in range(0, width, step):
        columns = slice(left, left + step)
        term = 0.0
        for hidden, weight in pairs:
            term = term + lax.dot_general(
                hidden,
                weight[:, columns],
                (((0,), (0,)), ((), ())),
                preferred_element_type=jnp.float32,
            )
        own_ref[:, columns] = term[:CAP]
        start = CAP
        for ref in far_refs:
            rows = ref.shape[0]
            ref[:, columns] = term[start : start + rows].astype(jnp.bfloat16)
            start += rows


def fwd_kernel(*refs):
    wide, behind, ahead, low, high = refs[:5]
    gate_own, up_own, down_own, gate_x, up_x, down_x = refs[5:11]
    own_ref, *far_refs = refs[11:16]
    rows, gate, up, down, sems = refs[16:]
    half = CAP // 2
    rows_in = fetch(whole(wide, behind, ahead) + ((low, 0, half), (high, 0, half)), rows, sems, 0)
    gate_in = fetch(whole(gate_own, gate_x), gate, sems, 5)
    up_in = fetch(whole(up_own, up_x), up, sems, 7)
    down_in = fetch(whole(down_own, down_x), down, sems, 9)
    arrive(rows_in)
    arrive(gate_in)
    pre = times_rows(gate[...], rows[...])
    arrive(up_in)
    hidden = (pre * jax.nn.sigmoid(pre) * times_rows(up[...], rows[...])).astype(jnp.bfloat16)
    arrive(down_in)
    spread_kernel_part(((hidden, down),), own_ref, far_refs)


def later_rows(refs):
    sent, behind, ahead, low, high = refs
    half = CAP // 2
    return (
        (sent, half, CAP),
        (behind, half, CAP),
        (ahead, half, CAP),
        (low, 0, half),
        (high, 0, half),
    )


def grad_kernel(*refs):
    down_own, down_x, hidden_ref, rows_out, rows, down, sems = refs[5:]
    rows_in = fetch(later_rows(refs[:5]), rows, sems, 0)
    down_in = fetch(whole(down_own, down_x), down, sems, 5)
    arrive(rows_in)
    keep = pltpu.make_async_copy(rows, rows_out, sems.at[7])
    keep.start()
    arrive(down_in)
    hidden_ref[...] = times_rows(down[...], rows[...])
    keep.wait()


def chunk_copies(sources, target, columns, sems):
    copies = []
    into = 0
    for index, (ref, start, rows) in enumerate(sources):
        copies.append(
            pltpu.make_async_copy(
                ref.at[pl.ds(start, rows), columns],
                target.at[pl.ds(into, rows), columns],
                sems.at[index],
            )
        )
        into += rows
    return copies


def back_kernel(*refs):
    pieces = later_rows(refs[:5])
    hidden_grad_ref, gate_own, up_own, gate_x, up_x = refs[5:10]
    block_outs, first_out, keep_out, send_out, rows_out = refs[10:15], *refs[15:19]
    rows, gate, up, block_own, block_far, hidden_all, in_sems, out_sems, rows_sem = refs[19:]
    units = gate_own.shape[0]
    width = rows.shape[1]
    step = width // CHUNKS
    loads = []
    for chunk in range(CHUNKS):
        columns = pl.ds(chunk * step, step)
        loads.append(
            chunk_copies(pieces, rows, columns, in_sems.at[chunk, 0])
            + chunk_copies(whole(gate_own, gate_x), gate, columns, in_sems.at[chunk, 1])
            + chunk_copies(whole(up_own, up_x), up, columns, in_sems.at[chunk, 2])
        )
    for copies in loads:
        for copy in copies:
            copy.start()
    pre_gate, pre_up = 0.0, 0.0
    for chunk, copies in enumerate(loads):
        columns = slice(chunk * step, (chunk + 1) * step)
        arrive(copies)
        pre_gate = pre_gate + times_rows(gate[:, columns], rows[:, columns])
        pre_up = pre_up + times_rows(up[:, columns], rows[:, columns])
    rows_back = pltpu.make_async_copy(rows, rows_out, rows_sem.at[0])
    rows_back.start()
    sigmoid_pre = jax.nn.sigmoid(pre_gate)
    activated = pre_gate * sigmoid_pre
    hidden_grad = hidden_grad_ref[...]
    hidden = (activated * pre_up).astype(jnp.bfloat16)
    gate_grad = (
        hidden_grad * pre_up * sigmoid_pre * (1.0 + pre_gate * (1.0 - sigmoid_pre))
    ).astype(jnp.bfloat16)
    up_grad = (hidden_grad * activated).astype(jnp.bfloat16)
    ordered = (
        hidden[:units],
        gate_grad[:units],
        up_grad[:units],
        hidden[units:],
        gate_grad[units:],
        up_grad[units:],
    )
    for index, array in enumerate(ordered):
        hidden_all[units * index : units * (index + 1)] = array
    stores = []
    for index, (out, start) in enumerate(((first_out, 0), (keep_out, 1), (send_out, 3))):
        part = pl.ds(units * start, out.shape[0])
        stores.append(pltpu.make_async_copy(hidden_all.at[part], out, rows_sem.at[index + 1]))
        stores[-1].start()
    for chunk in range(CHUNKS):
        columns = slice(chunk * step, (chunk + 1) * step)
        term = 0.0
        for array, weight in ((gate_grad, gate), (up_grad, up)):
            term = term + lax.dot_general(
                array,
                weight[:, columns],
                (((0,), (0,)), ((), ())),
                preferred_element_type=jnp.float32,
            )
        block_own[:, columns] = term[:CAP]
        block_far[:, columns] = term[CAP:].astype(jnp.bfloat16)
        columns = pl.ds(chunk * step, step)
        start = 0
        for index, out in enumerate(block_outs):
            source = block_own if index == 0 else block_far.at[pl.ds(start, out.shape[0])]
            start += out.shape[0] if index else 0
            stores.append(
                pltpu.make_async_copy(
                    source.at[:, columns], out.at[:, columns], out_sems.at[chunk, index]
                )
            )
            stores[-1].start()
    rows_back.wait()
    arrive(stores)


def weight_kernel(hidden_ref, hidden_x_ref, rows_ref, rows_x_ref, *outs):
    units = outs[0].shape[0]
    for index, out in enumerate(outs):
        part = slice(units * index, units * (index + 1))
        total = jnp.dot(hidden_ref[part], rows_ref[...], preferred_element_type=jnp.float32)
        total = total + jnp.dot(
            hidden_x_ref[part], rows_x_ref[...], preferred_element_type=jnp.float32
        )
        out[...] = total.astype(jnp.bfloat16)


HBM = pl.BlockSpec(memory_space=pltpu.HBM)
VMEM = pl.BlockSpec(memory_space=pltpu.VMEM)
CHUNKS = 4
PARAMS = pltpu.CompilerParams(vmem_limit_bytes=22 * 2**20)
SMALL = pl.CostEstimate(flops=1, bytes_accessed=1, transcendentals=0)


def block_shapes(width):
    sent = (CAP, CAP, CAP // 2, CAP // 2)
    return (jax.ShapeDtypeStruct((CAP, width), jnp.float32),) + tuple(
        jax.ShapeDtypeStruct((rows, width), jnp.bfloat16) for rows in sent
    )


def rows_shape(width):
    return jax.ShapeDtypeStruct((4 * CAP, width), jnp.bfloat16)


def scratch(units, width, weights, sems):
    return (
        [pltpu.VMEM((4 * CAP, width), jnp.bfloat16)]
        + [pltpu.VMEM((2 * units, width), jnp.bfloat16)] * weights
        + [pltpu.SemaphoreType.DMA((sems,))]
    )


def run_fwd(pieces, weights):
    units, width = weights[0].shape
    return pl.pallas_call(
        fwd_kernel,
        out_shape=block_shapes(width),
        in_specs=[HBM] * 11,
        out_specs=(VMEM,) * 5,
        scratch_shapes=scratch(units, width, 3, 11),
        compiler_params=PARAMS,
        cost_estimate=SMALL,
    )(*pieces, *weights)


def run_grad(pieces, weights):
    units, width = weights[0].shape
    return pl.pallas_call(
        grad_kernel,
        out_shape=(
            jax.ShapeDtypeStruct((2 * units, 4 * CAP), jnp.float32),
            rows_shape(width),
        ),
        in_specs=[HBM] * 7,
        out_specs=(VMEM, HBM),
        scratch_shapes=scratch(units, width, 1, 8),
        compiler_params=PARAMS,
        cost_estimate=SMALL,
    )(*pieces, *weights)


def run_back(pieces, hidden_grad, weights):
    units, width = weights[0].shape

    def hidden(count):
        return jax.ShapeDtypeStruct((count * units, 4 * CAP), jnp.bfloat16)

    return pl.pallas_call(
        back_kernel,
        out_shape=block_shapes(width) + (hidden(1), hidden(2), hidden(3), rows_shape(width)),
        in_specs=[HBM] * 5 + [VMEM] + [HBM] * 4,
        out_specs=(HBM,) * 9,
        scratch_shapes=[
            pltpu.VMEM((4 * CAP, width), jnp.bfloat16),
            pltpu.VMEM((2 * units, width), jnp.bfloat16),
            pltpu.VMEM((2 * units, width), jnp.bfloat16),
            pltpu.VMEM((CAP, width), jnp.float32),
            pltpu.VMEM((3 * CAP, width), jnp.bfloat16),
            pltpu.VMEM((6 * units, 4 * CAP), jnp.bfloat16),
            pltpu.SemaphoreType.DMA((CHUNKS, 3, 5)),
            pltpu.SemaphoreType.DMA((CHUNKS, 5)),
            pltpu.SemaphoreType.DMA((4,)),
        ],
        compiler_params=pltpu.CompilerParams(vmem_limit_bytes=30 * 2**20),
        cost_estimate=SMALL,
    )(*pieces, hidden_grad, *weights)


def run_weights(units, hidden, hidden_x, rows, rows_x):
    width = rows.shape[1]
    step = min(width, 1024)
    outs = hidden.shape[0] // units
    held = pl.BlockSpec(hidden.shape, lambda i: (0, 0))
    columns = pl.BlockSpec((rows.shape[0], step), lambda i: (0, i))
    return pl.pallas_call(
        weight_kernel,
        grid=(width // step,),
        out_shape=(jax.ShapeDtypeStruct((units, width), jnp.bfloat16),) * outs,
        in_specs=[held] * 2 + [columns] * 2,
        out_specs=(pl.BlockSpec((units, step), lambda i: (0, i)),) * outs,
        compiler_params=PARAMS,
        cost_estimate=SMALL,
    )(hidden, hidden_x, rows, rows_x)


def add_parts(own, parts):
    total = own
    for part in parts:
        total = total + part.astype(jnp.float32)
    return total


def near_with_far(behind, ahead, from_behind, from_ahead):
    half = from_behind.shape[0]

    def plus(block, start, extra):
        padded = jnp.pad(extra, ((start, block.shape[0] - half - start), (0, 0)))
        return (block.astype(jnp.float32) + padded.astype(jnp.float32)).astype(jnp.bfloat16)

    return both_ways(plus(ahead, 0, from_behind), plus(behind, half, from_ahead))


def split_mp(total, place):
    width = total.shape[1] // 4

    def columns(array, index):
        return lax.dynamic_slice_in_dim(array, index * width, width, axis=1)

    low = total.astype(jnp.bfloat16)
    return (columns(total, place),) + tuple(columns(low, place ^ flip) for flip in (1, 2, 3))


def send_mp(blocks):
    three, two, one = (along_mp(blocks[flip - 1], flip) for flip in (3, 2, 1))
    return (three, two, one)


def per_device(
    tokens_in,
    route_ids,
    route_weights,
    stash,
    returned_batch_index,
    back_ids,
    back_weights,
    upstream,
    window_expert,
    w_gate,
    w_up,
    w_down,
):
    expert = window_expert[0]
    place = lax.axis_index("mp")
    half = CAP // 2
    gate_w, up_w, down_w = (w_gate[0], w_up[0], w_down[0])

    fwd_gate, fwd_slot = routing(route_ids[0], route_weights[0], expert)
    fwd_pick = picker_of(fwd_slot)
    fwd_buf = pack(fwd_pick, tokens_in[0])
    held_rows = lax.dynamic_index_in_dim(
        stash[0], returned_batch_index[0, 0], axis=0, keepdims=False
    )
    fwd_buf, back_ids, back_weights = together(fwd_buf, back_ids, back_weights)
    back_gate, back_slot = routing(back_ids[0], back_weights[0], expert)
    back_pick = picker_of(back_slot)
    grad_tokens = (back_gate[:, None] * upstream[0].astype(jnp.float32)).astype(jnp.bfloat16)
    held_rows = mirrored(held_rows)
    three, two, one, gate_x, grad_buf = together(
        *ask_mp(fwd_buf), other_core(gate_w), pack(back_pick, grad_tokens)
    )

    fwd_wide = widen(fwd_buf, (three, two, one), place)
    three, two, one = ask_mp(grad_buf)
    back_buf, three = together(pack(back_pick, held_rows), three)
    fwd_behind, fwd_ahead = both_ways(fwd_wide, fwd_wide)
    fwd_behind, fwd_ahead, low, high, three, two, one, back_one, back_buf = together(
        fwd_behind,
        fwd_ahead,
        fwd_behind[:half],
        fwd_ahead[half:],
        three,
        two,
        one,
        along_mp(back_buf, 1),
        back_buf,
    )

    grad_wide = widen(grad_buf, (three, two, one), place)
    grad_sent = stacked(low, grad_wide)
    cw, ccw, three, two, up_x, down_w = together(
        *both_ways(grad_sent, stacked(high, grad_wide)),
        *(along_mp(back_buf, flip) for flip in (3, 2)),
        other_core(up_w),
        down_w,
    )

    down_x = other_core(down_w)
    fwd_terms = run_fwd(
        (fwd_wide, fwd_behind, fwd_ahead, cw, ccw), (gate_w, up_w, down_w, gate_x, up_x, down_x)
    )
    grad_pieces = (grad_sent, cw, ccw)
    back_wide = widen(back_buf, (three, two, back_one), place ^ 3)
    back_sent = stacked(cw[half:CAP], back_wide)
    cw, ccw, down_x, *fwd_terms = together(
        *both_ways(back_sent, stacked(ccw[CAP:], back_wide)),
        down_x,
        *fwd_terms,
    )
    fwd_own, fwd_to_behind, fwd_to_ahead, fwd_low, fwd_high = fwd_terms

    hidden_grad, grad_rows = run_grad((*grad_pieces, cw, ccw), (down_w, down_x))
    back_pieces = (back_sent, cw, ccw)
    cw, ccw, hidden_grad, grad_rows = together(
        *both_ways(stacked(cw[half:CAP], fwd_low), stacked(ccw[CAP:], fwd_high)),
        hidden_grad,
        grad_rows,
    )

    back_terms = run_back((*back_pieces, cw, ccw), hidden_grad, (gate_w, up_w, gate_x, up_x))
    p0, p1, grad_rows_x, *back_terms = together(
        *near_with_far(fwd_to_behind, fwd_to_ahead, cw[half:], ccw[half:]),
        other_core(grad_rows),
        *back_terms,
    )
    back_own, back_to_behind, back_to_ahead, back_low, back_high = back_terms[:5]
    hidden, pair_grads, hidden_send, back_rows = back_terms[5:]

    fwd_total = add_parts(fwd_own, (p0, p1))
    f0, f1, hidden_x, back_rows_x, *fwd_blocks = together(
        *both_ways(back_low, back_high),
        other_core(hidden_send),
        other_core(back_rows),
        *split_mp(fwd_total, place),
    )

    units = gate_w.shape[0]
    p0, p1, one, two, three, grad_down, pair_grads = together(
        *near_with_far(back_to_behind, back_to_ahead, f0, f1),
        *send_mp(fwd_blocks[1:]),
        *run_weights(units, hidden, hidden_x[:units], grad_rows, grad_rows_x),
        pair_grads,
    )

    back_here, *back_sent = split_mp(add_parts(back_own, (p0, p1)), place)
    grad_gate, grad_up, *back_sent = together(
        *run_weights(units, pair_grads, hidden_x[units:], back_rows, back_rows_x),
        *send_mp(back_sent),
    )
    fwd_sum = add_parts(fwd_blocks[0], (one, two, three))
    fwd_row_gate = jnp.sum(jnp.where(fwd_pick, fwd_gate[None, :], 0.0), axis=1)
    expert_out = unpack(fwd_pick, (fwd_sum * fwd_row_gate[:, None]).astype(jnp.bfloat16))
    input_grad = unpack(back_pick, add_parts(back_here, back_sent).astype(jnp.bfloat16))
    return (
        expert_out[None],
        input_grad[None],
        grad_gate[None],
        grad_up[None],
        grad_down[None],
    )


def solution(mesh):
    placed = (
        P("section", "expert", "mp"),
        P("section", "expert", None),
        P("section", "expert", None),
        P("section", None, "expert", "mp"),
        P("section", "expert"),
        P("section", "expert", None),
        P("section", "expert", None),
        P("section", "expert", "mp"),
        P("section"),
        P("section", ("expert", "mp"), None),
        P("section", ("expert", "mp"), None),
        P("section", ("expert", "mp"), None),
    )
    return jax.shard_map(
        per_device,
        mesh=mesh,
        in_specs=placed,
        out_specs=(
            P("section", "expert", "mp"),
            P("section", "expert", "mp"),
            P("section", ("expert", "mp"), None),
            P("section", ("expert", "mp"), None),
            P("section", ("expert", "mp"), None),
        ),
        check_vma=False,
    )
```
